32 devices in a mesh: stream: 2 (over core), span: 4 (over y, x), height: 4 (over z).
Axes of the slice: x: 2, y: 2, z: 4, core: 2. Of those that a mesh axis runs over, the one named last changes fastest.
Arguments:
- source: bfloat16 [32, 64, 128, 256], P('stream', 'span', 'height'), may hold values from -0.59765625 to 0.59765625
- inflow: bfloat16 [32, 64, 128, 256], P('stream', 'span', 'height'), may hold values from -6 to 6
- recovery: float32 [32, 64, 128], P('stream', 'span', 'height'), may hold values from 0 to 1
- obs_rows: int32 [1024], P(('stream', 'span', 'height')), may hold values from 0 to 8191, as said below
- obs: float32 [1024], P(('stream', 'span', 'height')), may hold values from -6 to 6
- observation_weight: float32 [1024], P(('stream', 'span', 'height')), may hold values from 0.1 to 1
- member_order: int32 [256], replicated, may hold values from 0 to 255, each once
Outputs:
- analysis: bfloat16 [32, 64, 128, 256], P('stream', 'span', 'height')
The draws below stay inside these ranges and needn't reach their ends.
Inputs may be any that keep to these rules, and one draw needn't show every extreme that they name: `obs_rows`: each entry indexes the rows of the device that holds it. `member_order`: a permutation.
All inputs are finite; a program needn't handle non-finite values.
Results may differ from the reference program's by a relative error of at most 0.0063.
Values may be sent and summed in bfloat16 or wider, within the bound.
No kernel may reach another device: no remote copies, remote signals or barrier semaphores. Data moves between devices by JAX's collectives and lax.ppermute only.
A program may use at most 320 MiB of HBM per device.

```python
import math
import jax
import jax.numpy as jnp
from jax import lax

M = 256
PL_DEV = 16
SP_DEV = 16
HT_DEV = 32
OBS_DEV = 32
DOWNWIND_SLICES = 32
SPAN = 64
HEIGHT = 128
ROWS_DEV = 8192
OBS = 1024
N_SPAN = 4
N_HEIGHT = 4


def draw_recovery(key, part):
    noise_seeds = jax.random.split(key, 5)
    slow_share = 0.5
    slow_cells = jax.random.uniform(noise_seeds[0], (1, SPAN, HEIGHT)) < slow_share
    slow_rate = jax.random.uniform(noise_seeds[1], (1, SPAN, HEIGHT), minval=0.2, maxval=1.0) * (math.log(10.0) * 0.4 / DOWNWIND_SLICES)
    fast_rate = 1.0 / jax.random.uniform(noise_seeds[2], (1, SPAN, HEIGHT), minval=8.0, maxval=16.0)
    base_rate = jnp.where(slow_cells, slow_rate, fast_rate)
    jitter = jax.random.uniform(noise_seeds[3], (DOWNWIND_SLICES, SPAN, HEIGHT), minval=0.67, maxval=1.5)
    stored_slices = jnp.exp(-base_rate * jitter)
    slices_each_batch = jax.random.randint(noise_seeds[4], (2,), 0, DOWNWIND_SLICES)
    slice_indices = jnp.arange(DOWNWIND_SLICES, dtype=jnp.int32)[:, None, None]
    slice_batches_list = (slice_indices == slices_each_batch[0]) | (slice_indices == slices_each_batch[1])
    stored_slices = jnp.where(slice_batches_list, stored_slices * 0.7, stored_slices)
    return stored_slices.astype(jnp.float32)


def draw_obs_rows(key, part):
    picked = jax.random.randint(key, (OBS,), 0, ROWS_DEV, dtype=jnp.int32)
    return picked.at[0].set(ROWS_DEV - 1).at[1].set(0)


def shard_levels(stream_key, extent, shards, smallest, high):
    def one(axis_at, shards_of):
        draws = jax.random.uniform(jax.random.fold_in(jax.random.fold_in(stream_key, 6), axis_at), (shards_of,), jnp.float32, smallest / len(shards), high / len(shards))
        return jnp.repeat(jnp.exp(draws), extent[axis_at] // shards_of).reshape((-1,) + (1,) * (len(extent) - axis_at - 1))

    loudness = one(*shards[0])
    for cut in shards[1:]:
        loudness = loudness * one(*cut)
    return loudness


def gaussian(rng, extent, deviation, reach, shards=(), held_as=jnp.bfloat16):
    entries = deviation * jax.random.normal(rng, extent, jnp.float32)
    if shards:
        entries = entries * shard_levels(rng, extent, shards, -0.22, 0.18)
    return jnp.clip(entries, -reach, reach).astype(held_as)


def setup_inputs(seed: int = 0) -> dict:
    key_list = jax.random.split(jax.random.key(seed), 8)
    source = gaussian(key_list[0], (DOWNWIND_SLICES, SPAN, HEIGHT, M), 0.1, 0.59765625, ((0, 2), (1, 4), (2, 4)))
    inflow = gaussian(key_list[1], (DOWNWIND_SLICES, SPAN, HEIGHT, M), 1.0, 6.0, ((0, 2), (1, 4), (2, 4)))
    recovery = draw_recovery(jax.random.fold_in(key_list[7], 71), 0)
    obs_rows = draw_obs_rows(jax.random.fold_in(key_list[7], 71), 0)
    obs = gaussian(key_list[4], (OBS,), 1.0, 6.0, ((0, 32),), jnp.float32)
    observation_weight = jnp.clip(jnp.exp(math.log(1.0) - 2.3025851 * jax.random.uniform(key_list[5], (OBS,), jnp.float32) ** shard_levels(key_list[5], (OBS,), ((0, 32),), -0.2, 0.2)), 0.1, 1.0)
    member_order = jax.random.permutation(key_list[6], M).astype(jnp.int32)
    return {"source": source, "inflow": inflow, "recovery": recovery, "obs_rows": obs_rows, "obs": obs, "observation_weight": observation_weight, "member_order": member_order}


vertical_mix = 0.25

def reference(source, inflow, recovery, obs_rows, obs, observation_weight, member_order):

    def advance_plane(carried, inputs):
        plane_source, inflow_at_plane, plane_rate = inputs
        centre = plane_source.astype(jnp.float32)
        padded = jnp.pad(centre, ((0, 0), (1, 1), (0, 0)))
        smoothed = centre + vertical_mix * (padded[:, 2:] + padded[:, :-2] - 2.0 * centre)
        velocity_deficit = plane_rate[..., None] * carried + smoothed
        prior_ensemble = inflow_at_plane.astype(jnp.float32) - velocity_deficit
        mean_of_plane = lax.optimization_barrier(jnp.mean(prior_ensemble, axis=-1))
        member_anomaly = (prior_ensemble - mean_of_plane[..., None]).astype(jnp.bfloat16)
        return (velocity_deficit, (member_anomaly, mean_of_plane))
    initial_plane = jnp.zeros((SPAN, HEIGHT, M), jnp.float32)
    unused_slot, (member_anomaly, prior_mean) = lax.scan(advance_plane, initial_plane, (source, inflow, recovery))
    owner = jnp.arange(OBS, dtype=jnp.int32) // OBS_DEV
    owner_height = owner % N_HEIGHT
    owner_span = owner // N_HEIGHT % N_SPAN
    holding_lane = owner // (N_HEIGHT * N_SPAN)
    plane_position = holding_lane * PL_DEV + obs_rows // (SP_DEV * HT_DEV)
    span_position = owner_span * SP_DEV + obs_rows // HT_DEV % SP_DEV
    height_position = owner_height * HT_DEV + obs_rows % HT_DEV
    picked = member_anomaly[plane_position, span_position, height_position].astype(jnp.float32) * observation_weight[:, None]
    observed = picked[:, member_order]
    observation_misfit = observation_weight * (obs - prior_mean[plane_position, span_position, height_position])
    highest = lax.Precision.HIGHEST
    identity = jnp.eye(M, dtype=jnp.float32)
    gram = jnp.dot(observed.T, observed, precision=highest) + (M - 1.0) * identity
    projection = jnp.dot(observed.T, observation_misfit, precision=highest)
    lower_factor = jnp.linalg.cholesky(gram)
    coefficients = lax.linalg.triangular_solve(lower_factor, projection[:, None], left_side=True, lower=True)
    upper_factor = lower_factor.T
    inverse = lax.linalg.triangular_solve(upper_factor, identity, left_side=True, lower=False)
    mean_weights = lax.linalg.triangular_solve(upper_factor, coefficients, left_side=True, lower=False)
    square_root_mapping = jnp.sqrt(M - 1.0) * inverse + mean_weights
    one_hot = (member_order[None, :] == jnp.arange(M, dtype=jnp.int32)[:, None]).astype(jnp.float32)
    weights = jnp.dot(jnp.dot(one_hot, square_root_mapping, precision=highest), one_hot.T, precision=highest).astype(jnp.bfloat16)

    def update_of_plane(pair):
        plane_anomaly, mean_of_plane = pair
        update = jnp.dot(plane_anomaly.reshape(-1, M).astype(jnp.float32), weights.astype(jnp.float32), preferred_element_type=jnp.float32)
        return (mean_of_plane[..., None] + update.reshape(SPAN, HEIGHT, M)).astype(jnp.bfloat16)
    return lax.map(update_of_plane, (member_anomaly, prior_mean))
```

```python
import functools

import jax
import jax.numpy as jnp
from jax import lax
from jax.experimental import pallas as pl
from jax.experimental.pallas import tpu as pltpu
from jax.sharding import PartitionSpec as P

vertical_mix = 0.25
MIB = 1024 * 1024
NT = (((1,), (1,)), ((), ()))
NN = (((1,), (0,)), ((), ()))
EXTRA = 8


def dot(a, b, dims=NN):
    return lax.dot_general(a, b, dims, preferred_element_type=jnp.float32)


def params(mib):
    return pltpu.CompilerParams(vmem_limit_bytes=mib * MIB)


def cost(flops, nbytes):
    return pl.CostEstimate(flops=flops, bytes_accessed=nbytes, transcendentals=0)


def march_kernel(source_ref, inflow_ref, rate_ref, *refs):
    forecast_ref, end_ref = refs[-2:]
    planes, cells, height, members = source_ref.shape
    row = lax.broadcasted_iota(jnp.int32, (height, members), 0)
    inner_low = jnp.where(row == 0, 0.0, vertical_mix)
    inner_high = jnp.where(row == height - 1, 0.0, vertical_mix)
    for a in range(cells):
        rates = rate_ref[a]
        deficit = None
        for p in range(planes):
            x = source_ref[p, a].astype(jnp.float32)
            term = (1.0 - 2.0 * vertical_mix) * x
            term = term + inner_low * pltpu.roll(x, 1, 0)
            term = term + inner_high * pltpu.roll(x, height - 1, 0)
            deficit = term if p == 0 else rates[:, p : p + 1] * deficit + term
            forecast_ref[p, a] = inflow_ref[p, a].astype(jnp.float32) - deficit
        end_ref[a] = deficit


def march(source, inflow, rates, part, parts, held=None):
    planes, span, height, members = source.shape
    step = 2 if span % (2 * parts) == 0 else 1
    count = span // parts // step
    first = part * count
    block = pl.BlockSpec((planes, step, height, members), lambda i: (0, i + first, 0, 0))
    edge = pl.BlockSpec((step, height, members), lambda i: (i + first, 0, 0))
    in_specs = [block, block, pl.BlockSpec((step, height, planes), lambda i: (i + first, 0, 0))]
    args = [source, inflow, rates]
    alias = {}
    if held is not None:
        in_specs += [pl.BlockSpec(memory_space=pl.ANY)] * 2
        args += list(held)
        alias = {3: 0, 4: 1}
    size = source.size // parts
    return pl.pallas_call(
        march_kernel,
        grid=(count,),
        in_specs=in_specs,
        out_specs=[block, edge],
        out_shape=[
            jax.ShapeDtypeStruct(source.shape, jnp.float32),
            jax.ShapeDtypeStruct((span, height, members), jnp.float32),
        ],
        input_output_aliases=alias,
        compiler_params=params(24),
        cost_estimate=cost(10 * size, 8 * size),
    )(*args)


def edge_kernel(parity_ref, first_ref, second_ref, low_rate_ref, high_rate_ref, edge_ref, last_ref):
    planes = first_ref.shape[0]
    even = parity_ref[0] == 0
    low, high = None, None
    for p in range(planes):
        one = vertical_mix * first_ref[p].astype(jnp.float32)
        two = vertical_mix * second_ref[p].astype(jnp.float32)
        low_term = jnp.where(even, two, one)
        high_term = jnp.where(even, one, two)
        low = low_term if p == 0 else low_rate_ref[:, p : p + 1] * low + low_term
        high = high_term if p == 0 else high_rate_ref[:, p : p + 1] * high + high_term
        edge_ref[0, p] = low
        edge_ref[1, p] = high
    last_ref[0] = low
    last_ref[1] = high


def edge_march(parity, first, second, low_rate, high_rate):
    planes, span, members = first.shape
    vmem = pl.BlockSpec(memory_space=pltpu.VMEM)
    return pl.pallas_call(
        edge_kernel,
        in_specs=[pl.BlockSpec(memory_space=pltpu.SMEM)] + [vmem] * 4,
        out_specs=[vmem, vmem],
        out_shape=[
            jax.ShapeDtypeStruct((2, planes, span, members), jnp.float32),
            jax.ShapeDtypeStruct((2, span, members), jnp.float32),
        ],
        compiler_params=params(8),
        cost_estimate=cost(4 * first.size, 8 * first.size),
    )(parity, first, second, low_rate, high_rate)


def observe_kernel(
    rows_ref, rows_column_ref, obs_ref, weight_ref, rate_ref, incoming_ref, edge_ref, last_ref,
    forecast_ref, out_ref, tiles, prior, arriving, halo, through, through_rows, sem,
):
    planes, span, height = rate_ref.shape
    members = out_ref.shape[1]
    count = prior.shape[0]

    def place(k):
        r = rows_ref[k]
        return r // (span * height), r // height % span, r % height

    def fetch(k):
        p, a, b = place(k)
        start = pl.multiple_of(b // 8 * 8, 8)
        return pltpu.make_async_copy(forecast_ref.at[p, a, pl.ds(start, 8), :], tiles.at[k], sem.at[k])

    for k in range(count):
        fetch(k).start()
    product = None
    for p in range(planes):
        product = rate_ref[p] if p == 0 else product * rate_ref[p]
        through[p] = product
    for k in range(count):
        p, a, b = place(k)
        side = jnp.where(b == height - 1, 1, 0)
        at_edge = jnp.where((b == 0) | (b == height - 1), 1.0, 0.0)
        arriving[pl.ds(k, 1), :] = (
            incoming_ref[a, pl.ds(b, 1), :] + at_edge * last_ref[side, pl.ds(a, 1), :]
        )
        halo[pl.ds(k, 1), :] = at_edge * edge_ref[side, p, pl.ds(a, 1), :]
        through_rows[pl.ds(k, 1), :] = through[p, pl.ds(a, 1), :]
    for k in range(count):
        fetch(k).wait()
        _, _, b = place(k)
        prior[pl.ds(k, 1), :] = tiles[k, pl.ds(b % 8, 1), :]
    cell = rows_column_ref[...] % height
    lane = lax.broadcasted_iota(jnp.int32, (count, height), 1)
    share = jnp.sum(jnp.where(lane == cell, through_rows[...], 0.0), axis=1, keepdims=True)
    forecast = prior[...] - halo[...] - share * arriving[...]
    mean = jnp.sum(forecast, axis=1, keepdims=True) * (1.0 / members)
    anomaly = (forecast - mean).astype(jnp.bfloat16).astype(jnp.float32)
    weight = weight_ref[...]
    observed = weight * anomaly
    misfit = weight * (obs_ref[...] - mean)
    projection = jnp.sum(observed * misfit, axis=0, keepdims=True)
    one = projection.astype(jnp.bfloat16).astype(jnp.float32)
    two = (projection - one).astype(jnp.bfloat16).astype(jnp.float32)
    three = projection - one - two
    row = lax.broadcasted_iota(jnp.int32, (EXTRA, members), 0)
    pieces = jnp.where(row == 0, one, jnp.where(row == 1, two, jnp.where(row == 2, three, 0.0)))
    out_ref[...] = jnp.concatenate([observed, pieces], axis=0).astype(jnp.bfloat16)


def observe(obs_rows, obs, weight, recovery, incoming, edge, last, forecast):
    planes, span, height, members = forecast.shape
    count = obs_rows.shape[0]
    vmem = pl.BlockSpec(memory_space=pltpu.VMEM)
    return pl.pallas_call(
        observe_kernel,
        in_specs=[pl.BlockSpec(memory_space=pltpu.SMEM)] + [vmem] * 7 + [pl.BlockSpec(memory_space=pl.ANY)],
        out_specs=vmem,
        out_shape=jax.ShapeDtypeStruct((count + EXTRA, members), jnp.bfloat16),
        scratch_shapes=[
            pltpu.VMEM((count, 8, members), jnp.float32),
            pltpu.VMEM((count, members), jnp.float32),
            pltpu.VMEM((count, members), jnp.float32),
            pltpu.VMEM((count, members), jnp.float32),
            pltpu.VMEM((planes, span, height), jnp.float32),
            pltpu.VMEM((count, height), jnp.float32),
            pltpu.SemaphoreType.DMA((count,)),
        ],
        compiler_params=params(8),
        cost_estimate=cost(40 * count * members, 64 * count * members),
    )(
        obs_rows, obs_rows[:, None], obs[:, None], weight[:, None], recovery, incoming, edge, last,
        forecast,
    )


def anomaly_kernel(first, forecast_ref, rate_ref, incoming_ref, edge_ref, last_ref, *refs):
    anomaly_ref, mean_ref = refs[-2:]
    planes, cells, height, members = forecast_ref.shape
    row = lax.broadcasted_iota(jnp.int32, (height, members), 0)
    for j in range(cells):
        a = (pl.program_id(0) + first) * cells + j
        rates = rate_ref[j]

        def at_edges(low, high):
            return jnp.where(row == 0, low, jnp.where(row == height - 1, high, 0.0))

        arriving = incoming_ref[j] + at_edges(last_ref[0, pl.ds(a, 1), :], last_ref[1, pl.ds(a, 1), :])
        for p in range(planes):
            arriving = rates[:, p : p + 1] * arriving
            halo = at_edges(edge_ref[0, p, pl.ds(a, 1), :], edge_ref[1, p, pl.ds(a, 1), :])
            forecast = forecast_ref[p, j] - arriving - halo
            mean = jnp.sum(forecast, axis=1, keepdims=True) * (1.0 / members)
            anomaly_ref[p, j] = (forecast - mean).astype(jnp.bfloat16)
            mean_ref[p, j] = jnp.broadcast_to(mean, (height, mean_ref.shape[-1]))


def anomalies(forecast, rates, incoming, edge, last, part, parts, held=None):
    planes, span, height, members = forecast.shape
    step = 2 if span % (2 * parts) == 0 else 1
    count = span // parts // step
    first = part * count
    wide = min(128, members)

    def block(width):
        return pl.BlockSpec((planes, step, height, width), lambda i: (0, i + first, 0, 0))

    whole = pl.BlockSpec(memory_space=pltpu.VMEM)
    in_specs = [
        block(members),
        pl.BlockSpec((step, height, planes), lambda i: (i + first, 0, 0)),
        pl.BlockSpec((step, height, members), lambda i: (i + first, 0, 0)),
        whole,
        whole,
    ]
    args = [forecast, rates, incoming, edge, last]
    alias = {}
    if held is not None:
        in_specs += [pl.BlockSpec(memory_space=pl.ANY)] * 2
        args += list(held)
        alias = {5: 0, 6: 1}
    size = forecast.size // parts
    return pl.pallas_call(
        functools.partial(anomaly_kernel, first),
        grid=(count,),
        in_specs=in_specs,
        out_specs=[block(members), block(wide)],
        out_shape=[
            jax.ShapeDtypeStruct(forecast.shape, jnp.bfloat16),
            jax.ShapeDtypeStruct((planes, span, height, wide), jnp.float32),
        ],
        input_output_aliases=alias,
        compiler_params=params(24),
        cost_estimate=cost(10 * size, 8 * size),
    )(*args)


def halves(x):
    big = x.astype(jnp.bfloat16)
    return big, (x - big.astype(jnp.float32)).astype(jnp.bfloat16)


def fine_dot(a, b, dims=NN):
    a_big, a_small = halves(a)
    b_big, b_small = halves(b)
    return dot(a_big, b_big, dims) + (dot(a_big, b_small, dims) + dot(a_small, b_big, dims))


def update_kernel(
    picked, gathered_ref, order_row_ref, order_column_ref, anomaly_ref, mean_ref, out_ref,
    gram, factor, anomalies_held, means_held, results, in_sem, mean_sem, out_sem,
):
    total, members = gathered_ref.shape
    chunks, chunk = anomalies_held.shape[:2]
    bf16, f32 = jnp.bfloat16, jnp.float32

    def rows(c):
        return pl.ds(c * chunk, chunk)

    def fetch(c):
        return (
            pltpu.make_async_copy(anomaly_ref.at[rows(c)], anomalies_held.at[c], in_sem.at[c]),
            pltpu.make_async_copy(mean_ref.at[rows(c)], means_held.at[c], mean_sem.at[c]),
        )

    for c in range(chunks):
        for copy in fetch(c):
            copy.start()

    row = lax.broadcasted_iota(jnp.int32, (members, members), 0)
    column = lax.broadcasted_iota(jnp.int32, (members, members), 1)
    select = jnp.where(order_row_ref[...] == row, 1.0, 0.0).astype(bf16)
    select_t = jnp.where(order_column_ref[...] == column, 1.0, 0.0).astype(bf16)
    block = picked + EXTRA
    gathered = gathered_ref[...]
    place = lax.broadcasted_iota(jnp.int32, (total, members), 0) % block
    observed = jnp.where(place < picked, gathered.astype(f32), 0.0).astype(bf16)
    ordered_t = dot(select_t, observed, NT).astype(bf16)
    slot = lax.broadcasted_iota(jnp.int32, (16, total), 1) % block
    pieces = dot(jnp.where(slot >= picked, 1.0, 0.0).astype(bf16), gathered)
    piece_one = pieces.astype(bf16)
    piece_two, piece_three = halves(pieces - piece_one.astype(f32))
    projection = dot(piece_one, select) + (dot(piece_two, select) + dot(piece_three, select))
    diagonal = row == column
    full = dot(ordered_t, ordered_t, NT) + jnp.where(diagonal, members - 1.0, 0.0)
    on_diagonal = jnp.where(diagonal, full, 0.0)
    scale_row = lax.rsqrt(jnp.sum(on_diagonal, axis=0, keepdims=True))
    scale_column = lax.rsqrt(jnp.sum(on_diagonal, axis=1, keepdims=True))
    unit = full * scale_row * scale_column
    gram[...] = full
    lower = row > column

    def lower_part(residual):
        return jnp.where(lower, residual, jnp.where(diagonal, 0.5 * residual, 0.0))

    identity = jnp.where(diagonal, 1.0, 0.0)
    factor[...] = identity - jnp.where(lower, unit, 0.0)
    unit_big = unit.astype(bf16)
    for _ in range(2):
        inverse = factor[...]
        inverse_big = inverse.astype(bf16)
        half_way = dot(inverse_big, unit_big).astype(bf16)
        residual = dot(half_way, inverse_big, NT) - identity
        factor[...] = inverse - dot(lower_part(residual).astype(bf16), inverse_big)

    def refine(carried):
        step, _ = carried
        inverse = factor[...]
        residual = fine_dot(fine_dot(inverse, unit), inverse, NT) - identity
        factor[...] = inverse - dot(lower_part(residual).astype(bf16), inverse.astype(bf16))
        return step + 1, jnp.sum(residual * residual)

    def unfinished(carried):
        step, error = carried
        return (step < 8) & (error > 0.04) & (error < 64.0)

    _, error = lax.while_loop(unfinished, refine, (0, jnp.float32(1.0)))
    factor[...] = factor[...] * scale_row

    @pl.when(jnp.logical_not(error <= 0.04))
    def _():
        factor[...] = identity

        def eliminate(k, carry):
            held = gram[...]
            pivot_row = gram[pl.ds(k, 1), :]
            pivot = jnp.sum(jnp.where(column[:1] == k, pivot_row, 0.0), axis=1, keepdims=True)
            pivot_column = jnp.sum(jnp.where(column == k, held, 0.0), axis=1, keepdims=True)
            share = jnp.where(row[:, :1] > k, pivot_column / pivot, 0.0)
            factor[...] = factor[...] - share * factor[pl.ds(k, 1), :]
            gram[...] = held - share * pivot_row
            return carry

        lax.fori_loop(0, members, eliminate, 0)
        pivots = jnp.sum(jnp.where(diagonal, gram[...], 0.0), axis=1, keepdims=True)
        factor[...] = factor[...] * lax.rsqrt(pivots)

    inverse = factor[...]
    coefficients = fine_dot(projection, inverse, NT)
    shift = fine_dot(coefficients, inverse)[:1]
    transform_t = ((members - 1.0) ** 0.5 * inverse + shift).astype(bf16)
    weights_t = dot(select, dot(transform_t, select, NT).astype(bf16)).astype(bf16)
    stores = []
    for c in range(chunks):
        for copy in fetch(c):
            copy.wait()
        update = dot(anomalies_held[c], weights_t, NT)
        mean = means_held[c]
        mean = jnp.concatenate([mean] * (members // mean.shape[1]), axis=1)
        results[c] = (mean + update).astype(bf16)
        store = pltpu.make_async_copy(results.at[c], out_ref.at[rows(c)], out_sem.at[c])
        store.start()
        stores.append(store)
    for store in stores:
        store.wait()


def updated(picked, gathered, member_order, anomaly, mean):
    count, members = anomaly.shape
    chunks = 8
    while count % (16 * chunks):
        chunks //= 2
    chunk = count // chunks
    vmem, hbm = pl.BlockSpec(memory_space=pltpu.VMEM), pl.BlockSpec(memory_space=pl.ANY)
    return pl.pallas_call(
        functools.partial(update_kernel, picked),
        in_specs=[vmem] * 3 + [hbm] * 2,
        out_specs=hbm,
        out_shape=jax.ShapeDtypeStruct((count, members), jnp.bfloat16),
        scratch_shapes=[
            pltpu.VMEM((members, members), jnp.float32),
            pltpu.VMEM((members, members), jnp.float32),
            pltpu.VMEM((chunks, chunk, members), jnp.bfloat16),
            pltpu.VMEM((chunks, chunk, mean.shape[1]), jnp.float32),
            pltpu.VMEM((chunks, chunk, members), jnp.bfloat16),
            pltpu.SemaphoreType.DMA((chunks,)),
            pltpu.SemaphoreType.DMA((chunks,)),
            pltpu.SemaphoreType.DMA((chunks,)),
        ],
        compiler_params=params(48),
        cost_estimate=cost(2 * count * members * members, 5 * count * members),
    )(gathered, member_order[None, :], member_order[:, None], anomaly, mean)


def pairs(count, first):
    low = [(i, i + 1) for i in range(first, count - 1, 2)]
    return low + [(j, i) for i, j in low]


def downstream(value, rate):
    count = lax.axis_size("stream")
    steps = [(i, i + 1) for i in range(count - 1)]
    incoming = lax.ppermute(value, "stream", steps)
    for _ in range(count - 2):
        incoming = lax.ppermute(rate * incoming + value, "stream", steps)
    return incoming


def gather_rows(rows, axes):
    for axis in axes:
        count = lax.axis_size(axis)
        if count & (count - 1):
            rows = lax.all_gather(rows, axis, axis=0, tiled=True)
            continue
        apart = count // 2
        while apart:
            other = lax.ppermute(rows, axis, [(i, i ^ apart) for i in range(count)])
            rows = jnp.concatenate([rows, other], axis=0)
            apart //= 2
    return rows


def shards(source, inflow, recovery, obs_rows, obs, observation_weight, member_order):
    planes, span, height, members = source.shape
    levels = lax.axis_size("height")
    parity = lax.axis_index("height") % 2

    def edge_row(at):
        return lax.dynamic_slice_in_dim(source, at, 1, axis=2)[:, :, 0]

    second = lax.ppermute(edge_row(jnp.where(parity == 0, 0, height - 1)), "height", pairs(levels, 1))
    first = lax.ppermute(edge_row(jnp.where(parity == 0, height - 1, 0)), "height", pairs(levels, 0))
    rates = jnp.transpose(recovery, (1, 2, 0))
    held = march(source, inflow, rates, 0, 2)
    forecast, local_end = march(source, inflow, rates, 1, 2, held)
    total = jnp.prod(recovery, axis=0)[..., None] if lax.axis_size("stream") > 2 else None
    incoming = downstream(local_end, total)
    edge, edge_end = edge_march(parity[None], first, second, rates[:, 0], rates[:, height - 1])
    total_edge = None if total is None else jnp.stack([total[:, 0], total[:, height - 1]])
    last = downstream(edge_end, total_edge)
    rows = observe(obs_rows, obs, observation_weight, recovery, incoming, edge, last, forecast)
    gathered = gather_rows(rows, ("height", "span", "stream"))
    parts = 4 if span % 4 == 0 else 1
    held = None
    for part in range(parts):
        held = anomalies(forecast, rates, incoming, edge, last, part, parts, held)
    anomaly, mean = held
    analysis = updated(
        obs_rows.shape[0], gathered, member_order,
        anomaly.reshape(-1, members), mean.reshape(-1, mean.shape[-1]),
    )
    return analysis.reshape(source.shape)


def solution(mesh):
    placed = (
        P("stream", "span", "height", None),
        P("stream", "span", "height", None),
        P("stream", "span", "height"),
        P(("stream", "span", "height")),
        P(("stream", "span", "height")),
        P(("stream", "span", "height")),
        P(),
    )
    return jax.shard_map(
        shards,
        mesh=mesh,
        in_specs=placed,
        out_specs=P("stream", "span", "height", None),
        check_vma=False,
    )
```

```python
import functools

import jax
import jax.numpy as jnp
from jax import lax
from jax.experimental import pallas as pl
from jax.experimental.pallas import tpu as pltpu
from jax.sharding import PartitionSpec as P

vertical_mix = 0.25
MIB = 1024 * 1024
NT = (((1,), (1,)), ((), ()))
NN = (((1,), (0,)), ((), ()))
LIMIT = 40
EXTRA = 8


def dot(a, b, dims=NN):
    return lax.dot_general(a, b, dims, preferred_element_type=jnp.float32)


def params(mib):
    return pltpu.CompilerParams(vmem_limit_bytes=mib * MIB)


def cost(elements, nbytes):
    return pl.CostEstimate(flops=1000 * elements, bytes_accessed=nbytes, transcendentals=0)


def border_kernel(high_ref, source_ref, out_ref, held, sems):
    planes, span, rows, members = held.shape
    height = source_ref.shape[2]
    high = high_ref[0] == 1
    start = pl.multiple_of(jnp.where(high, height - rows, 0), rows)
    count = sems.shape[0]
    step = planes // count

    def fetch(c):
        part = pl.ds(c * step, step)
        return pltpu.make_async_copy(
            source_ref.at[part, :, pl.ds(start, rows), :], held.at[part], sems.at[c]
        )

    for c in range(count):
        fetch(c).start()
    for c in range(count):
        fetch(c).wait()
        for p in range(c * step, (c + 1) * step):
            block = held[p].astype(jnp.float32)
            low = jnp.concatenate([block[a, :1] for a in range(span)], axis=0)
            top = jnp.concatenate([block[a, rows - 1 :] for a in range(span)], axis=0)
            out_ref[p] = jnp.where(high, top, low).astype(jnp.bfloat16)


def border(source, high):
    planes, span, height, members = source.shape
    count = 4 if planes % 4 == 0 else 1
    return pl.pallas_call(
        border_kernel,
        in_specs=[pl.BlockSpec(memory_space=pltpu.SMEM), pl.BlockSpec(memory_space=pltpu.HBM)],
        out_specs=pl.BlockSpec(memory_space=pltpu.VMEM),
        out_shape=jax.ShapeDtypeStruct((planes, span, members), jnp.bfloat16),
        scratch_shapes=[
            pltpu.VMEM((planes, span, 16, members), jnp.bfloat16),
            pltpu.SemaphoreType.DMA((count,)),
        ],
        compiler_params=params(LIMIT),
        cost_estimate=cost(source.size // 2, source.size),
    )(high, source)


def place_of(r, shape):
    _, span, height = shape
    return r // (span * height), r // height % span, r % height


def march_kernel(part, cells, has_more, *refs):
    if has_more:
        (rows_ref, rows_column_ref, source_ref, rate_ref, recovery_ref, picks_in_ref, inflow_ref,
         end_ref, picks_ref, share_ref, deficits, tiles, tiles_wide, through_rows, through, sems) = refs
    else:
        rows_ref, source_ref, rate_ref, end_ref, picks_ref, deficits = refs
    planes, step, height, members = source_ref.shape
    count = picks_ref.shape[0]
    at = pl.program_id(0)
    shape = recovery_ref.shape if has_more else (planes, cells, height)

    def fetch(k):
        p, a, b = place_of(rows_ref[k], shape)
        start = pl.multiple_of(b // 16 * 16, 16)
        return pltpu.make_async_copy(inflow_ref.at[p, a, pl.ds(start, 16), :], tiles.at[k], sems.at[k])

    if has_more:

        @pl.when(at == 0)
        def _():
            for k in range(count):
                fetch(k).start()

    row = lax.broadcasted_iota(jnp.int32, (height, members), 0)
    inner_low = jnp.where(row == 0, 0.0, vertical_mix)
    inner_high = jnp.where(row == height - 1, 0.0, vertical_mix)
    for j in range(step):
        rates = rate_ref[j]
        deficit = None
        for p in range(planes):
            x = source_ref[p, j].astype(jnp.float32)
            term = (1.0 - 2.0 * vertical_mix) * x
            term = term + inner_low * pltpu.roll(x, 1, 0)
            term = term + inner_high * pltpu.roll(x, height - 1, 0)
            deficit = term if p == 0 else rates[:, p : p + 1] * deficit + term
            deficits[p, at * step + j] = deficit
        end_ref[j] = deficit

    @pl.when(at == pl.num_programs(0) - 1)
    def _():
        local = deficits.shape[1]
        for k in range(count):
            p, a, b = place_of(rows_ref[k], (planes, cells, height))
            here = a - part * local
            inside = jnp.where((here >= 0) & (here < local), -1.0, 0.0)
            here = jnp.clip(here, 0, local - 1)
            picks_ref[pl.ds(k, 1), :] = inside * deficits[p, here, pl.ds(b, 1), :]
        if has_more:
            product = None
            for p in range(planes):
                product = recovery_ref[p] if p == 0 else product * recovery_ref[p]
                through[p] = product
            for k in range(count):
                p, a, _ = place_of(rows_ref[k], shape)
                through_rows[pl.ds(k, 1), :] = through[p, pl.ds(a, 1), :]
            cell = rows_column_ref[...] % height
            lane = lax.broadcasted_iota(jnp.int32, (count, height), 1)
            share = jnp.sum(jnp.where(lane == cell, through_rows[...], 0.0), axis=1, keepdims=True)
            share_ref[...] = jnp.broadcast_to(share, share_ref.shape)
            for k in range(count):
                fetch(k).wait()
            tiles_wide[...] = tiles[...].astype(jnp.float32)
            for k in range(count):
                _, _, b = place_of(rows_ref[k], shape)
                picks_ref[pl.ds(k, 1), :] = (
                    picks_ref[pl.ds(k, 1), :] + picks_in_ref[pl.ds(k, 1), :] + tiles_wide[k, pl.ds(b % 16, 1), :]
                )


def march(source, rates, obs_rows, part, parts, more=()):
    planes, span, height, members = source.shape
    observed = obs_rows.shape[0]
    local = span // parts
    step = 2 if local % 2 == 0 else 1
    count = local // step
    first = part * count
    vmem, hbm = pl.BlockSpec(memory_space=pltpu.VMEM), pl.BlockSpec(memory_space=pltpu.HBM)
    smem = pl.BlockSpec(memory_space=pltpu.SMEM)
    in_specs = [
        pl.BlockSpec((planes, step, height, members), lambda i: (0, i + first, 0, 0)),
        pl.BlockSpec((step, height, planes), lambda i: (i + first, 0, 0)),
    ]
    out_specs = [pl.BlockSpec((step, height, members), lambda i: (i, 0, 0)), vmem]
    out_shape = [
        jax.ShapeDtypeStruct((local, height, members), jnp.float32),
        jax.ShapeDtypeStruct((observed, members), jnp.float32),
    ]
    scratch = [pltpu.VMEM((planes, local, height, members), jnp.float32)]
    args = [obs_rows, source, rates]
    in_specs = [smem] + in_specs
    if more:
        recovery, picks, inflow = more
        in_specs = [smem, vmem] + in_specs[1:] + [vmem, vmem, hbm]
        args = [obs_rows, obs_rows[:, None], source, rates, recovery, picks, inflow]
        out_specs.append(vmem)
        out_shape.append(jax.ShapeDtypeStruct((observed, members), jnp.float32))
        scratch += [
            pltpu.VMEM((observed, 16, members), jnp.bfloat16),
            pltpu.VMEM((observed, 16, members), jnp.float32),
            pltpu.VMEM((observed, height), jnp.float32),
            pltpu.VMEM((planes, span, height), jnp.float32),
            pltpu.SemaphoreType.DMA((observed,)),
        ]
    size = source.size // parts
    return pl.pallas_call(
        functools.partial(march_kernel, part, span, bool(more)),
        grid=(count,),
        in_specs=in_specs,
        out_specs=out_specs,
        out_shape=out_shape,
        scratch_shapes=scratch,
        compiler_params=params(LIMIT),
        cost_estimate=cost(3 * size, 4 * size),
    )(*args)


def edge_kernel(parity_ref, first_ref, second_ref, low_rate_ref, high_rate_ref, term_ref, edge_ref, last_ref):
    planes = first_ref.shape[0]
    even = parity_ref[0] == 0
    low, high = None, None
    for p in range(planes):
        one = vertical_mix * first_ref[p].astype(jnp.float32)
        two = vertical_mix * second_ref[p].astype(jnp.float32)
        low_term = jnp.where(even, two, one)
        high_term = jnp.where(even, one, two)
        term_ref[0, p] = low_term
        term_ref[1, p] = high_term
        low = low_term if p == 0 else low_rate_ref[:, p : p + 1] * low + low_term
        high = high_term if p == 0 else high_rate_ref[:, p : p + 1] * high + high_term
        edge_ref[0, p] = low
        edge_ref[1, p] = high
    last_ref[0] = low
    last_ref[1] = high


def edge_march(parity, first, second, low_rate, high_rate):
    planes, span, members = first.shape
    vmem = pl.BlockSpec(memory_space=pltpu.VMEM)
    return pl.pallas_call(
        edge_kernel,
        in_specs=[pl.BlockSpec(memory_space=pltpu.SMEM)] + [vmem] * 4,
        out_specs=[vmem] * 3,
        out_shape=[
            jax.ShapeDtypeStruct((2, planes, span, members), jnp.float32),
            jax.ShapeDtypeStruct((2, planes, span, members), jnp.float32),
            jax.ShapeDtypeStruct((2, span, members), jnp.float32),
        ],
        compiler_params=params(LIMIT),
        cost_estimate=cost(first.size, 8 * first.size),
    )(parity, first, second, low_rate, high_rate)


def observe_kernel(
    rows_ref, obs_ref, weight_ref, picks_ref, share_ref, incoming_ref, edge_ref, last_ref,
    out_ref, arriving, halo,
):
    planes = edge_ref.shape[1]
    span, height, members = incoming_ref.shape
    count = picks_ref.shape[0]
    for k in range(count):
        p, a, b = place_of(rows_ref[k], (planes, span, height))
        side = jnp.where(b == height - 1, 1, 0)
        at_edge = jnp.where((b == 0) | (b == height - 1), 1.0, 0.0)
        arriving[pl.ds(k, 1), :] = (
            incoming_ref[a, pl.ds(b, 1), :] + at_edge * last_ref[side, pl.ds(a, 1), :]
        )
        halo[pl.ds(k, 1), :] = at_edge * edge_ref[side, p, pl.ds(a, 1), :]
    forecast = picks_ref[...] - halo[...] - share_ref[...] * arriving[...]
    mean = jnp.sum(forecast, axis=1, keepdims=True) * (1.0 / members)
    anomaly = (forecast - mean).astype(jnp.bfloat16).astype(jnp.float32)
    weight = weight_ref[...]
    observed = weight * anomaly
    misfit = weight * (obs_ref[...] - mean)
    projection = jnp.sum(observed * misfit, axis=0, keepdims=True)
    one = projection.astype(jnp.bfloat16).astype(jnp.float32)
    two = (projection - one).astype(jnp.bfloat16).astype(jnp.float32)
    three = projection - one - two
    row = lax.broadcasted_iota(jnp.int32, (EXTRA, members), 0)
    pieces = jnp.where(row == 0, one, jnp.where(row == 1, two, jnp.where(row == 2, three, 0.0)))
    out_ref[...] = jnp.concatenate([observed, pieces], axis=0).astype(jnp.bfloat16)


def observe(obs_rows, obs, weight, picks, share, incoming, edge, last):
    count, members = picks.shape
    vmem = pl.BlockSpec(memory_space=pltpu.VMEM)
    return pl.pallas_call(
        observe_kernel,
        in_specs=[pl.BlockSpec(memory_space=pltpu.SMEM)] + [vmem] * 7,
        out_specs=vmem,
        out_shape=jax.ShapeDtypeStruct((count + EXTRA, members), jnp.bfloat16),
        scratch_shapes=[pltpu.VMEM((count, members), jnp.float32)] * 2,
        compiler_params=params(LIMIT),
        cost_estimate=cost(40 * count * members, 64 * count * members),
    )(obs_rows, obs[:, None], weight[:, None], picks, share, incoming, edge, last)


def forecast_kernel(first, source_ref, inflow_ref, rate_ref, incoming_ref, term_ref, last_ref, *refs):
    out_ref = refs[-1]
    planes, step, height, members = source_ref.shape
    row = lax.broadcasted_iota(jnp.int32, (height, members), 0)
    for j in range(step):
        a = (pl.program_id(0) + first) * step + j
        rates = rate_ref[j]

        def outside(low, high):
            return jnp.where(row == 0, low, jnp.where(row == height - 1, high, 0.0))

        deficit = incoming_ref[j] + outside(last_ref[0, pl.ds(a, 1), :], last_ref[1, pl.ds(a, 1), :])
        for p in range(planes):
            x = vertical_mix * source_ref[p, j].astype(jnp.float32)
            below = jnp.where(row == 0, term_ref[0, p, pl.ds(a, 1), :], pltpu.roll(x, 1, 0))
            above = jnp.where(row == height - 1, term_ref[1, p, pl.ds(a, 1), :], pltpu.roll(x, height - 1, 0))
            term = (1.0 / vertical_mix - 2.0) * x + (below + above)
            deficit = rates[:, p : p + 1] * deficit + term
            out_ref[p, j] = (inflow_ref[p, j].astype(jnp.float32) - deficit).astype(jnp.bfloat16)


def forecasts(source, inflow, rates, incoming, term, last, part, parts, held=None):
    planes, span, height, members = source.shape
    local = span // parts
    step = 2 if local % 2 == 0 else 1
    count = local // step
    first = part * count
    block = pl.BlockSpec((planes, step, height, members), lambda i: (0, i + first, 0, 0))
    vmem = pl.BlockSpec(memory_space=pltpu.VMEM)
    in_specs = [
        block,
        block,
        pl.BlockSpec((step, height, planes), lambda i: (i + first, 0, 0)),
        pl.BlockSpec((step, height, members), lambda i: (i + first, 0, 0)),
        vmem,
        vmem,
    ]
    args = [source, inflow, rates, incoming, term, last]
    alias = {}
    if held is not None:
        in_specs.append(pl.BlockSpec(memory_space=pltpu.HBM))
        args.append(held)
        alias = {6: 0}
    size = source.size // parts
    return pl.pallas_call(
        functools.partial(forecast_kernel, first),
        grid=(count,),
        in_specs=in_specs,
        out_specs=block,
        out_shape=pltpu.HBM(source.shape, jnp.bfloat16),
        input_output_aliases=alias,
        compiler_params=params(LIMIT),
        cost_estimate=cost(4 * size, 6 * size),
    )(*args)


def halves(x):
    big = x.astype(jnp.bfloat16)
    return big, (x - big.astype(jnp.float32)).astype(jnp.bfloat16)


def fine_dot(a, b, dims=NN):
    a_big, a_small = halves(a)
    b_big, b_small = halves(b)
    return dot(a_big, b_big, dims) + (dot(a_big, b_small, dims) + dot(a_small, b_big, dims))


def update_kernel(
    picked, gathered_ref, order_row_ref, order_column_ref, forecast_ref, out_ref,
    gram, factor, forecasts_held, results, in_sem, out_sem,
):
    total, members = gathered_ref.shape
    chunks = forecasts_held.shape[0]
    cells = forecasts_held.shape[1:4]
    bf16, f32 = jnp.bfloat16, jnp.float32

    step = cells[0]

    def rows(c):
        return pl.ds(c * step, step)

    def fetch(c):
        return pltpu.make_async_copy(forecast_ref.at[rows(c)], forecasts_held.at[c], in_sem.at[c])

    for c in range(chunks):
        fetch(c).start()

    row = lax.broadcasted_iota(jnp.int32, (members, members), 0)
    column = lax.broadcasted_iota(jnp.int32, (members, members), 1)
    select = jnp.where(order_row_ref[...] == row, 1.0, 0.0).astype(bf16)
    select_t = jnp.where(order_column_ref[...] == column, 1.0, 0.0).astype(bf16)
    block = picked + EXTRA
    gathered = gathered_ref[...]
    place = lax.broadcasted_iota(jnp.int32, (total, members), 0) % block
    observed = jnp.where(place < picked, gathered.astype(f32), 0.0).astype(bf16)
    ordered_t = dot(select_t, observed, NT).astype(bf16)
    slot = lax.broadcasted_iota(jnp.int32, (16, total), 1) % block
    pieces = dot(jnp.where(slot >= picked, 1.0, 0.0).astype(bf16), gathered)
    piece_one = pieces.astype(bf16)
    piece_two, piece_three = halves(pieces - piece_one.astype(f32))
    projection = dot(piece_one, select) + (dot(piece_two, select) + dot(piece_three, select))
    diagonal = row == column
    full = dot(ordered_t, ordered_t, NT) + jnp.where(diagonal, members - 1.0, 0.0)
    on_diagonal = jnp.where(diagonal, full, 0.0)
    scale_row = lax.rsqrt(jnp.sum(on_diagonal, axis=0, keepdims=True))
    scale_column = lax.rsqrt(jnp.sum(on_diagonal, axis=1, keepdims=True))
    unit = full * scale_row * scale_column
    gram[...] = full
    lower = row > column

    def lower_part(residual):
        return jnp.where(lower, residual, jnp.where(diagonal, 0.5 * residual, 0.0))

    identity = jnp.where(diagonal, 1.0, 0.0)
    factor[...] = identity - jnp.where(lower, unit, 0.0)
    unit_big = unit.astype(bf16)
    for _ in range(2):
        inverse = factor[...]
        inverse_big = inverse.astype(bf16)
        half_way = dot(inverse_big, unit_big).astype(bf16)
        residual = dot(half_way, inverse_big, NT) - identity
        factor[...] = inverse - dot(lower_part(residual).astype(bf16), inverse_big)

    def refine(carried):
        step, _ = carried
        inverse = factor[...]
        residual = fine_dot(fine_dot(inverse, unit), inverse, NT) - identity
        factor[...] = inverse - dot(lower_part(residual).astype(bf16), inverse.astype(bf16))
        return step + 1, jnp.sum(residual * residual)

    def unfinished(carried):
        step, error = carried
        return (step < 8) & (error > 0.04) & (error < 64.0)

    _, error = lax.while_loop(unfinished, refine, (0, jnp.float32(1.0)))
    factor[...] = factor[...] * scale_row

    @pl.when(jnp.logical_not(error <= 0.04))
    def _():
        factor[...] = identity

        def eliminate(k, carry):
            held = gram[...]
            pivot_row = gram[pl.ds(k, 1), :]
            pivot = jnp.sum(jnp.where(column[:1] == k, pivot_row, 0.0), axis=1, keepdims=True)
            pivot_column = jnp.sum(jnp.where(column == k, held, 0.0), axis=1, keepdims=True)
            share = jnp.where(row[:, :1] > k, pivot_column / pivot, 0.0)
            factor[...] = factor[...] - share * factor[pl.ds(k, 1), :]
            gram[...] = held - share * pivot_row
            return carry

        lax.fori_loop(0, members, eliminate, 0)
        pivots = jnp.sum(jnp.where(diagonal, gram[...], 0.0), axis=1, keepdims=True)
        factor[...] = factor[...] * lax.rsqrt(pivots)

    inverse = factor[...]
    coefficients = fine_dot(projection, inverse, NT)
    shift = fine_dot(coefficients, inverse)[:1]
    transform_t = (members - 1.0) ** 0.5 * inverse + shift
    transform_t = transform_t + (1.0 - jnp.sum(transform_t, axis=1, keepdims=True)) * (1.0 / members)
    transform_t = transform_t.astype(bf16)
    weights_t = dot(select, dot(transform_t, select, NT).astype(bf16)).astype(bf16)
    stores = []
    for c in range(chunks):
        fetch(c).wait()
        forecast = forecasts_held[c].reshape(-1, members)
        results[c] = dot(forecast, weights_t, NT).astype(bf16).reshape(cells + (members,))
        store = pltpu.make_async_copy(results.at[c], out_ref.at[rows(c)], out_sem.at[c])
        store.start()
        stores.append(store)
    for store in stores:
        store.wait()


def updated(picked, gathered, member_order, forecast):
    planes, span, height, members = forecast.shape
    count = planes * span * height
    chunks = 8
    while planes % chunks:
        chunks //= 2
    held = (chunks, planes // chunks, span, height, members)
    vmem, hbm = pl.BlockSpec(memory_space=pltpu.VMEM), pl.BlockSpec(memory_space=pltpu.HBM)
    return pl.pallas_call(
        functools.partial(update_kernel, picked),
        in_specs=[vmem] * 3 + [hbm],
        out_specs=hbm,
        out_shape=jax.ShapeDtypeStruct(forecast.shape, jnp.bfloat16),
        scratch_shapes=[
            pltpu.VMEM((members, members), jnp.float32),
            pltpu.VMEM((members, members), jnp.float32),
            pltpu.VMEM(held, jnp.bfloat16),
            pltpu.VMEM(held, jnp.bfloat16),
            pltpu.SemaphoreType.DMA((chunks,)),
            pltpu.SemaphoreType.DMA((chunks,)),
        ],
        compiler_params=params(LIMIT),
        cost_estimate=cost(4 * count * members, 5 * count * members),
    )(gathered, member_order[None, :], member_order[:, None], forecast)


def pairs(count, first):
    low = [(i, i + 1) for i in range(first, count - 1, 2)]
    return low + [(j, i) for i, j in low]


def downstream(value, rate):
    count = lax.axis_size("stream")
    steps = [(i, i + 1) for i in range(count - 1)]
    incoming = lax.ppermute(value, "stream", steps)
    for _ in range(count - 2):
        incoming = lax.ppermute(rate * incoming + value, "stream", steps)
    return incoming


def exchanges(axes):
    for axis in axes:
        count = lax.axis_size(axis)
        if count & (count - 1):
            yield functools.partial(lax.all_gather, axis_name=axis, axis=0, tiled=True)
            continue
        apart = count // 2
        while apart:
            steps = [(i, i ^ apart) for i in range(count)]

            def swap(rows, axis=axis, steps=steps):
                return jnp.concatenate([rows, lax.ppermute(rows, axis, steps)], axis=0)

            yield swap
            apart //= 2


def shards(source, inflow, recovery, obs_rows, obs, observation_weight, member_order):
    planes, span, height, members = source.shape
    levels = lax.axis_size("height")
    parity = (lax.axis_index("height") % 2)[None]
    together = lax.optimization_barrier

    source = pltpu.with_memory_space_constraint(source, pltpu.HBM)
    inflow = pltpu.with_memory_space_constraint(inflow, pltpu.HBM)
    row = border(source, 1 - parity)
    first = lax.ppermute(row, "height", pairs(levels, 0))
    held_recovery, row = together((recovery, row))
    rates = jnp.transpose(held_recovery, (1, 2, 0))
    end_one, picks = march(source, rates, obs_rows, 0, 2)
    high, _ = together((parity, picks))
    row = border(source, high)
    row, first = together((row, first))
    second = lax.ppermute(row, "height", pairs(levels, 1))
    held_rates, picks, row = together((rates, picks, row))
    end_two, picks, share = march(source, held_rates, obs_rows, 1, 2, (recovery, picks, inflow))
    local_end = jnp.concatenate([end_one, end_two], axis=0)
    local_end, second = together((local_end, second))
    total = jnp.prod(recovery, axis=0)[..., None] if lax.axis_size("stream") > 2 else None
    incoming = downstream(local_end, total)
    term, edge, edge_end = edge_march(parity, first, second, rates[:, 0], rates[:, height - 1])
    total_edge = None if total is None else jnp.stack([total[:, 0], total[:, height - 1]])
    last = downstream(edge_end, total_edge)
    rows = observe(obs_rows, obs, observation_weight, picks, share, incoming, edge, last)
    parts = 4 if span % 4 == 0 else 1
    forecast = None
    part = 0
    for swap in exchanges(("height", "span", "stream")):
        swapped = swap(rows)
        if part < parts:
            held_source, rows = together((source, rows))
            forecast = forecasts(held_source, inflow, rates, incoming, term, last, part, parts, forecast)
            swapped, forecast = together((swapped, forecast))
            part += 1
        rows = swapped
    for part in range(part, parts):
        forecast = forecasts(source, inflow, rates, incoming, term, last, part, parts, forecast)
    forecast = pltpu.with_memory_space_constraint(forecast, pltpu.HBM)
    return updated(obs_rows.shape[0], rows, member_order, forecast)


def solution(mesh):
    placed = (
        P("stream", "span", "height", None),
        P("stream", "span", "height", None),
        P("stream", "span", "height"),
        P(("stream", "span", "height")),
        P(("stream", "span", "height")),
        P(("stream", "span", "height")),
        P(),
    )
    return jax.shard_map(
        shards,
        mesh=mesh,
        in_specs=placed,
        out_specs=P("stream", "span", "height", None),
        check_vma=False,
    )
```

```python
import functools

import jax
import jax.numpy as jnp
from jax import lax
from jax.experimental import pallas as pl
from jax.experimental.pallas import tpu as pltpu
from jax.sharding import PartitionSpec as P

vertical_mix = 0.25
MIB = 1024 * 1024
NT = (((1,), (1,)), ((), ()))
NN = (((1,), (0,)), ((), ()))
LIMIT = 24
CUTS = (0, 3, 7, 11, 16)
EXTRA = 8


def dot(a, b, dims=NN):
    return lax.dot_general(a, b, dims, preferred_element_type=jnp.float32)


def params(mib):
    return pltpu.CompilerParams(vmem_limit_bytes=mib * MIB)


def cost(elements, nbytes):
    return pl.CostEstimate(flops=1000 * elements, bytes_accessed=nbytes, transcendentals=0)


def take_border(out_ref, p, block, high):
    span, rows, _ = block.shape
    block = block.astype(jnp.float32)
    low = jnp.concatenate([block[a, :1] for a in range(span)], axis=0)
    top = jnp.concatenate([block[a, rows - 1 :] for a in range(span)], axis=0)
    out_ref[p] = jnp.where(high, top, low).astype(jnp.bfloat16)


def far_border_kernel(high_ref, source_ref, out_ref, held, sems):
    planes, span, rows, members = held.shape
    height = source_ref.shape[2]
    high = high_ref[0] == 1
    start = pl.multiple_of(jnp.where(high, height - rows, 0), rows)
    count = sems.shape[0]
    step = planes // count

    def fetch(c):
        part = pl.ds(c * step, step)
        return pltpu.make_async_copy(
            source_ref.at[part, :, pl.ds(start, rows), :], held.at[part], sems.at[c]
        )

    for c in range(count):
        fetch(c).start()
    for c in range(count):
        fetch(c).wait()
        for p in range(c * step, (c + 1) * step):
            take_border(out_ref, p, held[p], high)


def near_border_kernel(high_ref, source_ref, out_ref):
    high = high_ref[0] == 1
    height = source_ref.shape[2]
    start = pl.multiple_of(jnp.where(high, height - 16, 0), 16)
    for p in range(source_ref.shape[0]):
        take_border(out_ref, p, source_ref[p, :, pl.ds(start, 16), :], high)


def border(source, high, near):
    planes, span, height, members = source.shape
    count = 4 if planes % 4 == 0 else 1
    vmem = pl.BlockSpec(memory_space=pltpu.VMEM)
    scratch = [
        pltpu.VMEM((planes, span, 16, members), jnp.bfloat16),
        pltpu.SemaphoreType.DMA((count,)),
    ]
    return pl.pallas_call(
        near_border_kernel if near else far_border_kernel,
        in_specs=[pl.BlockSpec(memory_space=pltpu.SMEM), vmem if near else pl.BlockSpec(memory_space=pltpu.HBM)],
        out_specs=vmem,
        out_shape=jax.ShapeDtypeStruct((planes, span, members), jnp.bfloat16),
        scratch_shapes=[] if near else scratch,
        compiler_params=params(LIMIT),
        cost_estimate=cost(source.size // 2, source.size),
    )(high, source)


def place_of(r, shape):
    _, span, height = shape
    return r // (span * height), r // height % span, r % height


def group_of(span, height):
    cells = max(1, min(span, 256 // height))
    while span % cells:
        cells -= 1
    return cells


def stencil(rows, height):
    row = lax.broadcasted_iota(jnp.int32, (rows, rows), 0)
    column = lax.broadcasted_iota(jnp.int32, (rows, rows), 1)
    apart = jnp.where(row // height == column // height, jnp.abs(row - column), 2)
    entry = jnp.where(apart == 0, 1.0 - 2.0 * vertical_mix, jnp.where(apart == 1, vertical_mix, 0.0))
    return entry.astype(jnp.bfloat16)


def upright(row):
    count = row.shape[1]
    place = lax.broadcasted_iota(jnp.int32, (count, count), 0)
    lane = lax.broadcasted_iota(jnp.int32, (count, count), 1)
    return jnp.sum(jnp.where(place == lane, row, jnp.zeros_like(row)), axis=1, keepdims=True)


def march_kernel(start, last, *refs):
    if last:
        (rows_ref, rows_row_ref, source_ref, rate_ref, state_ref, recovery_ref, picks_in_ref, inflow_ref,
         end_ref, picks_ref, share_ref, deficits, tiles, through_rows, through) = refs
    else:
        (rows_ref, source_ref, recovery_ref, end_ref, picks_ref, rate_ref, low_rate_ref, high_rate_ref,
         deficits) = refs
    planes, _, members = deficits.shape
    shape = source_ref.shape[:3]
    _, span, height = shape
    count = picks_ref.shape[0]
    cells = group_of(span, height)
    group = cells * height
    if not last:
        blocks = [jnp.transpose(recovery_ref[:, a, :]) for a in range(span)]
        for a in range(span):
            rate_ref[a * height : (a + 1) * height] = blocks[a]
        low_rate_ref[...] = jnp.concatenate([block[:1] for block in blocks], axis=0)
        high_rate_ref[...] = jnp.concatenate([block[height - 1 :] for block in blocks], axis=0)
    mix = stencil(group, height)
    for p in range(planes):
        for c in range(span // cells):
            part = slice(c * group, (c + 1) * group)
            term = dot(mix, source_ref[start + p, c * cells : (c + 1) * cells].reshape(group, members))
            if p == 0 and not last:
                deficits[p, part] = term
            else:
                before = state_ref[part] if p == 0 else deficits[p - 1, part]
                deficits[p, part] = rate_ref[part, start + p : start + p + 1] * before + term
    end_ref[...] = deficits[planes - 1]
    for k in range(count):
        p, a, b = place_of(rows_ref[k], shape)
        inside = jnp.where((p >= start) & (p < start + planes), -1.0, 0.0)
        here = jnp.clip(p - start, 0, planes - 1)
        picks_ref[pl.ds(k, 1), :] = inside * deficits[here, pl.ds(a * height + b, 1), :]
    if last:
        product = None
        for p in range(shape[0]):
            product = recovery_ref[p] if p == 0 else product * recovery_ref[p]
            through[p] = product
        for k in range(count):
            p, a, _ = place_of(rows_ref[k], shape)
            through_rows[pl.ds(k, 1), :] = through[p, pl.ds(a, 1), :]
        cell = upright(rows_row_ref[...].astype(jnp.float32)).astype(jnp.int32) % height
        lane = lax.broadcasted_iota(jnp.int32, (count, height), 1)
        share = jnp.sum(jnp.where(lane == cell, through_rows[...], 0.0), axis=1, keepdims=True)
        share_ref[...] = jnp.broadcast_to(share, share_ref.shape)
        for k in range(count):
            p, a, b = place_of(rows_ref[k], shape)
            first = pl.multiple_of(b // 16 * 16, 16)
            tiles[k] = inflow_ref[p, a, pl.ds(first, 16), :].astype(jnp.float32)
        for k in range(count):
            _, _, b = place_of(rows_ref[k], shape)
            picks_ref[pl.ds(k, 1), :] = (
                picks_ref[pl.ds(k, 1), :] + picks_in_ref[pl.ds(k, 1), :] + tiles[k, pl.ds(b % 16, 1), :]
            )


def march(source, rates, obs_rows, start, stop, more=()):
    shape = source.shape
    _, span, height, members = shape
    observed = obs_rows.shape[0]
    planes, cells = stop - start, span * height
    vmem, smem = pl.BlockSpec(memory_space=pltpu.VMEM), pl.BlockSpec(memory_space=pltpu.SMEM)
    out_shape = [
        jax.ShapeDtypeStruct((cells, members), jnp.float32),
        jax.ShapeDtypeStruct((observed, members), jnp.float32),
    ]
    scratch = [pltpu.VMEM((planes, cells, members), jnp.float32)]
    args = [obs_rows, source, rates]
    in_specs = [smem, vmem, vmem]
    if not more:
        out_shape += [
            jax.ShapeDtypeStruct((cells, shape[0]), jnp.float32),
            jax.ShapeDtypeStruct((span, shape[0]), jnp.float32),
            jax.ShapeDtypeStruct((span, shape[0]), jnp.float32),
        ]
    else:
        state, recovery, picks, inflow = more
        in_specs = [smem] + [vmem] * 7
        args = [obs_rows, obs_rows[None, :], source, rates, state, recovery, picks, inflow]
        out_shape.append(jax.ShapeDtypeStruct((observed, members), jnp.float32))
        scratch += [
            pltpu.VMEM((observed, 16, members), jnp.float32),
            pltpu.VMEM((observed, height), jnp.float32),
            pltpu.VMEM(shape[:3], jnp.float32),
        ]
    size = planes * cells * members
    return pl.pallas_call(
        functools.partial(march_kernel, start, bool(more)),
        in_specs=in_specs,
        out_specs=[vmem] * len(out_shape),
        out_shape=out_shape,
        scratch_shapes=scratch,
        compiler_params=params(LIMIT),
        cost_estimate=cost(3 * size, 4 * size),
    )(*args)


def edge_kernel(
    parity_ref, first_ref, second_ref, low_rate_ref, high_rate_ref, end_ref, term_ref, edge_ref, leaving_ref
):
    planes, span, members = first_ref.shape
    height = leaving_ref.shape[1]
    even = parity_ref[0] == 0
    low, high = None, None
    for p in range(planes):
        one = vertical_mix * first_ref[p].astype(jnp.float32)
        two = vertical_mix * second_ref[p].astype(jnp.float32)
        low_term = jnp.where(even, two, one)
        high_term = jnp.where(even, one, two)
        term_ref[0, p] = low_term
        term_ref[1, p] = high_term
        low = low_term if p == 0 else low_rate_ref[:, p : p + 1] * low + low_term
        high = high_term if p == 0 else high_rate_ref[:, p : p + 1] * high + high_term
        edge_ref[0, p] = low
        edge_ref[1, p] = high
    row = lax.broadcasted_iota(jnp.int32, (height, members), 0)
    for a in range(span):
        share = jnp.where(row == 0, low[a : a + 1], jnp.where(row == height - 1, high[a : a + 1], 0.0))
        leaving_ref[a] = end_ref[a * height : (a + 1) * height] + share


def edge_march(parity, first, second, low_rate, high_rate, end):
    planes, span, members = first.shape
    vmem = pl.BlockSpec(memory_space=pltpu.VMEM)
    return pl.pallas_call(
        edge_kernel,
        in_specs=[pl.BlockSpec(memory_space=pltpu.SMEM)] + [vmem] * 5,
        out_specs=[vmem] * 3,
        out_shape=[
            jax.ShapeDtypeStruct((2, planes, span, members), jnp.float32),
            jax.ShapeDtypeStruct((2, planes, span, members), jnp.float32),
            jax.ShapeDtypeStruct((span, end.shape[0] // span, members), jnp.float32),
        ],
        compiler_params=params(LIMIT),
        cost_estimate=cost(first.size, 8 * first.size),
    )(parity, first, second, low_rate, high_rate, end)


def observe_kernel(
    rows_ref, obs_ref, weight_ref, picks_ref, share_ref, incoming_ref, edge_ref, out_ref, arriving, halo
):
    planes = edge_ref.shape[1]
    span, height, members = incoming_ref.shape
    count = picks_ref.shape[0]
    for k in range(count):
        p, a, b = place_of(rows_ref[k], (planes, span, height))
        side = jnp.where(b == height - 1, 1, 0)
        at_edge = jnp.where((b == 0) | (b == height - 1), 1.0, 0.0)
        arriving[pl.ds(k, 1), :] = incoming_ref[a, pl.ds(b, 1), :]
        halo[pl.ds(k, 1), :] = at_edge * edge_ref[side, p, pl.ds(a, 1), :]
    forecast = picks_ref[...] - halo[...] - share_ref[...] * arriving[...]
    mean = jnp.sum(forecast, axis=1, keepdims=True) * (1.0 / members)
    anomaly = (forecast - mean).astype(jnp.bfloat16).astype(jnp.float32)
    weight = upright(weight_ref[...])
    observed = weight * anomaly
    misfit = weight * (upright(obs_ref[...]) - mean)
    projection = jnp.sum(observed * misfit, axis=0, keepdims=True)
    one = projection.astype(jnp.bfloat16).astype(jnp.float32)
    two = (projection - one).astype(jnp.bfloat16).astype(jnp.float32)
    three = projection - one - two
    row = lax.broadcasted_iota(jnp.int32, (EXTRA, members), 0)
    pieces = jnp.where(row == 0, one, jnp.where(row == 1, two, jnp.where(row == 2, three, 0.0)))
    out_ref[...] = jnp.concatenate([observed, pieces], axis=0).astype(jnp.bfloat16)


def observe(obs_rows, obs, weight, picks, share, incoming, edge):
    count, members = picks.shape
    vmem = pl.BlockSpec(memory_space=pltpu.VMEM)
    return pl.pallas_call(
        observe_kernel,
        in_specs=[pl.BlockSpec(memory_space=pltpu.SMEM)] + [vmem] * 6,
        out_specs=vmem,
        out_shape=jax.ShapeDtypeStruct((count + EXTRA, members), jnp.bfloat16),
        scratch_shapes=[pltpu.VMEM((count, members), jnp.float32)] * 2,
        compiler_params=params(LIMIT),
        cost_estimate=cost(40 * count * members, 64 * count * members),
    )(obs_rows, obs[None, :], weight[None, :], picks, share, incoming, edge)


def forecast_kernel(start, planes, source_ref, inflow_ref, rate_ref, state_ref, term_ref, *refs):
    out_ref, end_ref = refs[-2:]
    _, span, height, members = source_ref.shape
    cells = group_of(span, height)
    group = cells * height
    mix = stencil(group, height)
    row = lax.broadcasted_iota(jnp.int32, (height, members), 0)
    for p in range(start, start + planes):
        before = state_ref if p == start else end_ref
        for c in range(span // cells):
            term = dot(mix, source_ref[p, c * cells : (c + 1) * cells].reshape(group, members))
            for a in range(c * cells, (c + 1) * cells):
                part = slice(a * height, (a + 1) * height)
                low, high = term_ref[0, p, a : a + 1, :], term_ref[1, p, a : a + 1, :]
                halo = jnp.where(row == 0, low, jnp.where(row == height - 1, high, 0.0))
                deficit = rate_ref[part, p : p + 1] * before[part] + (
                    term[a * height - c * group : (a + 1) * height - c * group] + halo
                )
                end_ref[part] = deficit
                out_ref[p - start, a] = (inflow_ref[p, a].astype(jnp.float32) - deficit).astype(jnp.bfloat16)


def forecasts(source, inflow, rates, state, term, start, stop):
    planes = stop - start
    vmem = pl.BlockSpec(memory_space=pltpu.VMEM)
    size = state.size * planes
    return pl.pallas_call(
        functools.partial(forecast_kernel, start, planes),
        in_specs=[vmem] * 5,
        out_specs=[vmem, vmem],
        out_shape=[
            pltpu.VMEM((planes,) + source.shape[1:], jnp.bfloat16),
            jax.ShapeDtypeStruct(state.shape, jnp.float32),
        ],
        compiler_params=params(LIMIT),
        cost_estimate=cost(4 * size, 6 * size),
    )(source, inflow, rates, state, term)


def halves(x):
    big = x.astype(jnp.bfloat16)
    return big, (x - big.astype(jnp.float32)).astype(jnp.bfloat16)


def fine_dot(a, b, dims=NN):
    a_big, a_small = halves(a)
    b_big, b_small = halves(b)
    return dot(a_big, b_big, dims) + (dot(a_big, b_small, dims) + dot(a_small, b_big, dims))


def update_kernel(picked, gathered_ref, order_ref, *refs):
    forecast_refs = refs[:-5]
    out_ref, gram, factor, results, out_sem = refs[-5:]
    total, members = gathered_ref.shape
    bf16, f32 = jnp.bfloat16, jnp.float32
    row = lax.broadcasted_iota(jnp.int32, (members, members), 0)
    column = lax.broadcasted_iota(jnp.int32, (members, members), 1)
    select = jnp.where(order_ref[...] == row, 1.0, 0.0).astype(bf16)
    select_t = jnp.where(upright(order_ref[...].astype(f32)) == column.astype(f32), 1.0, 0.0).astype(bf16)
    block = picked + EXTRA
    gathered = gathered_ref[...]
    place = lax.broadcasted_iota(jnp.int32, (total, members), 0) % block
    observed = jnp.where(place < picked, gathered.astype(f32), 0.0).astype(bf16)
    ordered_t = dot(select_t, observed, NT).astype(bf16)
    slot = lax.broadcasted_iota(jnp.int32, (16, total), 1) % block
    pieces = dot(jnp.where(slot >= picked, 1.0, 0.0).astype(bf16), gathered)
    piece_one = pieces.astype(bf16)
    piece_two, piece_three = halves(pieces - piece_one.astype(f32))
    projection = dot(piece_one, select) + (dot(piece_two, select) + dot(piece_three, select))
    diagonal = row == column
    full = dot(ordered_t, ordered_t, NT) + jnp.where(diagonal, members - 1.0, 0.0)
    on_diagonal = jnp.where(diagonal, full, 0.0)
    scale_row = lax.rsqrt(jnp.sum(on_diagonal, axis=0, keepdims=True))
    scale_column = lax.rsqrt(jnp.sum(on_diagonal, axis=1, keepdims=True))
    unit = full * scale_row * scale_column
    gram[...] = full
    lower = row > column

    def lower_part(residual):
        return jnp.where(lower, residual, jnp.where(diagonal, 0.5 * residual, 0.0))

    identity = jnp.where(diagonal, 1.0, 0.0)
    factor[...] = identity - jnp.where(lower, unit, 0.0)
    unit_big = unit.astype(bf16)
    for _ in range(2):
        inverse = factor[...]
        inverse_big = inverse.astype(bf16)
        half_way = dot(inverse_big, unit_big).astype(bf16)
        residual = dot(half_way, inverse_big, NT) - identity
        factor[...] = inverse - dot(lower_part(residual).astype(bf16), inverse_big)

    def refine(carried):
        step, _ = carried
        inverse = factor[...]
        residual = fine_dot(fine_dot(inverse, unit), inverse, NT) - identity
        factor[...] = inverse - dot(lower_part(residual).astype(bf16), inverse.astype(bf16))
        return step + 1, jnp.sum(residual * residual)

    def unfinished(carried):
        step, error = carried
        return (step < 8) & (error > 0.04) & (error < 64.0)

    _, error = lax.while_loop(unfinished, refine, (0, jnp.float32(1.0)))
    factor[...] = factor[...] * scale_row

    @pl.when(jnp.logical_not(error <= 0.04))
    def _():
        factor[...] = identity

        def eliminate(k, carry):
            held = gram[...]
            pivot_row = gram[pl.ds(k, 1), :]
            pivot = jnp.sum(jnp.where(column[:1] == k, pivot_row, 0.0), axis=1, keepdims=True)
            pivot_column = jnp.sum(jnp.where(column == k, held, 0.0), axis=1, keepdims=True)
            share = jnp.where(row[:, :1] > k, pivot_column / pivot, 0.0)
            factor[...] = factor[...] - share * factor[pl.ds(k, 1), :]
            gram[...] = held - share * pivot_row
            return carry

        lax.fori_loop(0, members, eliminate, 0)
        pivots = jnp.sum(jnp.where(diagonal, gram[...], 0.0), axis=1, keepdims=True)
        factor[...] = factor[...] * lax.rsqrt(pivots)

    inverse = factor[...]
    coefficients = fine_dot(projection, inverse, NT)
    shift = fine_dot(coefficients, inverse)[:1]
    transform_t = (members - 1.0) ** 0.5 * inverse + shift
    transform_t = transform_t + (1.0 - jnp.sum(transform_t, axis=1, keepdims=True)) * (1.0 / members)
    transform_t = transform_t.astype(bf16)
    weights_t = dot(select, dot(transform_t, select, NT).astype(bf16)).astype(bf16)
    stores = []
    for ref in forecast_refs:
        for p in range(ref.shape[0]):
            at = len(stores)
            forecast = ref[p].reshape(-1, members)
            results[at] = dot(forecast, weights_t, NT).astype(bf16).reshape(ref.shape[1:])
            store = pltpu.make_async_copy(results.at[at], out_ref.at[at], out_sem.at[at])
            store.start()
            stores.append(store)
    for store in stores:
        store.wait()


def updated(picked, gathered, member_order, forecasts, shape):
    planes, span, height, members = shape
    size = planes * span * height * members
    vmem = pl.BlockSpec(memory_space=pltpu.VMEM)
    return pl.pallas_call(
        functools.partial(update_kernel, picked),
        in_specs=[vmem] * (2 + len(forecasts)),
        out_specs=pl.BlockSpec(memory_space=pltpu.HBM),
        out_shape=jax.ShapeDtypeStruct(shape, jnp.bfloat16),
        scratch_shapes=[
            pltpu.VMEM((members, members), jnp.float32),
            pltpu.VMEM((members, members), jnp.float32),
            pltpu.VMEM(shape, jnp.bfloat16),
            pltpu.SemaphoreType.DMA((planes,)),
        ],
        compiler_params=params(LIMIT),
        cost_estimate=cost(4 * size, 5 * size),
    )(gathered, member_order[None, :], *forecasts)


def pairs(count, first):
    low = [(i, i + 1) for i in range(first, count - 1, 2)]
    return low + [(j, i) for i, j in low]


def downstream(value, rate):
    count = lax.axis_size("stream")
    steps = [(i, i + 1) for i in range(count - 1)]
    incoming = lax.ppermute(value, "stream", steps)
    for _ in range(count - 2):
        incoming = lax.ppermute(rate * incoming + value, "stream", steps)
    return incoming


def exchanges(axes):
    for axis in axes:
        count = lax.axis_size(axis)
        if count & (count - 1):
            yield functools.partial(lax.all_gather, axis_name=axis, axis=0, tiled=True)
            continue
        apart = count // 2
        while apart:
            steps = [(i, i ^ apart) for i in range(count)]

            def swap(rows, axis=axis, steps=steps):
                return jnp.concatenate([rows, lax.ppermute(rows, axis, steps)], axis=0)

            yield swap
            apart //= 2


def shards(source, inflow, recovery, obs_rows, obs, observation_weight, member_order):
    planes, span, height, members = source.shape
    levels = lax.axis_size("height")
    parity = (lax.axis_index("height") % 2)[None]
    together = lax.optimization_barrier

    row = border(pltpu.with_memory_space_constraint(source, pltpu.HBM), 1 - parity, False)
    source = pltpu.with_memory_space_constraint(source, pltpu.VMEM)
    inflow = pltpu.with_memory_space_constraint(inflow, pltpu.VMEM)
    first = lax.ppermute(row, "height", pairs(levels, 0))
    middle = (planes + 1) // 2
    held_recovery, row = together((recovery, row))
    state, picks, rates, low_rate, high_rate = march(source, held_recovery, obs_rows, 0, middle)
    high, _ = together((parity, picks))
    row = border(source, high, True)
    row, first = together((row, first))
    second = lax.ppermute(row, "height", pairs(levels, 1))
    held_rates, picks, row = together((rates, picks, row))
    end, picks, share = march(source, held_rates, obs_rows, middle, planes, (state, recovery, picks, inflow))
    end, second = together((end, second))
    term, edge, leaving = edge_march(parity, first, second, low_rate, high_rate, end)
    total = jnp.prod(recovery, axis=0)[..., None] if lax.axis_size("stream") > 2 else None
    incoming = downstream(leaving, total)
    rows = observe(obs_rows, obs, observation_weight, picks, share, incoming, edge)
    state = incoming.reshape(span * height, members)
    cuts = [planes * part // 16 for part in CUTS]
    parts = []
    for swap in exchanges(("height", "span", "stream")):
        swapped = swap(rows)
        if len(cuts) > 1:
            state, rows = together((state, rows))
            forecast, state = forecasts(source, inflow, rates, state, term, cuts[0], cuts[1])
            swapped, state, forecast = together((swapped, state, forecast))
            parts.append(forecast)
            cuts = cuts[1:]
        rows = swapped
    while len(cuts) > 1:
        forecast, state = forecasts(source, inflow, rates, state, term, cuts[0], cuts[1])
        parts.append(forecast)
        cuts = cuts[1:]
    return updated(obs_rows.shape[0], rows, member_order, parts, source.shape)


def solution(mesh):
    placed = (
        P("stream", "span", "height", None),
        P("stream", "span", "height", None),
        P("stream", "span", "height"),
        P(("stream", "span", "height")),
        P(("stream", "span", "height")),
        P(("stream", "span", "height")),
        P(),
    )
    return jax.shard_map(
        shards,
        mesh=mesh,
        in_specs=placed,
        out_specs=P("stream", "span", "height", None),
        check_vma=False,
    )
```

```python
import functools

import jax
import jax.numpy as jnp
from jax import lax
from jax.experimental import pallas as pl
from jax.experimental.pallas import tpu as pltpu
from jax.sharding import PartitionSpec as P

vertical_mix = 0.25
MIB = 1024 * 1024
NT = (((1,), (1,)), ((), ()))
NN = (((1,), (0,)), ((), ()))
LIMIT = 24
CUTS = (0, 4, 8, 12, 16)
EXTRA = 8


def dot(a, b, dims=NN):
    return lax.dot_general(a, b, dims, preferred_element_type=jnp.float32)


def params(mib):
    return pltpu.CompilerParams(vmem_limit_bytes=mib * MIB)


def cost(elements, nbytes):
    return pl.CostEstimate(flops=1000 * elements, bytes_accessed=nbytes, transcendentals=0)


def border_kernel(parity_ref, source_ref, held_ref, first_ref, second_ref, sems):
    planes, span, height, _ = source_ref.shape
    even = parity_ref[0] == 0

    def fetch(p):
        return pltpu.make_async_copy(source_ref.at[p], held_ref.at[p], sems.at[p])

    for p in range(planes):
        fetch(p).start()
    for p in range(planes):
        fetch(p).wait()
        low = held_ref[p, :, :16].astype(jnp.float32)
        top = held_ref[p, :, height - 16 :].astype(jnp.float32)
        low = jnp.concatenate([low[a, :1] for a in range(span)], axis=0)
        top = jnp.concatenate([top[a, 15:] for a in range(span)], axis=0)
        first_ref[p] = jnp.where(even, top, low).astype(jnp.bfloat16)
        second_ref[p] = jnp.where(even, low, top).astype(jnp.bfloat16)


def border(source, parity):
    planes, span, height, members = source.shape
    vmem = pl.BlockSpec(memory_space=pltpu.VMEM)
    row = jax.ShapeDtypeStruct((planes, span, members), jnp.bfloat16)
    return pl.pallas_call(
        border_kernel,
        in_specs=[pl.BlockSpec(memory_space=pltpu.SMEM), pl.BlockSpec(memory_space=pltpu.HBM)],
        out_specs=[vmem] * 3,
        out_shape=[pltpu.VMEM(source.shape, jnp.bfloat16), row, row],
        scratch_shapes=[pltpu.SemaphoreType.DMA((planes,))],
        compiler_params=params(LIMIT),
        cost_estimate=cost(source.size, source.size),
    )(parity, pltpu.with_memory_space_constraint(source, pltpu.HBM))


def place_of(r, shape):
    _, span, height = shape
    return r // (span * height), r // height % span, r % height


def group_of(span, height):
    cells = max(1, min(span, 256 // height))
    while span % cells:
        cells -= 1
    return cells


def stencil(rows, height):
    row = lax.broadcasted_iota(jnp.int32, (rows, rows), 0)
    column = lax.broadcasted_iota(jnp.int32, (rows, rows), 1)
    apart = jnp.where(row // height == column // height, jnp.abs(row - column), 2)
    entry = jnp.where(apart == 0, 1.0 - 2.0 * vertical_mix, jnp.where(apart == 1, vertical_mix, 0.0))
    return entry.astype(jnp.bfloat16)


def upright(row):
    count = row.shape[1]
    place = lax.broadcasted_iota(jnp.int32, (count, count), 0)
    lane = lax.broadcasted_iota(jnp.int32, (count, count), 1)
    return jnp.sum(jnp.where(place == lane, row, jnp.zeros_like(row)), axis=1, keepdims=True)


def march_kernel(
    rows_ref, rows_row_ref, source_ref, recovery_ref, inflow_ref,
    end_ref, picks_ref, share_ref, rate_ref, low_rate_ref, high_rate_ref,
    deficits, tiles, through_rows, through,
):
    shape = source_ref.shape[:3]
    planes, span, height = shape
    count, members = picks_ref.shape
    cells = group_of(span, height)
    group = cells * height
    blocks = [jnp.transpose(recovery_ref[:, a, :]) for a in range(span)]
    for a in range(span):
        rate_ref[a * height : (a + 1) * height] = blocks[a]
    low_rate_ref[...] = jnp.concatenate([block[:1] for block in blocks], axis=0)
    high_rate_ref[...] = jnp.concatenate([block[height - 1 :] for block in blocks], axis=0)
    mix = stencil(group, height)
    product = None
    for p in range(planes):
        product = recovery_ref[p] if p == 0 else product * recovery_ref[p]
        through[p] = product
        for c in range(span // cells):
            part = slice(c * group, (c + 1) * group)
            term = dot(mix, source_ref[p, c * cells : (c + 1) * cells].reshape(group, members))
            if p > 0:
                term = rate_ref[part, p : p + 1] * deficits[p - 1, part] + term
            deficits[p, part] = term
    end_ref[...] = deficits[planes - 1]
    for k in range(count):
        p, a, b = place_of(rows_ref[k], shape)
        first = pl.multiple_of(b // 16 * 16, 16)
        tiles[k] = inflow_ref[p, a, pl.ds(first, 16), :].astype(jnp.float32)
        through_rows[pl.ds(k, 1), :] = through[p, pl.ds(a, 1), :]
    for k in range(count):
        p, a, b = place_of(rows_ref[k], shape)
        picks_ref[pl.ds(k, 1), :] = (
            tiles[k, pl.ds(b % 16, 1), :] - deficits[p, pl.ds(a * height + b, 1), :]
        )
    cell = upright(rows_row_ref[...].astype(jnp.float32)).astype(jnp.int32) % height
    lane = lax.broadcasted_iota(jnp.int32, (count, height), 1)
    share = jnp.sum(jnp.where(lane == cell, through_rows[...], 0.0), axis=1, keepdims=True)
    share_ref[...] = jnp.broadcast_to(share, share_ref.shape)


def march(source, inflow, recovery, obs_rows):
    planes, span, height, members = source.shape
    observed = obs_rows.shape[0]
    cells = span * height
    f32 = jnp.float32
    vmem = pl.BlockSpec(memory_space=pltpu.VMEM)
    return pl.pallas_call(
        march_kernel,
        in_specs=[pl.BlockSpec(memory_space=pltpu.SMEM)] + [vmem] * 4,
        out_specs=[vmem] * 6,
        out_shape=[
            jax.ShapeDtypeStruct((cells, members), f32),
            jax.ShapeDtypeStruct((observed, members), f32),
            jax.ShapeDtypeStruct((observed, members), f32),
            jax.ShapeDtypeStruct((cells, planes), f32),
            jax.ShapeDtypeStruct((span, planes), f32),
            jax.ShapeDtypeStruct((span, planes), f32),
        ],
        scratch_shapes=[
            pltpu.VMEM((planes, cells, members), f32),
            pltpu.VMEM((observed, 16, members), f32),
            pltpu.VMEM((observed, height), f32),
            pltpu.VMEM((planes, span, height), f32),
        ],
        compiler_params=params(LIMIT),
        cost_estimate=cost(3 * source.size, 4 * source.size),
    )(obs_rows, obs_rows[None, :], source, recovery, inflow)


def edge_kernel(
    parity_ref, first_ref, second_ref, low_rate_ref, high_rate_ref, end_ref, term_ref, edge_ref, leaving_ref
):
    planes, span, members = first_ref.shape
    height = leaving_ref.shape[1]
    even = parity_ref[0] == 0
    low, high = None, None
    for p in range(planes):
        one = vertical_mix * first_ref[p].astype(jnp.float32)
        two = vertical_mix * second_ref[p].astype(jnp.float32)
        low_term = jnp.where(even, two, one)
        high_term = jnp.where(even, one, two)
        term_ref[0, p] = low_term
        term_ref[1, p] = high_term
        low = low_term if p == 0 else low_rate_ref[:, p : p + 1] * low + low_term
        high = high_term if p == 0 else high_rate_ref[:, p : p + 1] * high + high_term
        edge_ref[0, p] = low
        edge_ref[1, p] = high
    row = lax.broadcasted_iota(jnp.int32, (height, members), 0)
    for a in range(span):
        share = jnp.where(row == 0, low[a : a + 1], jnp.where(row == height - 1, high[a : a + 1], 0.0))
        leaving_ref[a] = end_ref[a * height : (a + 1) * height] + share


def edge_march(parity, first, second, low_rate, high_rate, end):
    planes, span, members = first.shape
    vmem = pl.BlockSpec(memory_space=pltpu.VMEM)
    return pl.pallas_call(
        edge_kernel,
        in_specs=[pl.BlockSpec(memory_space=pltpu.SMEM)] + [vmem] * 5,
        out_specs=[vmem] * 3,
        out_shape=[
            jax.ShapeDtypeStruct((2, planes, span, members), jnp.float32),
            jax.ShapeDtypeStruct((2, planes, span, members), jnp.float32),
            jax.ShapeDtypeStruct((span, end.shape[0] // span, members), jnp.float32),
        ],
        compiler_params=params(LIMIT),
        cost_estimate=cost(first.size, 8 * first.size),
    )(parity, first, second, low_rate, high_rate, end)


def observe_kernel(
    rows_ref, obs_ref, weight_ref, picks_ref, share_ref, incoming_ref, edge_ref, out_ref, arriving, halo
):
    planes = edge_ref.shape[1]
    span, height, members = incoming_ref.shape
    count = picks_ref.shape[0]
    for k in range(count):
        p, a, b = place_of(rows_ref[k], (planes, span, height))
        side = jnp.where(b == height - 1, 1, 0)
        at_edge = jnp.where((b == 0) | (b == height - 1), 1.0, 0.0)
        arriving[pl.ds(k, 1), :] = incoming_ref[a, pl.ds(b, 1), :]
        halo[pl.ds(k, 1), :] = at_edge * edge_ref[side, p, pl.ds(a, 1), :]
    forecast = picks_ref[...] - halo[...] - share_ref[...] * arriving[...]
    mean = jnp.sum(forecast, axis=1, keepdims=True) * (1.0 / members)
    anomaly = (forecast - mean).astype(jnp.bfloat16).astype(jnp.float32)
    weight = upright(weight_ref[...])
    observed = weight * anomaly
    misfit = weight * (upright(obs_ref[...]) - mean)
    projection = jnp.sum(observed * misfit, axis=0, keepdims=True)
    one = projection.astype(jnp.bfloat16).astype(jnp.float32)
    two = (projection - one).astype(jnp.bfloat16).astype(jnp.float32)
    three = projection - one - two
    row = lax.broadcasted_iota(jnp.int32, (EXTRA, members), 0)
    pieces = jnp.where(row == 0, one, jnp.where(row == 1, two, jnp.where(row == 2, three, 0.0)))
    out_ref[...] = jnp.concatenate([observed, pieces], axis=0).astype(jnp.bfloat16)


def observe(obs_rows, obs, weight, picks, share, incoming, edge):
    count, members = picks.shape
    vmem = pl.BlockSpec(memory_space=pltpu.VMEM)
    return pl.pallas_call(
        observe_kernel,
        in_specs=[pl.BlockSpec(memory_space=pltpu.SMEM)] + [vmem] * 6,
        out_specs=vmem,
        out_shape=jax.ShapeDtypeStruct((count + EXTRA, members), jnp.bfloat16),
        scratch_shapes=[pltpu.VMEM((count, members), jnp.float32)] * 2,
        compiler_params=params(LIMIT),
        cost_estimate=cost(40 * count * members, 64 * count * members),
    )(obs_rows, obs[None, :], weight[None, :], picks, share, incoming, edge)


def forecast_kernel(start, planes, source_ref, inflow_ref, rate_ref, state_ref, term_ref, *refs):
    out_ref, end_ref = refs[-2:]
    _, span, height, members = source_ref.shape
    cells = group_of(span, height)
    group = cells * height
    mix = stencil(group, height)
    row = lax.broadcasted_iota(jnp.int32, (height, members), 0)
    for p in range(start, start + planes):
        before = state_ref if p == start else end_ref
        for c in range(span // cells):
            term = dot(mix, source_ref[p, c * cells : (c + 1) * cells].reshape(group, members))
            for a in range(c * cells, (c + 1) * cells):
                part = slice(a * height, (a + 1) * height)
                low, high = term_ref[0, p, a : a + 1, :], term_ref[1, p, a : a + 1, :]
                halo = jnp.where(row == 0, low, jnp.where(row == height - 1, high, 0.0))
                deficit = rate_ref[part, p : p + 1] * before[part] + (
                    term[a * height - c * group : (a + 1) * height - c * group] + halo
                )
                end_ref[part] = deficit
                out_ref[p - start, a] = (inflow_ref[p, a].astype(jnp.float32) - deficit).astype(jnp.bfloat16)


def forecasts(source, inflow, rates, state, term, start, stop):
    planes = stop - start
    vmem = pl.BlockSpec(memory_space=pltpu.VMEM)
    size = state.size * planes
    return pl.pallas_call(
        functools.partial(forecast_kernel, start, planes),
        in_specs=[vmem] * 5,
        out_specs=[vmem, vmem],
        out_shape=[
            pltpu.VMEM((planes,) + source.shape[1:], jnp.bfloat16),
            jax.ShapeDtypeStruct(state.shape, jnp.float32),
        ],
        compiler_params=params(LIMIT),
        cost_estimate=cost(4 * size, 6 * size),
    )(source, inflow, rates, state, term)


def halves(x):
    big = x.astype(jnp.bfloat16)
    return big, (x - big.astype(jnp.float32)).astype(jnp.bfloat16)


def fine_dot(a, b, dims=NN):
    a_big, a_small = halves(a)
    b_big, b_small = halves(b)
    return dot(a_big, b_big, dims) + (dot(a_big, b_small, dims) + dot(a_small, b_big, dims))


def update_kernel(picked, gathered_ref, order_ref, *refs):
    forecast_refs = refs[:-5]
    out_ref, gram, factor, results, out_sem = refs[-5:]
    total, members = gathered_ref.shape
    bf16, f32 = jnp.bfloat16, jnp.float32
    row = lax.broadcasted_iota(jnp.int32, (members, members), 0)
    column = lax.broadcasted_iota(jnp.int32, (members, members), 1)
    select = jnp.where(order_ref[...] == row, 1.0, 0.0).astype(bf16)
    select_t = jnp.where(upright(order_ref[...].astype(f32)) == column.astype(f32), 1.0, 0.0).astype(bf16)
    block = picked + EXTRA
    gathered = gathered_ref[...]
    place = lax.broadcasted_iota(jnp.int32, (total, members), 0) % block
    observed = jnp.where(place < picked, gathered.astype(f32), 0.0).astype(bf16)
    ordered_t = dot(select_t, observed, NT).astype(bf16)
    slot = lax.broadcasted_iota(jnp.int32, (16, total), 1) % block
    pieces = dot(jnp.where(slot >= picked, 1.0, 0.0).astype(bf16), gathered)
    piece_one = pieces.astype(bf16)
    piece_two, piece_three = halves(pieces - piece_one.astype(f32))
    projection = dot(piece_one, select) + (dot(piece_two, select) + dot(piece_three, select))
    diagonal = row == column
    full = dot(ordered_t, ordered_t, NT) + jnp.where(diagonal, members - 1.0, 0.0)
    on_diagonal = jnp.where(diagonal, full, 0.0)
    scale_row = lax.rsqrt(jnp.sum(on_diagonal, axis=0, keepdims=True))
    scale_column = lax.rsqrt(jnp.sum(on_diagonal, axis=1, keepdims=True))
    unit = full * scale_row * scale_column
    gram[...] = full
    lower = row > column

    def lower_part(residual):
        return jnp.where(lower, residual, jnp.where(diagonal, 0.5 * residual, 0.0))

    identity = jnp.where(diagonal, 1.0, 0.0)
    factor[...] = identity - jnp.where(lower, unit, 0.0)
    unit_big = unit.astype(bf16)
    for _ in range(2):
        inverse = factor[...]
        inverse_big = inverse.astype(bf16)
        half_way = dot(inverse_big, unit_big).astype(bf16)
        residual = dot(half_way, inverse_big, NT) - identity
        factor[...] = inverse - dot(lower_part(residual).astype(bf16), inverse_big)

    def refine(carried):
        step, _ = carried
        inverse = factor[...]
        residual = fine_dot(fine_dot(inverse, unit), inverse, NT) - identity
        factor[...] = inverse - dot(lower_part(residual).astype(bf16), inverse.astype(bf16))
        return step + 1, jnp.sum(residual * residual)

    def unfinished(carried):
        step, error = carried
        return (step < 8) & (error > 0.04) & (error < 64.0)

    _, error = lax.while_loop(unfinished, refine, (0, jnp.float32(1.0)))
    factor[...] = factor[...] * scale_row

    @pl.when(jnp.logical_not(error <= 0.04))
    def _():
        factor[...] = identity

        def eliminate(k, carry):
            held = gram[...]
            pivot_row = gram[pl.ds(k, 1), :]
            pivot = jnp.sum(jnp.where(column[:1] == k, pivot_row, 0.0), axis=1, keepdims=True)
            pivot_column = jnp.sum(jnp.where(column == k, held, 0.0), axis=1, keepdims=True)
            share = jnp.where(row[:, :1] > k, pivot_column / pivot, 0.0)
            factor[...] = factor[...] - share * factor[pl.ds(k, 1), :]
            gram[...] = held - share * pivot_row
            return carry

        lax.fori_loop(0, members, eliminate, 0)
        pivots = jnp.sum(jnp.where(diagonal, gram[...], 0.0), axis=1, keepdims=True)
        factor[...] = factor[...] * lax.rsqrt(pivots)

    inverse = factor[...]
    coefficients = fine_dot(projection, inverse, NT)
    shift = fine_dot(coefficients, inverse)[:1]
    transform_t = (members - 1.0) ** 0.5 * inverse + shift
    transform_t = transform_t + (1.0 - jnp.sum(transform_t, axis=1, keepdims=True)) * (1.0 / members)
    transform_t = transform_t.astype(bf16)
    weights_t = dot(select, dot(transform_t, select, NT).astype(bf16)).astype(bf16)
    stores = []
    for ref in forecast_refs:
        for p in range(ref.shape[0]):
            at = len(stores)
            forecast = ref[p].reshape(-1, members)
            results[at] = dot(forecast, weights_t, NT).astype(bf16).reshape(ref.shape[1:])
            store = pltpu.make_async_copy(results.at[at], out_ref.at[at], out_sem.at[at])
            store.start()
            stores.append(store)
    for store in stores:
        store.wait()


def updated(picked, gathered, member_order, forecasts, shape):
    planes, span, height, members = shape
    size = planes * span * height * members
    vmem = pl.BlockSpec(memory_space=pltpu.VMEM)
    return pl.pallas_call(
        functools.partial(update_kernel, picked),
        in_specs=[vmem] * (2 + len(forecasts)),
        out_specs=pl.BlockSpec(memory_space=pltpu.HBM),
        out_shape=jax.ShapeDtypeStruct(shape, jnp.bfloat16),
        scratch_shapes=[
            pltpu.VMEM((members, members), jnp.float32),
            pltpu.VMEM((members, members), jnp.float32),
            pltpu.VMEM(shape, jnp.bfloat16),
            pltpu.SemaphoreType.DMA((planes,)),
        ],
        compiler_params=params(LIMIT),
        cost_estimate=cost(4 * size, 5 * size),
    )(gathered, member_order[None, :], *forecasts)


def pairs(count, first):
    low = [(i, i + 1) for i in range(first, count - 1, 2)]
    return low + [(j, i) for i, j in low]


def downstream(value, rate):
    count = lax.axis_size("stream")
    steps = [(i, i + 1) for i in range(count - 1)]
    incoming = lax.ppermute(value, "stream", steps)
    for _ in range(count - 2):
        incoming = lax.ppermute(rate * incoming + value, "stream", steps)
    return incoming


def rounds():
    steps = []
    for axis in ("height", "span"):
        bits = (lax.axis_size(axis) - 1).bit_length()
        steps.append([(axis, 1 << bit) for bit in reversed(range(bits))])
    mixed = []
    while steps[0] or steps[1]:
        pair = [axis.pop(0) for axis in steps if axis]
        mixed += [(pair[0], pair[-1]), (pair[-1], pair[0])][: len(pair)]
    return mixed


def exchanges():
    axes = ("stream", "span", "height")
    sizes = [lax.axis_size(axis) for axis in axes]
    if any(size & (size - 1) for size in sizes):
        yield functools.partial(lax.all_gather, axis_name=axes, axis=0, tiled=True)
        return

    def flat(place):
        return (place["stream"] * sizes[1] + place["span"]) * sizes[2] + place["height"]

    places = [
        {"stream": i // (sizes[1] * sizes[2]), "span": i // sizes[2] % sizes[1], "height": i % sizes[2]}
        for i in range(sizes[0] * sizes[1] * sizes[2])
    ]
    steps = rounds()
    apart = sizes[0] // 2
    while apart:
        steps.append((("stream", apart), ("stream", apart)))
        apart //= 2
    for step in steps:
        moves = []
        for place in places:
            axis, bit = step[place["stream"] % 2]
            moves.append((flat(place), flat(place | {axis: place[axis] ^ bit})))

        def swap(rows, moves=moves):
            return jnp.concatenate([rows, lax.ppermute(rows, axes, moves)], axis=0)

        yield swap


def shards(source, inflow, recovery, obs_rows, obs, observation_weight, member_order):
    planes, span, height, members = source.shape
    levels = lax.axis_size("height")
    parity = (lax.axis_index("height") % 2)[None]
    together = lax.optimization_barrier

    source, first, second = border(source, parity)
    inflow = pltpu.with_memory_space_constraint(inflow, pltpu.VMEM)
    first = lax.ppermute(first, "height", pairs(levels, 0))
    second = lax.ppermute(second, "height", pairs(levels, 1))
    end, picks, share, rates, low_rate, high_rate = march(source, inflow, recovery, obs_rows)
    end, first, second = together((end, first, second))
    term, edge, leaving = edge_march(parity, first, second, low_rate, high_rate, end)
    total = jnp.prod(recovery, axis=0)[..., None] if lax.axis_size("stream") > 2 else None
    incoming = downstream(leaving, total)
    rows = observe(obs_rows, obs, observation_weight, picks, share, incoming, edge)
    state = incoming.reshape(span * height, members)
    cuts = [planes * part // 16 for part in CUTS]
    parts = []
    for swap in exchanges():
        swapped = swap(rows)
        if len(cuts) > 1:
            state, rows = together((state, rows))
            forecast, state = forecasts(source, inflow, rates, state, term, cuts[0], cuts[1])
            swapped, state, forecast = together((swapped, state, forecast))
            parts.append(forecast)
            cuts = cuts[1:]
        rows = swapped
    while len(cuts) > 1:
        forecast, state = forecasts(source, inflow, rates, state, term, cuts[0], cuts[1])
        parts.append(forecast)
        cuts = cuts[1:]
    return updated(obs_rows.shape[0], rows, member_order, parts, source.shape)


def solution(mesh):
    placed = (
        P("stream", "span", "height", None),
        P("stream", "span", "height", None),
        P("stream", "span", "height"),
        P(("stream", "span", "height")),
        P(("stream", "span", "height")),
        P(("stream", "span", "height")),
        P(),
    )
    return jax.shard_map(
        shards,
        mesh=mesh,
        in_specs=placed,
        out_specs=P("stream", "span", "height", None),
        check_vma=False,
    )
```

```python
import functools

import jax
import jax.numpy as jnp
from jax import lax
from jax.experimental import pallas as pl
from jax.experimental.pallas import tpu as pltpu
from jax.sharding import PartitionSpec as P

vertical_mix = 0.25
MIB = 1024 * 1024
NT = (((1,), (1,)), ((), ()))
NN = (((1,), (0,)), ((), ()))
LIMIT = 24
CUTS = (0, 4, 8, 12, 16)
AXES = ("stream", "span", "height")
EXTRA = 8


def dot(a, b, dims=NN):
    return lax.dot_general(a, b, dims, preferred_element_type=jnp.float32)


def params(mib):
    return pltpu.CompilerParams(vmem_limit_bytes=mib * MIB)


def cost(elements, nbytes):
    return pl.CostEstimate(flops=1000 * elements, bytes_accessed=nbytes, transcendentals=0)


def border_kernel(parity_ref, source_ref, held_ref, first_ref, second_ref, sems):
    planes, span, height, _ = source_ref.shape
    even = parity_ref[0] == 0

    def fetch(p):
        return pltpu.make_async_copy(source_ref.at[p], held_ref.at[p], sems.at[p])

    for p in range(planes):
        fetch(p).start()
    for p in range(planes):
        fetch(p).wait()
        low = held_ref[p, :, :16].astype(jnp.float32)
        top = held_ref[p, :, height - 16 :].astype(jnp.float32)
        low = jnp.concatenate([low[a, :1] for a in range(span)], axis=0)
        top = jnp.concatenate([top[a, 15:] for a in range(span)], axis=0)
        first_ref[p] = jnp.where(even, top, low).astype(jnp.bfloat16)
        second_ref[p] = jnp.where(even, low, top).astype(jnp.bfloat16)


def border(source, parity):
    planes, span, height, members = source.shape
    vmem = pl.BlockSpec(memory_space=pltpu.VMEM)
    row = jax.ShapeDtypeStruct((planes, span, members), jnp.bfloat16)
    return pl.pallas_call(
        border_kernel,
        in_specs=[pl.BlockSpec(memory_space=pltpu.SMEM), pl.BlockSpec(memory_space=pltpu.HBM)],
        out_specs=[vmem] * 3,
        out_shape=[pltpu.VMEM(source.shape, jnp.bfloat16), row, row],
        scratch_shapes=[pltpu.SemaphoreType.DMA((planes,))],
        compiler_params=params(LIMIT),
        cost_estimate=cost(source.size, source.size),
    )(parity, pltpu.with_memory_space_constraint(source, pltpu.HBM))


def place_of(r, shape):
    _, span, height = shape
    return r // (span * height), r // height % span, r % height


def group_of(span, height):
    cells = max(1, min(span, 256 // height))
    while span % cells:
        cells -= 1
    return cells


def stencil(rows, height):
    row = lax.broadcasted_iota(jnp.int32, (rows, rows), 0)
    column = lax.broadcasted_iota(jnp.int32, (rows, rows), 1)
    apart = jnp.where(row // height == column // height, jnp.abs(row - column), 2)
    entry = jnp.where(apart == 0, 1.0 - 2.0 * vertical_mix, jnp.where(apart == 1, vertical_mix, 0.0))
    return entry.astype(jnp.bfloat16)


def upright(row):
    count = row.shape[1]
    place = lax.broadcasted_iota(jnp.int32, (count, count), 0)
    lane = lax.broadcasted_iota(jnp.int32, (count, count), 1)
    return jnp.sum(jnp.where(place == lane, row, jnp.zeros_like(row)), axis=1, keepdims=True)


def march_kernel(
    rows_ref, rows_row_ref, source_ref, recovery_ref, inflow_ref,
    end_ref, picks_ref, share_ref, rate_ref, low_rate_ref, high_rate_ref,
    deficits, tiles, through_rows, through,
):
    shape = source_ref.shape[:3]
    planes, span, height = shape
    count, members = picks_ref.shape
    cells = group_of(span, height)
    group = cells * height
    blocks = [jnp.transpose(recovery_ref[:, a, :]) for a in range(span)]
    for a in range(span):
        rate_ref[a * height : (a + 1) * height] = blocks[a]
    low_rate_ref[...] = jnp.concatenate([block[:1] for block in blocks], axis=0)
    high_rate_ref[...] = jnp.concatenate([block[height - 1 :] for block in blocks], axis=0)
    mix = stencil(group, height)
    product = None
    for p in range(planes):
        product = recovery_ref[p] if p == 0 else product * recovery_ref[p]
        through[p] = product
        for c in range(span // cells):
            part = slice(c * group, (c + 1) * group)
            term = dot(mix, source_ref[p, c * cells : (c + 1) * cells].reshape(group, members))
            if p > 0:
                term = rate_ref[part, p : p + 1] * deficits[p - 1, part] + term
            deficits[p, part] = term
    end_ref[...] = deficits[planes - 1]
    for k in range(count):
        p, a, b = place_of(rows_ref[k], shape)
        first = pl.multiple_of(b // 16 * 16, 16)
        tiles[k] = inflow_ref[p, a, pl.ds(first, 16), :].astype(jnp.float32)
        through_rows[pl.ds(k, 1), :] = through[p, pl.ds(a, 1), :]
    for k in range(count):
        p, a, b = place_of(rows_ref[k], shape)
        picks_ref[pl.ds(k, 1), :] = (
            tiles[k, pl.ds(b % 16, 1), :] - deficits[p, pl.ds(a * height + b, 1), :]
        )
    cell = upright(rows_row_ref[...].astype(jnp.float32)).astype(jnp.int32) % height
    lane = lax.broadcasted_iota(jnp.int32, (count, height), 1)
    share = jnp.sum(jnp.where(lane == cell, through_rows[...], 0.0), axis=1, keepdims=True)
    share_ref[...] = jnp.broadcast_to(share, share_ref.shape)


def march(source, inflow, recovery, obs_rows):
    planes, span, height, members = source.shape
    observed = obs_rows.shape[0]
    cells = span * height
    f32 = jnp.float32
    vmem = pl.BlockSpec(memory_space=pltpu.VMEM)
    return pl.pallas_call(
        march_kernel,
        in_specs=[pl.BlockSpec(memory_space=pltpu.SMEM)] + [vmem] * 4,
        out_specs=[vmem] * 6,
        out_shape=[
            jax.ShapeDtypeStruct((cells, members), f32),
            jax.ShapeDtypeStruct((observed, members), f32),
            jax.ShapeDtypeStruct((observed, members), f32),
            jax.ShapeDtypeStruct((cells, planes), f32),
            jax.ShapeDtypeStruct((span, planes), f32),
            jax.ShapeDtypeStruct((span, planes), f32),
        ],
        scratch_shapes=[
            pltpu.VMEM((planes, cells, members), f32),
            pltpu.VMEM((observed, 16, members), f32),
            pltpu.VMEM((observed, height), f32),
            pltpu.VMEM((planes, span, height), f32),
        ],
        compiler_params=params(LIMIT),
        cost_estimate=cost(3 * source.size, 4 * source.size),
    )(obs_rows, obs_rows[None, :], source, recovery, inflow)


def edge_kernel(
    parity_ref, first_ref, second_ref, low_rate_ref, high_rate_ref, end_ref, term_ref, edge_ref, leaving_ref
):
    planes, span, members = first_ref.shape
    height = leaving_ref.shape[1]
    even = parity_ref[0] == 0
    low, high = None, None
    for p in range(planes):
        one = vertical_mix * first_ref[p].astype(jnp.float32)
        two = vertical_mix * second_ref[p].astype(jnp.float32)
        low_term = jnp.where(even, two, one)
        high_term = jnp.where(even, one, two)
        term_ref[0, p] = low_term
        term_ref[1, p] = high_term
        low = low_term if p == 0 else low_rate_ref[:, p : p + 1] * low + low_term
        high = high_term if p == 0 else high_rate_ref[:, p : p + 1] * high + high_term
        edge_ref[0, p] = low
        edge_ref[1, p] = high
    row = lax.broadcasted_iota(jnp.int32, (height, members), 0)
    for a in range(span):
        share = jnp.where(row == 0, low[a : a + 1], jnp.where(row == height - 1, high[a : a + 1], 0.0))
        leaving_ref[a] = end_ref[a * height : (a + 1) * height] + share


def edge_march(parity, first, second, low_rate, high_rate, end):
    planes, span, members = first.shape
    vmem = pl.BlockSpec(memory_space=pltpu.VMEM)
    return pl.pallas_call(
        edge_kernel,
        in_specs=[pl.BlockSpec(memory_space=pltpu.SMEM)] + [vmem] * 5,
        out_specs=[vmem] * 3,
        out_shape=[
            jax.ShapeDtypeStruct((2, planes, span, members), jnp.float32),
            jax.ShapeDtypeStruct((2, planes, span, members), jnp.float32),
            jax.ShapeDtypeStruct((span, end.shape[0] // span, members), jnp.float32),
        ],
        compiler_params=params(LIMIT),
        cost_estimate=cost(first.size, 8 * first.size),
    )(parity, first, second, low_rate, high_rate, end)


def prepare_kernel(height, rows_ref, edge_ref, picks_ref, obs_ref, weight_ref, out_ref, obs_out_ref, weight_out_ref):
    _, planes, span, _ = edge_ref.shape
    for k in range(picks_ref.shape[0]):
        p, a, b = place_of(rows_ref[k], (planes, span, height))
        side = jnp.where(b == height - 1, 1, 0)
        at_edge = jnp.where((b == 0) | (b == height - 1), 1.0, 0.0)
        out_ref[pl.ds(k, 1), :] = picks_ref[pl.ds(k, 1), :] - at_edge * edge_ref[side, p, pl.ds(a, 1), :]
    obs_out_ref[...] = jnp.broadcast_to(upright(obs_ref[...]), obs_out_ref.shape)
    weight_out_ref[...] = jnp.broadcast_to(upright(weight_ref[...]), weight_out_ref.shape)


def prepare(obs_rows, obs, weight, picks, edge, height):
    vmem = pl.BlockSpec(memory_space=pltpu.VMEM)
    out = jax.ShapeDtypeStruct(picks.shape, jnp.float32)
    return pl.pallas_call(
        functools.partial(prepare_kernel, height),
        in_specs=[pl.BlockSpec(memory_space=pltpu.SMEM)] + [vmem] * 4,
        out_specs=[vmem] * 3,
        out_shape=[out] * 3,
        compiler_params=params(LIMIT),
        cost_estimate=cost(100 * picks.size, 64 * picks.size),
    )(obs_rows, edge, picks, obs[None, :], weight[None, :])


def observe_kernel(rows_ref, obs_ref, weight_ref, picks_ref, share_ref, incoming_ref, out_ref, arriving):
    span, height, members = incoming_ref.shape
    count = picks_ref.shape[0]
    for k in range(count):
        _, a, b = place_of(rows_ref[k], (0, span, height))
        arriving[pl.ds(k, 1), :] = incoming_ref[a, pl.ds(b, 1), :]
    forecast = picks_ref[...] - share_ref[...] * arriving[...]
    mean = jnp.sum(forecast, axis=1, keepdims=True) * (1.0 / members)
    anomaly = (forecast - mean).astype(jnp.bfloat16).astype(jnp.float32)
    weight = weight_ref[...]
    observed = weight * anomaly
    misfit = weight * (obs_ref[...] - mean)
    projection = jnp.sum(observed * misfit, axis=0, keepdims=True)
    one = projection.astype(jnp.bfloat16).astype(jnp.float32)
    two = (projection - one).astype(jnp.bfloat16).astype(jnp.float32)
    three = projection - one - two
    row = lax.broadcasted_iota(jnp.int32, (EXTRA, members), 0)
    pieces = jnp.where(row == 0, one, jnp.where(row == 1, two, jnp.where(row == 2, three, 0.0)))
    out_ref[...] = jnp.concatenate([observed, pieces], axis=0).astype(jnp.bfloat16)


def observe(obs_rows, obs, weight, picks, share, incoming):
    count, members = picks.shape
    vmem = pl.BlockSpec(memory_space=pltpu.VMEM)
    return pl.pallas_call(
        observe_kernel,
        in_specs=[pl.BlockSpec(memory_space=pltpu.SMEM)] + [vmem] * 5,
        out_specs=vmem,
        out_shape=jax.ShapeDtypeStruct((count + EXTRA, members), jnp.bfloat16),
        scratch_shapes=[pltpu.VMEM((count, members), jnp.float32)],
        compiler_params=params(LIMIT),
        cost_estimate=cost(40 * count * members, 64 * count * members),
    )(obs_rows, obs, weight, picks, share, incoming)


def forecast_kernel(start, planes, source_ref, inflow_ref, rate_ref, state_ref, term_ref, *refs):
    out_ref, end_ref = refs[:2]
    _, span, height, members = source_ref.shape
    cells = group_of(span, height)
    group = cells * height
    mix = stencil(group, height)
    row = lax.broadcasted_iota(jnp.int32, (height, members), 0)
    for p in range(start, start + planes):
        before = state_ref if p == start else end_ref
        for c in range(span // cells):
            term = dot(mix, source_ref[p, c * cells : (c + 1) * cells].reshape(group, members))
            for a in range(c * cells, (c + 1) * cells):
                part = slice(a * height, (a + 1) * height)
                low, high = term_ref[0, p, a : a + 1, :], term_ref[1, p, a : a + 1, :]
                halo = jnp.where(row == 0, low, jnp.where(row == height - 1, high, 0.0))
                deficit = rate_ref[part, p : p + 1] * before[part] + (
                    term[a * height - c * group : (a + 1) * height - c * group] + halo
                )
                end_ref[part] = deficit
                out_ref[p - start, a] = (inflow_ref[p, a].astype(jnp.float32) - deficit).astype(jnp.bfloat16)


def forecasts(source, inflow, rates, state, term, start, stop):
    planes = stop - start
    vmem = pl.BlockSpec(memory_space=pltpu.VMEM)
    size = state.size * planes
    return pl.pallas_call(
        functools.partial(forecast_kernel, start, planes),
        in_specs=[vmem] * 5,
        out_specs=[vmem, vmem],
        out_shape=[
            pltpu.VMEM((planes,) + source.shape[1:], jnp.bfloat16),
            pltpu.VMEM(state.shape, jnp.float32),
        ],
        compiler_params=params(LIMIT),
        cost_estimate=cost(4 * size, 6 * size),
    )(source, inflow, rates, state, term)


def halves(x):
    big = x.astype(jnp.bfloat16)
    return big, (x - big.astype(jnp.float32)).astype(jnp.bfloat16)


def fine_dot(a, b, dims=NN):
    a_big, a_small = halves(a)
    b_big, b_small = halves(b)
    return dot(a_big, b_big, dims) + (dot(a_big, b_small, dims) + dot(a_small, b_big, dims))


def split_rows(picked, rows):
    total, members = rows.shape
    block = picked + EXTRA
    place = lax.broadcasted_iota(jnp.int32, (total, members), 0) % block
    observed = jnp.where(place < picked, rows.astype(jnp.float32), 0.0).astype(jnp.bfloat16)
    slot = lax.broadcasted_iota(jnp.int32, (16, total), 1) % block
    return observed, dot(jnp.where(slot >= picked, 1.0, 0.0).astype(jnp.bfloat16), rows)


def gram_kernel(picked, rows_ref, order_ref, gram_ref, pieces_ref, select_ref, select_t_ref):
    members = rows_ref.shape[1]
    bf16, f32 = jnp.bfloat16, jnp.float32
    row = lax.broadcasted_iota(jnp.int32, (members, members), 0)
    column = lax.broadcasted_iota(jnp.int32, (members, members), 1)
    order = order_ref[...]
    select_ref[...] = jnp.where(order == row, 1.0, 0.0).astype(bf16)
    select_t = jnp.where(upright(order.astype(f32)) == column.astype(f32), 1.0, 0.0).astype(bf16)
    select_t_ref[...] = select_t
    observed, pieces_ref[...] = split_rows(picked, rows_ref[...])
    ordered_t = dot(select_t, observed, NT).astype(bf16)
    gram_ref[...] = dot(ordered_t, ordered_t, NT) + jnp.where(row == column, members - 1.0, 0.0)


def gram_part(picked, rows, member_order):
    total, members = rows.shape
    vmem = pl.BlockSpec(memory_space=pltpu.VMEM)
    square = (members, members)
    return pl.pallas_call(
        functools.partial(gram_kernel, picked),
        in_specs=[vmem] * 2,
        out_specs=[vmem] * 4,
        out_shape=[
            jax.ShapeDtypeStruct(square, jnp.float32),
            jax.ShapeDtypeStruct((16, members), jnp.float32),
            jax.ShapeDtypeStruct(square, jnp.bfloat16),
            jax.ShapeDtypeStruct(square, jnp.bfloat16),
        ],
        compiler_params=params(LIMIT),
        cost_estimate=cost(1000 * members * 4, 4 * total * members),
    )(rows, member_order[None, :])


def update_kernel(picked, rows_ref, gram_ref, pieces_ref, select_ref, select_t_ref, *refs):
    forecast_refs = refs[:-6]
    out_ref, gram, factor, weights_t, results, out_sem = refs[-6:]
    members = rows_ref.shape[1]
    bf16, f32 = jnp.bfloat16, jnp.float32
    row = lax.broadcasted_iota(jnp.int32, (members, members), 0)
    column = lax.broadcasted_iota(jnp.int32, (members, members), 1)
    diagonal, lower = row == column, row > column
    identity = jnp.where(diagonal, 1.0, 0.0)
    select = select_ref[...]
    observed, pieces = split_rows(picked, rows_ref[...])
    ordered_t = dot(select_t_ref[...], observed, NT).astype(bf16)
    full = gram_ref[...] + dot(ordered_t, ordered_t, NT)
    gram[...] = full
    pieces = pieces_ref[...] + pieces
    piece_one = pieces.astype(bf16)
    piece_two, piece_three = halves(pieces - piece_one.astype(f32))
    projection = dot(piece_one, select) + (dot(piece_two, select) + dot(piece_three, select))
    on_diagonal = jnp.where(diagonal, full, 0.0)
    scale_row = lax.rsqrt(jnp.sum(on_diagonal, axis=0, keepdims=True))
    scale_column = lax.rsqrt(jnp.sum(on_diagonal, axis=1, keepdims=True))
    unit = full * scale_row * scale_column

    def lower_part(residual):
        return jnp.where(lower, residual, jnp.where(diagonal, 0.5 * residual, 0.0)).astype(bf16)

    def refine(inverse, unit):
        unit_big, unit_small = halves(unit)
        inverse = inverse.astype(bf16)
        half_way = dot(inverse, unit_big) + dot(inverse, unit_small)
        big, small = halves(half_way)
        residual = dot(big, inverse, NT) + dot(small, inverse, NT) - identity
        better = inverse.astype(f32) - dot(lower_part(residual), inverse)
        return better, jnp.sum(residual * residual)

    def finish(inverse):
        inverse_big, inverse_small = halves(inverse)
        turned = dot(inverse_big, select, NT) + dot(inverse_small, select, NT)
        coefficients = fine_dot(projection, inverse, NT)
        big, small = halves(turned)
        placed = dot(select, big) + dot(select, small)
        shift = fine_dot(coefficients, turned)[:1]
        whole = (members - 1.0) ** 0.5 * placed + shift
        whole = whole + (1.0 - jnp.sum(whole, axis=1, keepdims=True)) * (1.0 / members)
        weights_t[...] = whole.astype(bf16)

    inverse = identity - jnp.where(lower, unit, 0.0)
    unit_big = unit.astype(bf16)
    for _ in range(2):
        inverse_big = inverse.astype(bf16)
        half_way = dot(inverse_big, unit_big).astype(bf16)
        residual = dot(half_way, inverse_big, NT) - identity
        inverse = inverse - dot(lower_part(residual), inverse_big)
    inverse, error = refine(inverse, unit)
    factor[...] = inverse
    finish(inverse * scale_row)

    @pl.when(jnp.logical_not(error <= 0.04))
    def _():
        def again(carried):
            step, _ = carried
            better, error = refine(factor[...], gram[...] * scale_row * scale_column)
            factor[...] = better
            return step + 1, error

        def unfinished(carried):
            step, error = carried
            return (step < 8) & (error > 0.04) & (error < 64.0)

        _, last_error = lax.while_loop(unfinished, again, (0, error))
        factor[...] = factor[...] * scale_row

        @pl.when(jnp.logical_not(last_error <= 0.04))
        def _():
            factor[...] = identity

            def eliminate(k, carry):
                held = gram[...]
                pivot_row = gram[pl.ds(k, 1), :]
                pivot = jnp.sum(jnp.where(column[:1] == k, pivot_row, 0.0), axis=1, keepdims=True)
                pivot_column = jnp.sum(jnp.where(column == k, held, 0.0), axis=1, keepdims=True)
                share = jnp.where(row[:, :1] > k, pivot_column / pivot, 0.0)
                factor[...] = factor[...] - share * factor[pl.ds(k, 1), :]
                gram[...] = held - share * pivot_row
                return carry

            lax.fori_loop(0, members, eliminate, 0)
            pivots = jnp.sum(jnp.where(diagonal, gram[...], 0.0), axis=1, keepdims=True)
            factor[...] = factor[...] * lax.rsqrt(pivots)

        finish(factor[...])

    stores = []
    for ref in forecast_refs:
        for p in range(ref.shape[0]):
            at = len(stores)
            forecast = ref[p].reshape(-1, members)
            results[at] = dot(forecast, weights_t[...], NT).astype(bf16).reshape(ref.shape[1:])
            store = pltpu.make_async_copy(results.at[at], out_ref.at[at], out_sem.at[at])
            store.start()
            stores.append(store)
    for store in stores:
        store.wait()


def updated(picked, rows, part, forecasts, shape):
    planes, span, height, members = shape
    size = planes * span * height * members
    vmem = pl.BlockSpec(memory_space=pltpu.VMEM)
    return pl.pallas_call(
        functools.partial(update_kernel, picked),
        in_specs=[vmem] * (1 + len(part) + len(forecasts)),
        out_specs=pl.BlockSpec(memory_space=pltpu.HBM),
        out_shape=jax.ShapeDtypeStruct(shape, jnp.bfloat16),
        scratch_shapes=[
            pltpu.VMEM((members, members), jnp.float32),
            pltpu.VMEM((members, members), jnp.float32),
            pltpu.VMEM((members, members), jnp.bfloat16),
            pltpu.VMEM(shape, jnp.bfloat16),
            pltpu.SemaphoreType.DMA((planes,)),
        ],
        compiler_params=params(LIMIT),
        cost_estimate=cost(4 * size, 5 * size),
    )(rows, *part, *forecasts)


def pairs(count, first):
    low = [(i, i + 1) for i in range(first, count - 1, 2)]
    return low + [(j, i) for i, j in low]


def downstream(value, rate):
    count = lax.axis_size("stream")
    steps = [(i, i + 1) for i in range(count - 1)]
    incoming = lax.ppermute(value, "stream", steps)
    for _ in range(count - 2):
        incoming = lax.ppermute(rate * incoming + value, "stream", steps)
    return incoming


def rounds():
    steps = []
    for axis in ("height", "span"):
        bits = (lax.axis_size(axis) - 1).bit_length()
        steps.append([(axis, 1 << bit) for bit in reversed(range(bits))])
    mixed = []
    while steps[0] or steps[1]:
        pair = [axis.pop(0) for axis in steps if axis]
        mixed += [(pair[0], pair[-1]), (pair[-1], pair[0])][: len(pair)]
    return mixed


def exchanges():
    sizes = [lax.axis_size(axis) for axis in AXES]
    places = [
        {"stream": i // (sizes[1] * sizes[2]), "span": i // sizes[2] % sizes[1], "height": i % sizes[2]}
        for i in range(sizes[0] * sizes[1] * sizes[2])
    ]

    def flat(place):
        return (place["stream"] * sizes[1] + place["span"]) * sizes[2] + place["height"]

    steps = rounds()
    apart = sizes[0] // 2
    while apart:
        steps.append((("stream", apart), ("stream", apart)))
        apart //= 2
    moves = []
    for step in steps:
        taken = [(place, *step[place["stream"] % 2]) for place in places]
        moves.append([(flat(at), flat(at | {axis: at[axis] ^ bit})) for at, axis, bit in taken])
    return moves


def shards(source, inflow, recovery, obs_rows, obs, observation_weight, member_order):
    planes, span, height, members = source.shape
    levels = lax.axis_size("height")
    parity = (lax.axis_index("height") % 2)[None]
    together = lax.optimization_barrier

    source, first, second = border(source, parity)
    inflow, first = together((inflow, first))
    inflow = pltpu.with_memory_space_constraint(inflow, pltpu.VMEM)
    first = lax.ppermute(first, "height", pairs(levels, 0))
    second = lax.ppermute(second, "height", pairs(levels, 1))
    end, picks, share, rates, low_rate, high_rate = march(source, inflow, recovery, obs_rows)
    end, first, second = together((end, first, second))
    term, edge, leaving = edge_march(parity, first, second, low_rate, high_rate, end)
    total = jnp.prod(recovery, axis=0)[..., None] if lax.axis_size("stream") > 2 else None
    incoming = downstream(leaving, total)
    picks, obs, weight = prepare(obs_rows, obs, observation_weight, picks, edge, height)
    rows = observe(obs_rows, obs, weight, picks, share, incoming)
    state = incoming.reshape(span * height, members)
    cuts = [planes * part // 16 for part in CUTS]
    parts = []
    *moves, last_moves = exchanges()
    for pairing in moves:
        other = lax.ppermute(rows, AXES, pairing)
        if len(cuts) > 1:
            state, rows = together((state, rows))
            forecast, state = forecasts(source, inflow, rates, state, term, cuts[0], cuts[1])
            other, state, forecast = together((other, state, forecast))
            parts.append(forecast)
            cuts = cuts[1:]
        rows = jnp.concatenate([rows, other], axis=0)
    while len(cuts) > 1:
        forecast, state = forecasts(source, inflow, rates, state, term, cuts[0], cuts[1])
        parts.append(forecast)
        cuts = cuts[1:]
    other = lax.ppermute(rows, AXES, last_moves)
    part = gram_part(obs_rows.shape[0], rows, member_order)
    return updated(obs_rows.shape[0], other, part, parts, source.shape)


def solution(mesh):
    placed = (
        P("stream", "span", "height", None),
        P("stream", "span", "height", None),
        P("stream", "span", "height"),
        P(("stream", "span", "height")),
        P(("stream", "span", "height")),
        P(("stream", "span", "height")),
        P(),
    )
    return jax.shard_map(
        shards,
        mesh=mesh,
        in_specs=placed,
        out_specs=P("stream", "span", "height", None),
        check_vma=False,
    )
```

```python
import functools

import jax
import jax.numpy as jnp
from jax import lax
from jax.experimental import pallas as pl
from jax.experimental.pallas import tpu as pltpu
from jax.sharding import PartitionSpec as P

vertical_mix = 0.25
MIB = 1024 * 1024
NT = (((1,), (1,)), ((), ()))
NN = (((1,), (0,)), ((), ()))
LIMIT = 24
CUTS = (0, 4, 8, 12, 16)
AXES = ("stream", "span", "height")
EXTRA = 8


def dot(a, b, dims=NN):
    return lax.dot_general(a, b, dims, preferred_element_type=jnp.float32)


def params(mib):
    return pltpu.CompilerParams(vmem_limit_bytes=mib * MIB)


def cost(elements, nbytes):
    return pl.CostEstimate(flops=1000 * elements, bytes_accessed=nbytes, transcendentals=0)


def border_kernel(parity_ref, source_ref, held_ref, first_ref, second_ref, sems):
    planes, span, height, _ = source_ref.shape
    even = parity_ref[0] == 0

    def fetch(p):
        return pltpu.make_async_copy(source_ref.at[p], held_ref.at[p], sems.at[p])

    for p in range(planes):
        fetch(p).start()
    for p in range(planes):
        fetch(p).wait()
        low = held_ref[p, :, :16].astype(jnp.float32)
        top = held_ref[p, :, height - 16 :].astype(jnp.float32)
        low = jnp.concatenate([low[a, :1] for a in range(span)], axis=0)
        top = jnp.concatenate([top[a, 15:] for a in range(span)], axis=0)
        first_ref[p] = jnp.where(even, top, low).astype(jnp.bfloat16)
        second_ref[p] = jnp.where(even, low, top).astype(jnp.bfloat16)


def border(source, parity):
    planes, span, height, members = source.shape
    vmem = pl.BlockSpec(memory_space=pltpu.VMEM)
    row = jax.ShapeDtypeStruct((planes, span, members), jnp.bfloat16)
    return pl.pallas_call(
        border_kernel,
        in_specs=[pl.BlockSpec(memory_space=pltpu.SMEM), pl.BlockSpec(memory_space=pltpu.HBM)],
        out_specs=[vmem] * 3,
        out_shape=[pltpu.VMEM(source.shape, jnp.bfloat16), row, row],
        scratch_shapes=[pltpu.SemaphoreType.DMA((planes,))],
        compiler_params=params(LIMIT),
        cost_estimate=cost(source.size, source.size),
    )(parity, pltpu.with_memory_space_constraint(source, pltpu.HBM))


def place_of(r, shape):
    _, span, height = shape
    return r // (span * height), r // height % span, r % height


def group_of(span, height):
    cells = max(1, min(span, 256 // height))
    while span % cells:
        cells -= 1
    return cells


def stencil(rows, height):
    row = lax.broadcasted_iota(jnp.int32, (rows, rows), 0)
    column = lax.broadcasted_iota(jnp.int32, (rows, rows), 1)
    apart = jnp.where(row // height == column // height, jnp.abs(row - column), 2)
    entry = jnp.where(apart == 0, 1.0 - 2.0 * vertical_mix, jnp.where(apart == 1, vertical_mix, 0.0))
    return entry.astype(jnp.bfloat16)


def upright(row):
    count = row.shape[1]
    place = lax.broadcasted_iota(jnp.int32, (count, count), 0)
    lane = lax.broadcasted_iota(jnp.int32, (count, count), 1)
    return jnp.sum(jnp.where(place == lane, row, jnp.zeros_like(row)), axis=1, keepdims=True)


def march_kernel(
    rows_ref, rows_row_ref, source_ref, recovery_ref, inflow_ref,
    end_ref, picks_ref, share_ref, rate_ref, low_rate_ref, high_rate_ref,
    deficits, tiles, through_rows, through,
):
    shape = source_ref.shape[:3]
    planes, span, height = shape
    count, members = picks_ref.shape
    cells = group_of(span, height)
    group = cells * height
    blocks = [jnp.transpose(recovery_ref[:, a, :]) for a in range(span)]
    for a in range(span):
        rate_ref[a * height : (a + 1) * height] = blocks[a]
    low_rate_ref[...] = jnp.concatenate([block[:1] for block in blocks], axis=0)
    high_rate_ref[...] = jnp.concatenate([block[height - 1 :] for block in blocks], axis=0)
    mix = stencil(group, height)
    product = None
    for p in range(planes):
        product = recovery_ref[p] if p == 0 else product * recovery_ref[p]
        through[p] = product
        for c in range(span // cells):
            part = slice(c * group, (c + 1) * group)
            term = dot(mix, source_ref[p, c * cells : (c + 1) * cells].reshape(group, members))
            if p > 0:
                term = rate_ref[part, p : p + 1] * deficits[p - 1, part] + term
            deficits[p, part] = term
    end_ref[...] = deficits[planes - 1]
    for k in range(count):
        p, a, b = place_of(rows_ref[k], shape)
        first = pl.multiple_of(b // 16 * 16, 16)
        tiles[k] = inflow_ref[p, a, pl.ds(first, 16), :].astype(jnp.float32)
        through_rows[pl.ds(k, 1), :] = through[p, pl.ds(a, 1), :]
    for k in range(count):
        p, a, b = place_of(rows_ref[k], shape)
        picks_ref[pl.ds(k, 1), :] = (
            tiles[k, pl.ds(b % 16, 1), :] - deficits[p, pl.ds(a * height + b, 1), :]
        )
    cell = upright(rows_row_ref[...].astype(jnp.float32)).astype(jnp.int32) % height
    lane = lax.broadcasted_iota(jnp.int32, (count, height), 1)
    share = jnp.sum(jnp.where(lane == cell, through_rows[...], 0.0), axis=1, keepdims=True)
    share_ref[...] = jnp.broadcast_to(share, share_ref.shape)


def march(source, inflow, recovery, obs_rows):
    planes, span, height, members = source.shape
    observed = obs_rows.shape[0]
    cells = span * height
    f32 = jnp.float32
    vmem = pl.BlockSpec(memory_space=pltpu.VMEM)
    return pl.pallas_call(
        march_kernel,
        in_specs=[pl.BlockSpec(memory_space=pltpu.SMEM)] + [vmem] * 4,
        out_specs=[vmem] * 6,
        out_shape=[
            jax.ShapeDtypeStruct((cells, members), f32),
            jax.ShapeDtypeStruct((observed, members), f32),
            jax.ShapeDtypeStruct((observed, members), f32),
            jax.ShapeDtypeStruct((cells, planes), f32),
            jax.ShapeDtypeStruct((span, planes), f32),
            jax.ShapeDtypeStruct((span, planes), f32),
        ],
        scratch_shapes=[
            pltpu.VMEM((planes, cells, members), f32),
            pltpu.VMEM((observed, 16, members), f32),
            pltpu.VMEM((observed, height), f32),
            pltpu.VMEM((planes, span, height), f32),
        ],
        compiler_params=params(LIMIT),
        cost_estimate=cost(3 * source.size, 4 * source.size),
    )(obs_rows, obs_rows[None, :], source, recovery, inflow)


def edge_kernel(
    parity_ref, first_ref, second_ref, low_rate_ref, high_rate_ref, end_ref, term_ref, edge_ref, leaving_ref
):
    planes, span, members = first_ref.shape
    height = leaving_ref.shape[1]
    even = parity_ref[0] == 0
    low, high = None, None
    for p in range(planes):
        one = vertical_mix * first_ref[p].astype(jnp.float32)
        two = vertical_mix * second_ref[p].astype(jnp.float32)
        low_term = jnp.where(even, two, one)
        high_term = jnp.where(even, one, two)
        term_ref[0, p] = low_term
        term_ref[1, p] = high_term
        low = low_term if p == 0 else low_rate_ref[:, p : p + 1] * low + low_term
        high = high_term if p == 0 else high_rate_ref[:, p : p + 1] * high + high_term
        edge_ref[0, p] = low
        edge_ref[1, p] = high
    row = lax.broadcasted_iota(jnp.int32, (height, members), 0)
    for a in range(span):
        share = jnp.where(row == 0, low[a : a + 1], jnp.where(row == height - 1, high[a : a + 1], 0.0))
        leaving_ref[a] = end_ref[a * height : (a + 1) * height] + share


def edge_march(parity, first, second, low_rate, high_rate, end):
    planes, span, members = first.shape
    vmem = pl.BlockSpec(memory_space=pltpu.VMEM)
    return pl.pallas_call(
        edge_kernel,
        in_specs=[pl.BlockSpec(memory_space=pltpu.SMEM)] + [vmem] * 5,
        out_specs=[vmem] * 3,
        out_shape=[
            jax.ShapeDtypeStruct((2, planes, span, members), jnp.float32),
            jax.ShapeDtypeStruct((2, planes, span, members), jnp.float32),
            jax.ShapeDtypeStruct((span, end.shape[0] // span, members), jnp.float32),
        ],
        compiler_params=params(LIMIT),
        cost_estimate=cost(first.size, 8 * first.size),
    )(parity, first, second, low_rate, high_rate, end)


def prepare_kernel(height, rows_ref, edge_ref, picks_ref, obs_ref, weight_ref, out_ref, obs_out_ref, weight_out_ref):
    _, planes, span, _ = edge_ref.shape
    for k in range(picks_ref.shape[0]):
        p, a, b = place_of(rows_ref[k], (planes, span, height))
        side = jnp.where(b == height - 1, 1, 0)
        at_edge = jnp.where((b == 0) | (b == height - 1), 1.0, 0.0)
        out_ref[pl.ds(k, 1), :] = picks_ref[pl.ds(k, 1), :] - at_edge * edge_ref[side, p, pl.ds(a, 1), :]
    obs_out_ref[...] = jnp.broadcast_to(upright(obs_ref[...]), obs_out_ref.shape)
    weight_out_ref[...] = jnp.broadcast_to(upright(weight_ref[...]), weight_out_ref.shape)


def prepare(obs_rows, obs, weight, picks, edge, height):
    vmem = pl.BlockSpec(memory_space=pltpu.VMEM)
    out = jax.ShapeDtypeStruct(picks.shape, jnp.float32)
    return pl.pallas_call(
        functools.partial(prepare_kernel, height),
        in_specs=[pl.BlockSpec(memory_space=pltpu.SMEM)] + [vmem] * 4,
        out_specs=[vmem] * 3,
        out_shape=[out] * 3,
        compiler_params=params(LIMIT),
        cost_estimate=cost(100 * picks.size, 64 * picks.size),
    )(obs_rows, edge, picks, obs[None, :], weight[None, :])


def observe_kernel(rows_ref, obs_ref, weight_ref, picks_ref, share_ref, incoming_ref, out_ref, arriving):
    span, height, members = incoming_ref.shape
    count = picks_ref.shape[0]
    for k in range(count):
        _, a, b = place_of(rows_ref[k], (0, span, height))
        arriving[pl.ds(k, 1), :] = incoming_ref[a, pl.ds(b, 1), :]
    forecast = picks_ref[...] - share_ref[...] * arriving[...]
    mean = jnp.sum(forecast, axis=1, keepdims=True) * (1.0 / members)
    anomaly = (forecast - mean).astype(jnp.bfloat16).astype(jnp.float32)
    weight = weight_ref[...]
    observed = weight * anomaly
    misfit = weight * (obs_ref[...] - mean)
    projection = jnp.sum(observed * misfit, axis=0, keepdims=True)
    one = projection.astype(jnp.bfloat16).astype(jnp.float32)
    two = (projection - one).astype(jnp.bfloat16).astype(jnp.float32)
    three = projection - one - two
    row = lax.broadcasted_iota(jnp.int32, (EXTRA, members), 0)
    pieces = jnp.where(row == 0, one, jnp.where(row == 1, two, jnp.where(row == 2, three, 0.0)))
    out_ref[...] = jnp.concatenate([observed, pieces], axis=0).astype(jnp.bfloat16)


def observe(obs_rows, obs, weight, picks, share, incoming):
    count, members = picks.shape
    vmem = pl.BlockSpec(memory_space=pltpu.VMEM)
    return pl.pallas_call(
        observe_kernel,
        in_specs=[pl.BlockSpec(memory_space=pltpu.SMEM)] + [vmem] * 5,
        out_specs=vmem,
        out_shape=jax.ShapeDtypeStruct((count + EXTRA, members), jnp.bfloat16),
        scratch_shapes=[pltpu.VMEM((count, members), jnp.float32)],
        compiler_params=params(LIMIT),
        cost_estimate=cost(40 * count * members, 64 * count * members),
    )(obs_rows, obs, weight, picks, share, incoming)


def anomaly_kernel(start, planes, source_ref, inflow_ref, rate_ref, state_ref, term_ref, *refs):
    out_ref, mean_ref, end_ref = refs
    _, span, height, members = source_ref.shape
    wide = mean_ref.shape[2]
    cells = group_of(span, height)
    group = cells * height
    mix = stencil(group, height)
    row = lax.broadcasted_iota(jnp.int32, (height, members), 0)
    for p in range(start, start + planes):
        before = state_ref if p == start else end_ref
        for c in range(span // cells):
            term = dot(mix, source_ref[p, c * cells : (c + 1) * cells].reshape(group, members))
            some = slice(c * cells, (c + 1) * cells)
            part = slice(c * group, (c + 1) * group)
            halo = []
            for a in range(c * cells, (c + 1) * cells):
                low, high = term_ref[0, p, a : a + 1, :], term_ref[1, p, a : a + 1, :]
                halo.append(jnp.where(row == 0, low, jnp.where(row == height - 1, high, 0.0)))
            deficit = rate_ref[part, p : p + 1] * before[part] + (term + jnp.concatenate(halo, axis=0))
            end_ref[part] = deficit
            forecast = inflow_ref[p, some].astype(jnp.float32).reshape(group, members) - deficit
            mean = jnp.sum(forecast, axis=1, keepdims=True) * (1.0 / members)
            anomaly = (forecast - mean).astype(jnp.bfloat16)
            out_ref[p - start, some] = anomaly.reshape(cells, height, members)
            mean_ref[p - start, part] = jnp.broadcast_to(mean, (group, wide))


def anomalies(source, inflow, rates, state, term, start, stop):
    planes = stop - start
    vmem = pl.BlockSpec(memory_space=pltpu.VMEM)
    size = state.size * planes
    return pl.pallas_call(
        functools.partial(anomaly_kernel, start, planes),
        in_specs=[vmem] * 5,
        out_specs=[vmem] * 3,
        out_shape=[
            pltpu.VMEM((planes,) + source.shape[1:], jnp.bfloat16),
            pltpu.VMEM((planes, state.shape[0], min(128, state.shape[1])), jnp.float32),
            pltpu.VMEM(state.shape, jnp.float32),
        ],
        compiler_params=params(LIMIT),
        cost_estimate=cost(4 * size, 6 * size),
    )(source, inflow, rates, state, term)


def halves(x):
    big = x.astype(jnp.bfloat16)
    return big, (x - big.astype(jnp.float32)).astype(jnp.bfloat16)


def fine_dot(a, b, dims=NN):
    a_big, a_small = halves(a)
    b_big, b_small = halves(b)
    return dot(a_big, b_big, dims) + (dot(a_big, b_small, dims) + dot(a_small, b_big, dims))


def split_rows(picked, rows):
    total, members = rows.shape
    block = picked + EXTRA
    place = lax.broadcasted_iota(jnp.int32, (total, members), 0) % block
    observed = jnp.where(place < picked, rows.astype(jnp.float32), 0.0).astype(jnp.bfloat16)
    slot = lax.broadcasted_iota(jnp.int32, (16, total), 1) % block
    return observed, dot(jnp.where(slot >= picked, 1.0, 0.0).astype(jnp.bfloat16), rows)


def gram_kernel(picked, rows_ref, order_ref, gram_ref, pieces_ref, select_ref, select_t_ref):
    members = rows_ref.shape[1]
    bf16, f32 = jnp.bfloat16, jnp.float32
    row = lax.broadcasted_iota(jnp.int32, (members, members), 0)
    column = lax.broadcasted_iota(jnp.int32, (members, members), 1)
    order = order_ref[...]
    select_ref[...] = jnp.where(order == row, 1.0, 0.0).astype(bf16)
    select_t = jnp.where(upright(order.astype(f32)) == column.astype(f32), 1.0, 0.0).astype(bf16)
    select_t_ref[...] = select_t
    observed, pieces_ref[...] = split_rows(picked, rows_ref[...])
    ordered_t = dot(select_t, observed, NT).astype(bf16)
    gram_ref[...] = dot(ordered_t, ordered_t, NT) + jnp.where(row == column, members - 1.0, 0.0)


def gram_part(picked, rows, member_order):
    total, members = rows.shape
    vmem = pl.BlockSpec(memory_space=pltpu.VMEM)
    square = (members, members)
    return pl.pallas_call(
        functools.partial(gram_kernel, picked),
        in_specs=[vmem] * 2,
        out_specs=[vmem] * 4,
        out_shape=[
            jax.ShapeDtypeStruct(square, jnp.float32),
            jax.ShapeDtypeStruct((16, members), jnp.float32),
            jax.ShapeDtypeStruct(square, jnp.bfloat16),
            jax.ShapeDtypeStruct(square, jnp.bfloat16),
        ],
        compiler_params=params(LIMIT),
        cost_estimate=cost(1000 * members * 4, 4 * total * members),
    )(rows, member_order[None, :])


def update_kernel(picked, rows_ref, gram_ref, pieces_ref, select_ref, select_t_ref, *refs):
    part_refs = refs[:-6]
    out_ref, gram, factor, weights_t, results, out_sem = refs[-6:]
    members = rows_ref.shape[1]
    bf16, f32 = jnp.bfloat16, jnp.float32
    row = lax.broadcasted_iota(jnp.int32, (members, members), 0)
    column = lax.broadcasted_iota(jnp.int32, (members, members), 1)
    diagonal, lower = row == column, row > column
    identity = jnp.where(diagonal, 1.0, 0.0)
    select = select_ref[...]
    observed, pieces = split_rows(picked, rows_ref[...])
    ordered_t = dot(select_t_ref[...], observed, NT).astype(bf16)
    full = gram_ref[...] + dot(ordered_t, ordered_t, NT)
    gram[...] = full
    pieces = pieces_ref[...] + pieces
    piece_one = pieces.astype(bf16)
    piece_two, piece_three = halves(pieces - piece_one.astype(f32))
    projection = dot(piece_one, select) + (dot(piece_two, select) + dot(piece_three, select))
    on_diagonal = jnp.where(diagonal, full, 0.0)
    scale_row = lax.rsqrt(jnp.sum(on_diagonal, axis=0, keepdims=True))
    scale_column = lax.rsqrt(jnp.sum(on_diagonal, axis=1, keepdims=True))
    unit = full * scale_row * scale_column

    def lower_part(residual):
        return jnp.where(lower, residual, jnp.where(diagonal, 0.5 * residual, 0.0)).astype(bf16)

    def refine(inverse, unit):
        unit_big, unit_small = halves(unit)
        inverse = inverse.astype(bf16)
        half_way = dot(inverse, unit_big) + dot(inverse, unit_small)
        big, small = halves(half_way)
        residual = dot(big, inverse, NT) + dot(small, inverse, NT) - identity
        better = inverse.astype(f32) - dot(lower_part(residual), inverse)
        return better, jnp.sum(residual * residual)

    def finish(inverse):
        inverse_big, inverse_small = halves(inverse)
        turned = dot(inverse_big, select, NT) + dot(inverse_small, select, NT)
        coefficients = fine_dot(projection, inverse, NT)
        big, small = halves(turned)
        placed = dot(select, big) + dot(select, small)
        shift = fine_dot(coefficients, turned)[:1]
        weights_t[...] = ((members - 1.0) ** 0.5 * placed + shift).astype(bf16)

    inverse = identity - jnp.where(lower, unit, 0.0)
    unit_big = unit.astype(bf16)
    for _ in range(2):
        inverse_big = inverse.astype(bf16)
        half_way = dot(inverse_big, unit_big).astype(bf16)
        residual = dot(half_way, inverse_big, NT) - identity
        inverse = inverse - dot(lower_part(residual), inverse_big)
    inverse, error = refine(inverse, unit)
    factor[...] = inverse
    finish(inverse * scale_row)

    @pl.when(jnp.logical_not(error <= 0.04))
    def _():
        def again(carried):
            step, _ = carried
            better, error = refine(factor[...], gram[...] * scale_row * scale_column)
            factor[...] = better
            return step + 1, error

        def unfinished(carried):
            step, error = carried
            return (step < 8) & (error > 0.04) & (error < 64.0)

        _, last_error = lax.while_loop(unfinished, again, (0, error))
        factor[...] = factor[...] * scale_row

        @pl.when(jnp.logical_not(last_error <= 0.04))
        def _():
            factor[...] = identity

            def eliminate(k, carry):
                held = gram[...]
                pivot_row = gram[pl.ds(k, 1), :]
                pivot = jnp.sum(jnp.where(column[:1] == k, pivot_row, 0.0), axis=1, keepdims=True)
                pivot_column = jnp.sum(jnp.where(column == k, held, 0.0), axis=1, keepdims=True)
                share = jnp.where(row[:, :1] > k, pivot_column / pivot, 0.0)
                factor[...] = factor[...] - share * factor[pl.ds(k, 1), :]
                gram[...] = held - share * pivot_row
                return carry

            lax.fori_loop(0, members, eliminate, 0)
            pivots = jnp.sum(jnp.where(diagonal, gram[...], 0.0), axis=1, keepdims=True)
            factor[...] = factor[...] * lax.rsqrt(pivots)

        finish(factor[...])

    stores = []
    for ref, mean_ref in zip(part_refs[::2], part_refs[1::2]):
        for p in range(ref.shape[0]):
            at = len(stores)
            mean = jnp.concatenate([mean_ref[p]] * (members // mean_ref.shape[2]), axis=1)
            analysis = mean + dot(ref[p].reshape(-1, members), weights_t[...], NT)
            results[at] = analysis.astype(bf16).reshape(ref.shape[1:])
            store = pltpu.make_async_copy(results.at[at], out_ref.at[at], out_sem.at[at])
            store.start()
            stores.append(store)
    for store in stores:
        store.wait()


def updated(picked, rows, part, parts, shape):
    planes, span, height, members = shape
    size = planes * span * height * members
    vmem = pl.BlockSpec(memory_space=pltpu.VMEM)
    return pl.pallas_call(
        functools.partial(update_kernel, picked),
        in_specs=[vmem] * (1 + len(part) + len(parts)),
        out_specs=pl.BlockSpec(memory_space=pltpu.HBM),
        out_shape=jax.ShapeDtypeStruct(shape, jnp.bfloat16),
        scratch_shapes=[
            pltpu.VMEM((members, members), jnp.float32),
            pltpu.VMEM((members, members), jnp.float32),
            pltpu.VMEM((members, members), jnp.bfloat16),
            pltpu.VMEM(shape, jnp.bfloat16),
            pltpu.SemaphoreType.DMA((planes,)),
        ],
        compiler_params=params(LIMIT),
        cost_estimate=cost(4 * size, 5 * size),
    )(rows, *part, *parts)


def pairs(count, first):
    low = [(i, i + 1) for i in range(first, count - 1, 2)]
    return low + [(j, i) for i, j in low]


def downstream(value, rate):
    count = lax.axis_size("stream")
    steps = [(i, i + 1) for i in range(count - 1)]
    incoming = lax.ppermute(value, "stream", steps)
    for _ in range(count - 2):
        incoming = lax.ppermute(rate * incoming + value, "stream", steps)
    return incoming


def rounds():
    steps = []
    for axis in ("height", "span"):
        bits = (lax.axis_size(axis) - 1).bit_length()
        steps.append([(axis, 1 << bit) for bit in reversed(range(bits))])
    mixed = []
    while steps[0] or steps[1]:
        pair = [axis.pop(0) for axis in steps if axis]
        mixed += [(pair[0], pair[-1]), (pair[-1], pair[0])][: len(pair)]
    return mixed


def exchanges():
    sizes = [lax.axis_size(axis) for axis in AXES]
    places = [
        {"stream": i // (sizes[1] * sizes[2]), "span": i // sizes[2] % sizes[1], "height": i % sizes[2]}
        for i in range(sizes[0] * sizes[1] * sizes[2])
    ]

    def flat(place):
        return (place["stream"] * sizes[1] + place["span"]) * sizes[2] + place["height"]

    steps = rounds()
    apart = sizes[0] // 2
    while apart:
        steps.append((("stream", apart), ("stream", apart)))
        apart //= 2
    moves = []
    for step in steps:
        taken = [(place, *step[place["stream"] % 2]) for place in places]
        moves.append([(flat(at), flat(at | {axis: at[axis] ^ bit})) for at, axis, bit in taken])
    return moves


def shards(source, inflow, recovery, obs_rows, obs, observation_weight, member_order):
    planes, span, height, members = source.shape
    levels = lax.axis_size("height")
    parity = (lax.axis_index("height") % 2)[None]
    together = lax.optimization_barrier

    source, first, second = border(source, parity)
    inflow, first = together((inflow, first))
    inflow = pltpu.with_memory_space_constraint(inflow, pltpu.VMEM)
    first = lax.ppermute(first, "height", pairs(levels, 0))
    second = lax.ppermute(second, "height", pairs(levels, 1))
    end, picks, share, rates, low_rate, high_rate = march(source, inflow, recovery, obs_rows)
    end, first, second = together((end, first, second))
    term, edge, leaving = edge_march(parity, first, second, low_rate, high_rate, end)
    total = jnp.prod(recovery, axis=0)[..., None] if lax.axis_size("stream") > 2 else None
    incoming = downstream(leaving, total)
    picks, obs, weight = prepare(obs_rows, obs, observation_weight, picks, edge, height)
    rows = observe(obs_rows, obs, weight, picks, share, incoming)
    state = incoming.reshape(span * height, members)
    cuts = [planes * part // 16 for part in CUTS]
    parts = []
    *moves, last_moves = exchanges()
    for pairing in moves:
        other = lax.ppermute(rows, AXES, pairing)
        if len(cuts) > 1:
            state, rows = together((state, rows))
            anomaly, mean, state = anomalies(source, inflow, rates, state, term, cuts[0], cuts[1])
            other, state, anomaly, mean = together((other, state, anomaly, mean))
            parts += [anomaly, mean]
            cuts = cuts[1:]
        rows = jnp.concatenate([rows, other], axis=0)
    while len(cuts) > 1:
        anomaly, mean, state = anomalies(source, inflow, rates, state, term, cuts[0], cuts[1])
        parts += [anomaly, mean]
        cuts = cuts[1:]
    other = lax.ppermute(rows, AXES, last_moves)
    part = gram_part(obs_rows.shape[0], rows, member_order)
    return updated(obs_rows.shape[0], other, part, parts, source.shape)


def solution(mesh):
    placed = (
        P("stream", "span", "height", None),
        P("stream", "span", "height", None),
        P("stream", "span", "height"),
        P(("stream", "span", "height")),
        P(("stream", "span", "height")),
        P(("stream", "span", "height")),
        P(),
    )
    return jax.shard_map(
        shards,
        mesh=mesh,
        in_specs=placed,
        out_specs=P("stream", "span", "height", None),
        check_vma=False,
    )
```

```python
import functools

import jax
import jax.numpy as jnp
from jax import lax
from jax.experimental import pallas as pl
from jax.experimental.pallas import tpu as pltpu
from jax.sharding import PartitionSpec as P

vertical_mix = 0.25
MIB = 1024 * 1024
NT = (((1,), (1,)), ((), ()))
NN = (((1,), (0,)), ((), ()))
LIMIT = 24
CUTS = (0, 4, 8, 12, 16)
AXES = ("stream", "span", "height")
EXTRA = 8


def dot(a, b, dims=NN):
    return lax.dot_general(a, b, dims, preferred_element_type=jnp.float32)


def params(mib):
    return pltpu.CompilerParams(vmem_limit_bytes=mib * MIB)


def cost(elements, nbytes):
    return pl.CostEstimate(flops=1000 * elements, bytes_accessed=nbytes, transcendentals=0)


def border_kernel(place_ref, source_ref, held_ref, first_ref, second_ref, sems):
    planes, span, height, _ = source_ref.shape
    even = lax.bitwise_and(place_ref[0], 1) == 0

    def fetch(p):
        return pltpu.make_async_copy(source_ref.at[p], held_ref.at[p], sems.at[p])

    for p in range(planes):
        fetch(p).start()
    for p in range(planes):
        fetch(p).wait()
        low = held_ref[p, :, :16].astype(jnp.float32)
        top = held_ref[p, :, height - 16 :].astype(jnp.float32)
        low = jnp.concatenate([low[a, :1] for a in range(span)], axis=0)
        top = jnp.concatenate([top[a, 15:] for a in range(span)], axis=0)
        first_ref[p] = jnp.where(even, top, low).astype(jnp.bfloat16)
        second_ref[p] = jnp.where(even, low, top).astype(jnp.bfloat16)


def border(source, place):
    planes, span, height, members = source.shape
    vmem = pl.BlockSpec(memory_space=pltpu.VMEM)
    row = jax.ShapeDtypeStruct((planes, span, members), jnp.bfloat16)
    return pl.pallas_call(
        border_kernel,
        in_specs=[pl.BlockSpec(memory_space=pltpu.SMEM), pl.BlockSpec(memory_space=pltpu.HBM)],
        out_specs=[vmem] * 3,
        out_shape=[pltpu.VMEM(source.shape, jnp.bfloat16), row, row],
        scratch_shapes=[pltpu.SemaphoreType.DMA((planes,))],
        compiler_params=params(LIMIT),
        cost_estimate=cost(source.size, source.size),
    )(place, pltpu.with_memory_space_constraint(source, pltpu.HBM))


def parted(value, size):
    if size & (size - 1):
        return lax.div(value, size), lax.rem(value, size)
    return lax.shift_right_logical(value, size.bit_length() - 1), lax.bitwise_and(value, size - 1)


def place_of(r, shape):
    _, span, height = shape
    rest, b = parted(r, height)
    p, a = parted(rest, span)
    return p, a, b


def group_of(span, height):
    cells = max(1, min(span, 256 // height))
    while span % cells:
        cells -= 1
    return cells


def stencil(rows, height):
    row = lax.broadcasted_iota(jnp.int32, (rows, rows), 0)
    column = lax.broadcasted_iota(jnp.int32, (rows, rows), 1)
    apart = jnp.where(row // height == column // height, jnp.abs(row - column), 2)
    entry = jnp.where(apart == 0, 1.0 - 2.0 * vertical_mix, jnp.where(apart == 1, vertical_mix, 0.0))
    return entry.astype(jnp.bfloat16)


def upright(row):
    count = row.shape[1]
    place = lax.broadcasted_iota(jnp.int32, (count, count), 0)
    lane = lax.broadcasted_iota(jnp.int32, (count, count), 1)
    return jnp.sum(jnp.where(place == lane, row, jnp.zeros_like(row)), axis=1, keepdims=True)


def march_kernel(
    rows_ref, rows_row_ref, source_ref, recovery_ref, inflow_ref,
    end_ref, picks_ref, share_ref, rate_ref, low_rate_ref, high_rate_ref,
    deficits, tiles, through_rows, through,
):
    shape = source_ref.shape[:3]
    planes, span, height = shape
    count, members = picks_ref.shape
    cells = group_of(span, height)
    group = cells * height
    blocks = [jnp.transpose(recovery_ref[:, a, :]) for a in range(span)]
    for a in range(span):
        rate_ref[a * height : (a + 1) * height] = blocks[a]
    low_rate_ref[...] = jnp.concatenate([block[:1] for block in blocks], axis=0)
    high_rate_ref[...] = jnp.concatenate([block[height - 1 :] for block in blocks], axis=0)
    mix = stencil(group, height)
    product = None
    for p in range(planes):
        product = recovery_ref[p] if p == 0 else product * recovery_ref[p]
        through[p] = product
        for c in range(span // cells):
            part = slice(c * group, (c + 1) * group)
            term = dot(mix, source_ref[p, c * cells : (c + 1) * cells].reshape(group, members))
            if p > 0:
                term = rate_ref[part, p : p + 1] * deficits[p - 1, part] + term
            deficits[p, part] = term
    end_ref[...] = deficits[planes - 1]
    for k in range(count):
        p, a, b = place_of(rows_ref[k], shape)
        first = pl.multiple_of(b - lax.bitwise_and(b, 15), 16)
        tiles[k] = inflow_ref[p, a, pl.ds(first, 16), :].astype(jnp.float32)
        through_rows[pl.ds(k, 1), :] = through[p, pl.ds(a, 1), :]
    for k in range(count):
        p, a, b = place_of(rows_ref[k], shape)
        picks_ref[pl.ds(k, 1), :] = (
            tiles[k, pl.ds(lax.bitwise_and(b, 15), 1), :] - deficits[p, pl.ds(a * height + b, 1), :]
        )
    cell = upright(rows_row_ref[...].astype(jnp.float32)).astype(jnp.int32) % height
    lane = lax.broadcasted_iota(jnp.int32, (count, height), 1)
    share = jnp.sum(jnp.where(lane == cell, through_rows[...], 0.0), axis=1, keepdims=True)
    share_ref[...] = jnp.broadcast_to(share, share_ref.shape)


def march(source, inflow, recovery, obs_rows):
    planes, span, height, members = source.shape
    observed = obs_rows.shape[0]
    cells = span * height
    f32 = jnp.float32
    vmem = pl.BlockSpec(memory_space=pltpu.VMEM)
    return pl.pallas_call(
        march_kernel,
        in_specs=[pl.BlockSpec(memory_space=pltpu.SMEM)] + [vmem] * 4,
        out_specs=[vmem] * 6,
        out_shape=[
            jax.ShapeDtypeStruct((cells, members), f32),
            jax.ShapeDtypeStruct((observed, members), f32),
            jax.ShapeDtypeStruct((observed, members), f32),
            jax.ShapeDtypeStruct((cells, planes), f32),
            jax.ShapeDtypeStruct((span, planes), f32),
            jax.ShapeDtypeStruct((span, planes), f32),
        ],
        scratch_shapes=[
            pltpu.VMEM((planes, cells, members), f32),
            pltpu.VMEM((observed, 16, members), f32),
            pltpu.VMEM((observed, height), f32),
            pltpu.VMEM((planes, span, height), f32),
        ],
        compiler_params=params(LIMIT),
        cost_estimate=cost(3 * source.size, 4 * source.size),
    )(obs_rows, obs_rows[None, :], source, recovery, inflow)


def edge_kernel(
    place_ref, first_ref, second_ref, low_rate_ref, high_rate_ref, end_ref, term_ref, edge_ref, leaving_ref
):
    planes, span, members = first_ref.shape
    height = leaving_ref.shape[1]
    even = lax.bitwise_and(place_ref[0], 1) == 0
    low, high = None, None
    for p in range(planes):
        one = vertical_mix * first_ref[p].astype(jnp.float32)
        two = vertical_mix * second_ref[p].astype(jnp.float32)
        low_term = jnp.where(even, two, one)
        high_term = jnp.where(even, one, two)
        term_ref[0, p] = low_term
        term_ref[1, p] = high_term
        low = low_term if p == 0 else low_rate_ref[:, p : p + 1] * low + low_term
        high = high_term if p == 0 else high_rate_ref[:, p : p + 1] * high + high_term
        edge_ref[0, p] = low
        edge_ref[1, p] = high
    row = lax.broadcasted_iota(jnp.int32, (height, members), 0)
    for a in range(span):
        share = jnp.where(row == 0, low[a : a + 1], jnp.where(row == height - 1, high[a : a + 1], 0.0))
        leaving_ref[a] = end_ref[a * height : (a + 1) * height] + share


def edge_march(place, first, second, low_rate, high_rate, end):
    planes, span, members = first.shape
    vmem = pl.BlockSpec(memory_space=pltpu.VMEM)
    return pl.pallas_call(
        edge_kernel,
        in_specs=[pl.BlockSpec(memory_space=pltpu.SMEM)] + [vmem] * 5,
        out_specs=[vmem] * 3,
        out_shape=[
            jax.ShapeDtypeStruct((2, planes, span, members), jnp.float32),
            jax.ShapeDtypeStruct((2, planes, span, members), jnp.float32),
            jax.ShapeDtypeStruct((span, end.shape[0] // span, members), jnp.float32),
        ],
        compiler_params=params(LIMIT),
        cost_estimate=cost(first.size, 8 * first.size),
    )(place, first, second, low_rate, high_rate, end)


def payload(forecast, obs, weight):
    members = forecast.shape[1]
    mean = jnp.sum(forecast, axis=1, keepdims=True) * (1.0 / members)
    anomaly = (forecast - mean).astype(jnp.bfloat16).astype(jnp.float32)
    observed = weight * anomaly
    misfit = weight * (obs - mean)
    projection = jnp.sum(observed * misfit, axis=0, keepdims=True)
    one = projection.astype(jnp.bfloat16).astype(jnp.float32)
    two = (projection - one).astype(jnp.bfloat16).astype(jnp.float32)
    three = projection - one - two
    row = lax.broadcasted_iota(jnp.int32, (EXTRA, members), 0)
    pieces = jnp.where(row == 0, one, jnp.where(row == 1, two, jnp.where(row == 2, three, 0.0)))
    return jnp.concatenate([observed, pieces], axis=0).astype(jnp.bfloat16)


def prepare_kernel(
    height, rows_ref, edge_ref, picks_ref, obs_ref, weight_ref, out_ref, obs_out_ref, weight_out_ref, first_ref
):
    _, planes, span, _ = edge_ref.shape
    for k in range(picks_ref.shape[0]):
        p, a, b = place_of(rows_ref[k], (planes, span, height))
        side = jnp.where(b == height - 1, 1, 0)
        at_edge = jnp.where((b == 0) | (b == height - 1), 1.0, 0.0)
        out_ref[pl.ds(k, 1), :] = picks_ref[pl.ds(k, 1), :] - at_edge * edge_ref[side, p, pl.ds(a, 1), :]
    obs, weight = upright(obs_ref[...]), upright(weight_ref[...])
    obs_out_ref[...] = jnp.broadcast_to(obs, obs_out_ref.shape)
    weight_out_ref[...] = jnp.broadcast_to(weight, weight_out_ref.shape)
    first_ref[...] = payload(out_ref[...], obs, weight)


def prepare(obs_rows, obs, weight, picks, edge, height):
    count, members = picks.shape
    vmem = pl.BlockSpec(memory_space=pltpu.VMEM)
    out = jax.ShapeDtypeStruct(picks.shape, jnp.float32)
    return pl.pallas_call(
        functools.partial(prepare_kernel, height),
        in_specs=[pl.BlockSpec(memory_space=pltpu.SMEM)] + [vmem] * 4,
        out_specs=[vmem] * 4,
        out_shape=[out] * 3 + [jax.ShapeDtypeStruct((count + EXTRA, members), jnp.bfloat16)],
        compiler_params=params(LIMIT),
        cost_estimate=cost(100 * picks.size, 64 * picks.size),
    )(obs_rows, edge, picks, obs[None, :], weight[None, :])


def observe_kernel(
    place_ref, rows_ref, obs_ref, weight_ref, picks_ref, share_ref, first_ref, incoming_ref, out_ref, arriving
):
    @pl.when(place_ref[0] < 2)
    def _():
        out_ref[...] = first_ref[...]

    @pl.when(place_ref[0] >= 2)
    def _():
        for k in range(picks_ref.shape[0]):
            _, a, b = place_of(rows_ref[k], (0,) + incoming_ref.shape[:2])
            arriving[pl.ds(k, 1), :] = incoming_ref[a, pl.ds(b, 1), :]
        forecast = picks_ref[...] - share_ref[...] * arriving[...]
        out_ref[...] = payload(forecast, obs_ref[...], weight_ref[...])


def observe(place, obs_rows, obs, weight, picks, share, first, incoming):
    count, members = picks.shape
    vmem, smem = pl.BlockSpec(memory_space=pltpu.VMEM), pl.BlockSpec(memory_space=pltpu.SMEM)
    return pl.pallas_call(
        observe_kernel,
        in_specs=[smem, smem] + [vmem] * 6,
        out_specs=vmem,
        out_shape=jax.ShapeDtypeStruct((count + EXTRA, members), jnp.bfloat16),
        scratch_shapes=[pltpu.VMEM((count, members), jnp.float32)],
        compiler_params=params(LIMIT),
        cost_estimate=cost(40 * count * members, 64 * count * members),
    )(place, obs_rows, obs, weight, picks, share, first, incoming)


def anomaly_kernel(start, planes, source_ref, inflow_ref, rate_ref, state_ref, term_ref, *refs):
    out_ref, mean_ref, end_ref = refs
    _, span, height, members = source_ref.shape
    wide = mean_ref.shape[2]
    cells = group_of(span, height)
    group = cells * height
    mix = stencil(group, height)
    row = lax.broadcasted_iota(jnp.int32, (height, members), 0)
    for p in range(start, start + planes):
        before = state_ref if p == start else end_ref
        for c in range(span // cells):
            term = dot(mix, source_ref[p, c * cells : (c + 1) * cells].reshape(group, members))
            some = slice(c * cells, (c + 1) * cells)
            part = slice(c * group, (c + 1) * group)
            halo = []
            for a in range(c * cells, (c + 1) * cells):
                low, high = term_ref[0, p, a : a + 1, :], term_ref[1, p, a : a + 1, :]
                halo.append(jnp.where(row == 0, low, jnp.where(row == height - 1, high, 0.0)))
            deficit = rate_ref[part, p : p + 1] * before[part] + (term + jnp.concatenate(halo, axis=0))
            end_ref[part] = deficit
            forecast = inflow_ref[p, some].astype(jnp.float32).reshape(group, members) - deficit
            mean = jnp.sum(forecast, axis=1, keepdims=True) * (1.0 / members)
            anomaly = (forecast - mean).astype(jnp.bfloat16)
            out_ref[p - start, some] = anomaly.reshape(cells, height, members)
            mean_ref[p - start, part] = jnp.broadcast_to(mean, (group, wide))


def anomalies(source, inflow, rates, state, term, start, stop):
    planes = stop - start
    vmem = pl.BlockSpec(memory_space=pltpu.VMEM)
    size = state.size * planes
    return pl.pallas_call(
        functools.partial(anomaly_kernel, start, planes),
        in_specs=[vmem] * 5,
        out_specs=[vmem] * 3,
        out_shape=[
            pltpu.VMEM((planes,) + source.shape[1:], jnp.bfloat16),
            pltpu.VMEM((planes, state.shape[0], min(128, state.shape[1])), jnp.float32),
            pltpu.VMEM(state.shape, jnp.float32),
        ],
        compiler_params=params(LIMIT),
        cost_estimate=cost(4 * size, 6 * size),
    )(source, inflow, rates, state, term)


def halves(x):
    big = x.astype(jnp.bfloat16)
    return big, (x - big.astype(jnp.float32)).astype(jnp.bfloat16)


def fine_dot(a, b, dims=NN):
    a_big, a_small = halves(a)
    b_big, b_small = halves(b)
    return dot(a_big, b_big, dims) + (dot(a_big, b_small, dims) + dot(a_small, b_big, dims))


def split_rows(picked, rows):
    total, members = rows.shape
    block = picked + EXTRA
    place = lax.broadcasted_iota(jnp.int32, (total, members), 0) % block
    observed = jnp.where(place < picked, rows.astype(jnp.float32), 0.0).astype(jnp.bfloat16)
    slot = lax.broadcasted_iota(jnp.int32, (16, total), 1) % block
    return observed, dot(jnp.where(slot >= picked, 1.0, 0.0).astype(jnp.bfloat16), rows)


def gram_kernel(picked, rows_ref, order_ref, gram_ref, pieces_ref, select_ref, select_t_ref):
    members = rows_ref.shape[1]
    bf16, f32 = jnp.bfloat16, jnp.float32
    row = lax.broadcasted_iota(jnp.int32, (members, members), 0)
    column = lax.broadcasted_iota(jnp.int32, (members, members), 1)
    order = order_ref[...]
    select_ref[...] = jnp.where(order == row, 1.0, 0.0).astype(bf16)
    select_t = jnp.where(upright(order.astype(f32)) == column.astype(f32), 1.0, 0.0).astype(bf16)
    select_t_ref[...] = select_t
    observed, pieces_ref[...] = split_rows(picked, rows_ref[...])
    ordered_t = dot(select_t, observed, NT).astype(bf16)
    gram_ref[...] = dot(ordered_t, ordered_t, NT) + jnp.where(row == column, members - 1.0, 0.0)


def gram_part(picked, rows, member_order):
    total, members = rows.shape
    vmem = pl.BlockSpec(memory_space=pltpu.VMEM)
    square = (members, members)
    return pl.pallas_call(
        functools.partial(gram_kernel, picked),
        in_specs=[vmem] * 2,
        out_specs=[vmem] * 4,
        out_shape=[
            jax.ShapeDtypeStruct(square, jnp.float32),
            jax.ShapeDtypeStruct((16, members), jnp.float32),
            jax.ShapeDtypeStruct(square, jnp.bfloat16),
            jax.ShapeDtypeStruct(square, jnp.bfloat16),
        ],
        compiler_params=params(LIMIT),
        cost_estimate=cost(1000 * members * 4, 4 * total * members),
    )(rows, member_order[None, :])


def update_kernel(picked, rows_ref, gram_ref, pieces_ref, select_ref, select_t_ref, *refs):
    part_refs = refs[:-6]
    out_ref, gram, factor, weights_t, results, out_sem = refs[-6:]
    members = rows_ref.shape[1]
    bf16, f32 = jnp.bfloat16, jnp.float32
    row = lax.broadcasted_iota(jnp.int32, (members, members), 0)
    column = lax.broadcasted_iota(jnp.int32, (members, members), 1)
    diagonal, lower = row == column, row > column
    identity = jnp.where(diagonal, 1.0, 0.0)
    select = select_ref[...]
    observed, pieces = split_rows(picked, rows_ref[...])
    ordered_t = dot(select_t_ref[...], observed, NT).astype(bf16)
    full = gram_ref[...] + dot(ordered_t, ordered_t, NT)
    gram[...] = full
    pieces = pieces_ref[...] + pieces
    piece_one = pieces.astype(bf16)
    piece_two, piece_three = halves(pieces - piece_one.astype(f32))
    projection = dot(piece_one, select) + (dot(piece_two, select) + dot(piece_three, select))
    on_diagonal = jnp.where(diagonal, full, 0.0)
    scale_row = lax.rsqrt(jnp.sum(on_diagonal, axis=0, keepdims=True))
    scale_column = lax.rsqrt(jnp.sum(on_diagonal, axis=1, keepdims=True))
    unit = full * scale_row * scale_column

    def lower_part(residual):
        return jnp.where(lower, residual, jnp.where(diagonal, 0.5 * residual, 0.0)).astype(bf16)

    def refine(inverse, unit):
        unit_big, unit_small = halves(unit)
        inverse = inverse.astype(bf16)
        half_way = dot(inverse, unit_big) + dot(inverse, unit_small)
        big, small = halves(half_way)
        residual = dot(big, inverse, NT) + dot(small, inverse, NT) - identity
        better = inverse.astype(f32) - dot(lower_part(residual), inverse)
        return better, jnp.sum(residual * residual)

    def finish(inverse):
        inverse_big, inverse_small = halves(inverse)
        turned = dot(inverse_big, select, NT) + dot(inverse_small, select, NT)
        coefficients = fine_dot(projection, inverse, NT)
        big, small = halves(turned)
        placed = dot(select, big) + dot(select, small)
        shift = fine_dot(coefficients, turned)[:1]
        weights_t[...] = ((members - 1.0) ** 0.5 * placed + shift).astype(bf16)

    inverse = identity - jnp.where(lower, unit, 0.0)
    unit_big = unit.astype(bf16)
    for _ in range(2):
        inverse_big = inverse.astype(bf16)
        half_way = dot(inverse_big, unit_big).astype(bf16)
        residual = dot(half_way, inverse_big, NT) - identity
        inverse = inverse - dot(lower_part(residual), inverse_big)
    inverse, error = refine(inverse, unit)
    factor[...] = inverse
    finish(inverse * scale_row)

    @pl.when(jnp.logical_not(error <= 0.04))
    def _():
        def again(carried):
            step, _ = carried
            better, error = refine(factor[...], gram[...] * scale_row * scale_column)
            factor[...] = better
            return step + 1, error

        def unfinished(carried):
            step, error = carried
            return (step < 8) & (error > 0.04) & (error < 64.0)

        _, last_error = lax.while_loop(unfinished, again, (0, error))
        factor[...] = factor[...] * scale_row

        @pl.when(jnp.logical_not(last_error <= 0.04))
        def _():
            factor[...] = identity

            def eliminate(k, carry):
                held = gram[...]
                pivot_row = gram[pl.ds(k, 1), :]
                pivot = jnp.sum(jnp.where(column[:1] == k, pivot_row, 0.0), axis=1, keepdims=True)
                pivot_column = jnp.sum(jnp.where(column == k, held, 0.0), axis=1, keepdims=True)
                share = jnp.where(row[:, :1] > k, pivot_column / pivot, 0.0)
                factor[...] = factor[...] - share * factor[pl.ds(k, 1), :]
                gram[...] = held - share * pivot_row
                return carry

            lax.fori_loop(0, members, eliminate, 0)
            pivots = jnp.sum(jnp.where(diagonal, gram[...], 0.0), axis=1, keepdims=True)
            factor[...] = factor[...] * lax.rsqrt(pivots)

        finish(factor[...])

    stores = []
    for ref, mean_ref in zip(part_refs[::2], part_refs[1::2]):
        for p in range(ref.shape[0]):
            at = len(stores)
            mean = jnp.concatenate([mean_ref[p]] * (members // mean_ref.shape[2]), axis=1)
            analysis = mean + dot(ref[p].reshape(-1, members), weights_t[...], NT)
            results[at] = analysis.astype(bf16).reshape(ref.shape[1:])
            store = pltpu.make_async_copy(results.at[at], out_ref.at[at], out_sem.at[at])
            store.start()
            stores.append(store)
    for store in stores:
        store.wait()


def updated(picked, rows, part, parts, shape):
    planes, span, height, members = shape
    size = planes * span * height * members
    vmem = pl.BlockSpec(memory_space=pltpu.VMEM)
    return pl.pallas_call(
        functools.partial(update_kernel, picked),
        in_specs=[vmem] * (1 + len(part) + len(parts)),
        out_specs=pl.BlockSpec(memory_space=pltpu.HBM),
        out_shape=jax.ShapeDtypeStruct(shape, jnp.bfloat16),
        scratch_shapes=[
            pltpu.VMEM((members, members), jnp.float32),
            pltpu.VMEM((members, members), jnp.float32),
            pltpu.VMEM((members, members), jnp.bfloat16),
            pltpu.VMEM(shape, jnp.bfloat16),
            pltpu.SemaphoreType.DMA((planes,)),
        ],
        compiler_params=params(LIMIT),
        cost_estimate=cost(4 * size, 5 * size),
    )(rows, *part, *parts)


def pairs(count, first):
    low = [(i, i + 1) for i in range(first, count - 1, 2)]
    return low + [(j, i) for i, j in low]


def downstream(value, rate):
    count = lax.axis_size("stream")
    steps = [(i, i + 1) for i in range(count - 1)]
    incoming = lax.ppermute(value, "stream", steps)
    for _ in range(count - 2):
        incoming = lax.ppermute(rate * incoming + value, "stream", steps)
    return incoming


def rounds():
    steps = []
    for axis in ("height", "span"):
        bits = (lax.axis_size(axis) - 1).bit_length()
        steps.append([(axis, (2 << bit) - 1 if axis == "height" else 1 << bit) for bit in reversed(range(bits))])
    mixed = []
    while steps[0] or steps[1]:
        pair = [axis.pop(0) for axis in steps if axis]
        mixed += [(pair[0], pair[-1]), (pair[-1], pair[0])][: len(pair)]
    return mixed


def exchanges():
    sizes = [lax.axis_size(axis) for axis in AXES]
    places = [
        {"stream": i // (sizes[1] * sizes[2]), "span": i // sizes[2] % sizes[1], "height": i % sizes[2]}
        for i in range(sizes[0] * sizes[1] * sizes[2])
    ]

    def flat(place):
        return (place["stream"] * sizes[1] + place["span"]) * sizes[2] + place["height"]

    steps = rounds()
    apart = sizes[0] // 2
    while apart:
        steps.append((("stream", apart), ("stream", apart)))
        apart //= 2
    moves = []
    for step in steps:
        taken = [(place, *step[place["stream"] % 2]) for place in places]
        moves.append([(flat(at), flat(at | {axis: at[axis] ^ bit})) for at, axis, bit in taken])
    return moves


def shards(source, inflow, recovery, obs_rows, obs, observation_weight, member_order):
    planes, span, height, members = source.shape
    levels = lax.axis_size("height")
    place = (lax.axis_index("height") % 2 + 2 * lax.axis_index("stream"))[None]
    together = lax.optimization_barrier

    source, first, second = border(source, place)
    inflow, first = together((inflow, first))
    inflow = pltpu.with_memory_space_constraint(inflow, pltpu.VMEM)
    first = lax.ppermute(first, "height", pairs(levels, 0))
    second = lax.ppermute(second, "height", pairs(levels, 1))
    end, picks, share, rates, low_rate, high_rate = march(source, inflow, recovery, obs_rows)
    end, first, second = together((end, first, second))
    term, edge, leaving = edge_march(place, first, second, low_rate, high_rate, end)
    total = jnp.prod(recovery, axis=0)[..., None] if lax.axis_size("stream") > 2 else None
    incoming = downstream(leaving, total)
    picks, obs, weight, first = prepare(obs_rows, obs, observation_weight, picks, edge, height)
    rows = observe(place, obs_rows, obs, weight, picks, share, first, incoming)
    state = incoming.reshape(span * height, members)
    cuts = [planes * part // 16 for part in CUTS]
    parts = []
    *moves, last_moves = exchanges()
    for pairing in moves:
        other = lax.ppermute(rows, AXES, pairing)
        if len(cuts) > 1:
            state, rows = together((state, rows))
            anomaly, mean, state = anomalies(source, inflow, rates, state, term, cuts[0], cuts[1])
            other, state, anomaly, mean = together((other, state, anomaly, mean))
            parts += [anomaly, mean]
            cuts = cuts[1:]
        rows = jnp.concatenate([rows, other], axis=0)
    while len(cuts) > 1:
        anomaly, mean, state = anomalies(source, inflow, rates, state, term, cuts[0], cuts[1])
        parts += [anomaly, mean]
        cuts = cuts[1:]
    other = lax.ppermute(rows, AXES, last_moves)
    part = gram_part(obs_rows.shape[0], rows, member_order)
    return updated(obs_rows.shape[0], other, part, parts, source.shape)


def solution(mesh):
    placed = (
        P("stream", "span", "height", None),
        P("stream", "span", "height", None),
        P("stream", "span", "height"),
        P(("stream", "span", "height")),
        P(("stream", "span", "height")),
        P(("stream", "span", "height")),
        P(),
    )
    return jax.shard_map(
        shards,
        mesh=mesh,
        in_specs=placed,
        out_specs=P("stream", "span", "height", None),
        check_vma=False,
    )
```

```python
import functools

import jax
import jax.numpy as jnp
from jax import lax
from jax.experimental import pallas as pl
from jax.experimental.pallas import tpu as pltpu
from jax.sharding import PartitionSpec as P

vertical_mix = 0.25
MIB = 1024 * 1024
NT = (((1,), (1,)), ((), ()))
NN = (((1,), (0,)), ((), ()))
LIMIT = 24
CUTS = (0, 4, 8, 12, 16)
AXES = ("stream", "span", "height")
EXTRA = 8


def dot(a, b, dims=NN):
    return lax.dot_general(a, b, dims, preferred_element_type=jnp.float32)


def params(mib):
    return pltpu.CompilerParams(vmem_limit_bytes=mib * MIB)


def cost(elements, nbytes):
    return pl.CostEstimate(flops=1000 * elements, bytes_accessed=nbytes, transcendentals=0)


def take_border(out_ref, p, block, top):
    span = block.shape[0]
    block = block.astype(jnp.float32)
    low = jnp.concatenate([block[a, :1] for a in range(span)], axis=0)
    high = jnp.concatenate([block[a, 15:] for a in range(span)], axis=0)
    out_ref[p] = jnp.where(top, high, low).astype(jnp.bfloat16)


def first_border_kernel(place_ref, source_ref, out_ref, held, sems):
    planes, _, height, _ = source_ref.shape
    top = lax.bitwise_and(place_ref[0], 1) == 0
    start = pl.multiple_of(jnp.where(top, height - 16, 0), 16)
    step = planes // sems.shape[0]

    def fetch(c):
        part = pl.ds(c * step, step)
        return pltpu.make_async_copy(source_ref.at[part, :, pl.ds(start, 16), :], held.at[part], sems.at[c])

    for c in range(sems.shape[0]):
        fetch(c).start()
    for c in range(sems.shape[0]):
        fetch(c).wait()
        for p in range(c * step, (c + 1) * step):
            take_border(out_ref, p, held[p], top)


def second_border_kernel(place_ref, source_ref, out_ref):
    height = source_ref.shape[2]
    top = lax.bitwise_and(place_ref[0], 1) == 1
    start = pl.multiple_of(jnp.where(top, height - 16, 0), 16)
    for p in range(source_ref.shape[0]):
        take_border(out_ref, p, source_ref[p, :, pl.ds(start, 16), :], top)


def border(source, place, far):
    planes, span, _, members = source.shape
    count = 4 if planes % 4 == 0 else 1
    vmem, hbm = pl.BlockSpec(memory_space=pltpu.VMEM), pl.BlockSpec(memory_space=pltpu.HBM)
    scratch = [
        pltpu.VMEM((planes, span, 16, members), jnp.bfloat16),
        pltpu.SemaphoreType.DMA((count,)),
    ]
    return pl.pallas_call(
        first_border_kernel if far else second_border_kernel,
        in_specs=[pl.BlockSpec(memory_space=pltpu.SMEM), hbm if far else vmem],
        out_specs=vmem,
        out_shape=jax.ShapeDtypeStruct((planes, span, members), jnp.bfloat16),
        scratch_shapes=scratch if far else [],
        compiler_params=params(LIMIT),
        cost_estimate=cost(source.size // 2, source.size),
    )(place, source)


def parted(value, size):
    if size & (size - 1):
        return lax.div(value, size), lax.rem(value, size)
    return lax.shift_right_logical(value, size.bit_length() - 1), lax.bitwise_and(value, size - 1)


def place_of(r, shape):
    _, span, height = shape
    rest, b = parted(r, height)
    p, a = parted(rest, span)
    return p, a, b


def group_of(span, height):
    cells = max(1, min(span, 256 // height))
    while span % cells:
        cells -= 1
    return cells


def stencil(rows, height):
    row = lax.broadcasted_iota(jnp.int32, (rows, rows), 0)
    column = lax.broadcasted_iota(jnp.int32, (rows, rows), 1)
    apart = jnp.where(row // height == column // height, jnp.abs(row - column), 2)
    entry = jnp.where(apart == 0, 1.0 - 2.0 * vertical_mix, jnp.where(apart == 1, vertical_mix, 0.0))
    return entry.astype(jnp.bfloat16)


def upright(row):
    count = row.shape[1]
    place = lax.broadcasted_iota(jnp.int32, (count, count), 0)
    lane = lax.broadcasted_iota(jnp.int32, (count, count), 1)
    return jnp.sum(jnp.where(place == lane, row, jnp.zeros_like(row)), axis=1, keepdims=True)


def march_kernel(
    rows_ref, rows_row_ref, source_ref, recovery_ref, inflow_ref,
    end_ref, picks_ref, share_ref, rate_ref, low_rate_ref, high_rate_ref,
    deficits, tiles, through_rows, through,
):
    shape = source_ref.shape[:3]
    planes, span, height = shape
    count, members = picks_ref.shape
    cells = group_of(span, height)
    group = cells * height
    blocks = [jnp.transpose(recovery_ref[:, a, :]) for a in range(span)]
    for a in range(span):
        rate_ref[a * height : (a + 1) * height] = blocks[a]
    low_rate_ref[...] = jnp.concatenate([block[:1] for block in blocks], axis=0)
    high_rate_ref[...] = jnp.concatenate([block[height - 1 :] for block in blocks], axis=0)
    mix = stencil(group, height)
    product = None
    for p in range(planes):
        product = recovery_ref[p] if p == 0 else product * recovery_ref[p]
        through[p] = product
        for c in range(span // cells):
            part = slice(c * group, (c + 1) * group)
            term = dot(mix, source_ref[p, c * cells : (c + 1) * cells].reshape(group, members))
            if p > 0:
                term = rate_ref[part, p : p + 1] * deficits[p - 1, part] + term
            deficits[p, part] = term
    end_ref[...] = deficits[planes - 1]
    for k in range(count):
        p, a, b = place_of(rows_ref[k], shape)
        first = pl.multiple_of(b - lax.bitwise_and(b, 15), 16)
        tiles[k] = inflow_ref[p, a, pl.ds(first, 16), :].astype(jnp.float32)
        through_rows[pl.ds(k, 1), :] = through[p, pl.ds(a, 1), :]
    for k in range(count):
        p, a, b = place_of(rows_ref[k], shape)
        picks_ref[pl.ds(k, 1), :] = (
            tiles[k, pl.ds(lax.bitwise_and(b, 15), 1), :] - deficits[p, pl.ds(a * height + b, 1), :]
        )
    cell = upright(rows_row_ref[...].astype(jnp.float32)).astype(jnp.int32) % height
    lane = lax.broadcasted_iota(jnp.int32, (count, height), 1)
    share = jnp.sum(jnp.where(lane == cell, through_rows[...], 0.0), axis=1, keepdims=True)
    share_ref[...] = jnp.broadcast_to(share, share_ref.shape)


def march(source, inflow, recovery, obs_rows):
    planes, span, height, members = source.shape
    observed = obs_rows.shape[0]
    cells = span * height
    f32 = jnp.float32
    vmem = pl.BlockSpec(memory_space=pltpu.VMEM)
    return pl.pallas_call(
        march_kernel,
        in_specs=[pl.BlockSpec(memory_space=pltpu.SMEM)] + [vmem] * 4,
        out_specs=[vmem] * 6,
        out_shape=[
            jax.ShapeDtypeStruct((cells, members), f32),
            jax.ShapeDtypeStruct((observed, members), f32),
            jax.ShapeDtypeStruct((observed, members), f32),
            jax.ShapeDtypeStruct((cells, planes), f32),
            jax.ShapeDtypeStruct((span, planes), f32),
            jax.ShapeDtypeStruct((span, planes), f32),
        ],
        scratch_shapes=[
            pltpu.VMEM((planes, cells, members), f32),
            pltpu.VMEM((observed, 16, members), f32),
            pltpu.VMEM((observed, height), f32),
            pltpu.VMEM((planes, span, height), f32),
        ],
        compiler_params=params(LIMIT),
        cost_estimate=cost(3 * source.size, 4 * source.size),
    )(obs_rows, obs_rows[None, :], source, recovery, inflow)


def edge_kernel(
    place_ref, first_ref, second_ref, low_rate_ref, high_rate_ref, end_ref, term_ref, edge_ref, leaving_ref
):
    planes, span, members = first_ref.shape
    height = leaving_ref.shape[1]
    even = lax.bitwise_and(place_ref[0], 1) == 0
    low, high = None, None
    for p in range(planes):
        one = vertical_mix * first_ref[p].astype(jnp.float32)
        two = vertical_mix * second_ref[p].astype(jnp.float32)
        low_term = jnp.where(even, two, one)
        high_term = jnp.where(even, one, two)
        term_ref[0, p] = low_term
        term_ref[1, p] = high_term
        low = low_term if p == 0 else low_rate_ref[:, p : p + 1] * low + low_term
        high = high_term if p == 0 else high_rate_ref[:, p : p + 1] * high + high_term
        edge_ref[0, p] = low
        edge_ref[1, p] = high
    row = lax.broadcasted_iota(jnp.int32, (height, members), 0)
    for a in range(span):
        share = jnp.where(row == 0, low[a : a + 1], jnp.where(row == height - 1, high[a : a + 1], 0.0))
        leaving_ref[a] = end_ref[a * height : (a + 1) * height] + share


def edge_march(place, first, second, low_rate, high_rate, end):
    planes, span, members = first.shape
    vmem = pl.BlockSpec(memory_space=pltpu.VMEM)
    return pl.pallas_call(
        edge_kernel,
        in_specs=[pl.BlockSpec(memory_space=pltpu.SMEM)] + [vmem] * 5,
        out_specs=[vmem] * 3,
        out_shape=[
            jax.ShapeDtypeStruct((2, planes, span, members), jnp.float32),
            jax.ShapeDtypeStruct((2, planes, span, members), jnp.float32),
            jax.ShapeDtypeStruct((span, end.shape[0] // span, members), jnp.float32),
        ],
        compiler_params=params(LIMIT),
        cost_estimate=cost(first.size, 8 * first.size),
    )(place, first, second, low_rate, high_rate, end)


def payload(forecast, obs, weight):
    members = forecast.shape[1]
    mean = jnp.sum(forecast, axis=1, keepdims=True) * (1.0 / members)
    anomaly = (forecast - mean).astype(jnp.bfloat16).astype(jnp.float32)
    observed = weight * anomaly
    misfit = weight * (obs - mean)
    projection = jnp.sum(observed * misfit, axis=0, keepdims=True)
    one = projection.astype(jnp.bfloat16).astype(jnp.float32)
    two = (projection - one).astype(jnp.bfloat16).astype(jnp.float32)
    three = projection - one - two
    row = lax.broadcasted_iota(jnp.int32, (EXTRA, members), 0)
    pieces = jnp.where(row == 0, one, jnp.where(row == 1, two, jnp.where(row == 2, three, 0.0)))
    return jnp.concatenate([observed, pieces], axis=0).astype(jnp.bfloat16)


def prepare_kernel(
    height, rows_ref, edge_ref, picks_ref, obs_ref, weight_ref, out_ref, obs_out_ref, weight_out_ref, first_ref
):
    _, planes, span, _ = edge_ref.shape
    for k in range(picks_ref.shape[0]):
        p, a, b = place_of(rows_ref[k], (planes, span, height))
        side = jnp.where(b == height - 1, 1, 0)
        at_edge = jnp.where((b == 0) | (b == height - 1), 1.0, 0.0)
        out_ref[pl.ds(k, 1), :] = picks_ref[pl.ds(k, 1), :] - at_edge * edge_ref[side, p, pl.ds(a, 1), :]
    obs, weight = upright(obs_ref[...]), upright(weight_ref[...])
    obs_out_ref[...] = jnp.broadcast_to(obs, obs_out_ref.shape)
    weight_out_ref[...] = jnp.broadcast_to(weight, weight_out_ref.shape)
    first_ref[...] = payload(out_ref[...], obs, weight)


def prepare(obs_rows, obs, weight, picks, edge, height):
    count, members = picks.shape
    vmem = pl.BlockSpec(memory_space=pltpu.VMEM)
    out = jax.ShapeDtypeStruct(picks.shape, jnp.float32)
    return pl.pallas_call(
        functools.partial(prepare_kernel, height),
        in_specs=[pl.BlockSpec(memory_space=pltpu.SMEM)] + [vmem] * 4,
        out_specs=[vmem] * 4,
        out_shape=[out] * 3 + [jax.ShapeDtypeStruct((count + EXTRA, members), jnp.bfloat16)],
        compiler_params=params(LIMIT),
        cost_estimate=cost(100 * picks.size, 64 * picks.size),
    )(obs_rows, edge, picks, obs[None, :], weight[None, :])


def observe_kernel(
    place_ref, rows_ref, obs_ref, weight_ref, picks_ref, share_ref, first_ref, incoming_ref, out_ref, arriving
):
    @pl.when(place_ref[0] < 2)
    def _():
        out_ref[...] = first_ref[...]

    @pl.when(place_ref[0] >= 2)
    def _():
        for k in range(picks_ref.shape[0]):
            _, a, b = place_of(rows_ref[k], (0,) + incoming_ref.shape[:2])
            arriving[pl.ds(k, 1), :] = incoming_ref[a, pl.ds(b, 1), :]
        forecast = picks_ref[...] - share_ref[...] * arriving[...]
        out_ref[...] = payload(forecast, obs_ref[...], weight_ref[...])


def observe(place, obs_rows, obs, weight, picks, share, first, incoming):
    count, members = picks.shape
    vmem, smem = pl.BlockSpec(memory_space=pltpu.VMEM), pl.BlockSpec(memory_space=pltpu.SMEM)
    return pl.pallas_call(
        observe_kernel,
        in_specs=[smem, smem] + [vmem] * 6,
        out_specs=vmem,
        out_shape=jax.ShapeDtypeStruct((count + EXTRA, members), jnp.bfloat16),
        scratch_shapes=[pltpu.VMEM((count, members), jnp.float32)],
        compiler_params=params(LIMIT),
        cost_estimate=cost(40 * count * members, 64 * count * members),
    )(place, obs_rows, obs, weight, picks, share, first, incoming)


def anomaly_kernel(start, planes, source_ref, inflow_ref, rate_ref, state_ref, term_ref, *refs):
    out_ref, mean_ref, end_ref = refs
    _, span, height, members = source_ref.shape
    wide = mean_ref.shape[2]
    cells = group_of(span, height)
    group = cells * height
    mix = stencil(group, height)
    row = lax.broadcasted_iota(jnp.int32, (height, members), 0)
    for p in range(start, start + planes):
        before = state_ref if p == start else end_ref
        for c in range(span // cells):
            term = dot(mix, source_ref[p, c * cells : (c + 1) * cells].reshape(group, members))
            some = slice(c * cells, (c + 1) * cells)
            part = slice(c * group, (c + 1) * group)
            halo = []
            for a in range(c * cells, (c + 1) * cells):
                low, high = term_ref[0, p, a : a + 1, :], term_ref[1, p, a : a + 1, :]
                halo.append(jnp.where(row == 0, low, jnp.where(row == height - 1, high, 0.0)))
            deficit = rate_ref[part, p : p + 1] * before[part] + (term + jnp.concatenate(halo, axis=0))
            end_ref[part] = deficit
            forecast = inflow_ref[p, some].astype(jnp.float32).reshape(group, members) - deficit
            mean = jnp.sum(forecast, axis=1, keepdims=True) * (1.0 / members)
            anomaly = (forecast - mean).astype(jnp.bfloat16)
            out_ref[p - start, some] = anomaly.reshape(cells, height, members)
            mean_ref[p - start, part] = jnp.broadcast_to(mean, (group, wide))


def anomalies(source, inflow, rates, state, term, start, stop):
    planes = stop - start
    vmem = pl.BlockSpec(memory_space=pltpu.VMEM)
    size = state.size * planes
    return pl.pallas_call(
        functools.partial(anomaly_kernel, start, planes),
        in_specs=[vmem] * 5,
        out_specs=[vmem] * 3,
        out_shape=[
            pltpu.VMEM((planes,) + source.shape[1:], jnp.bfloat16),
            pltpu.VMEM((planes, state.shape[0], min(128, state.shape[1])), jnp.float32),
            pltpu.VMEM(state.shape, jnp.float32),
        ],
        compiler_params=params(LIMIT),
        cost_estimate=cost(4 * size, 6 * size),
    )(source, inflow, rates, state, term)


def halves(x):
    big = x.astype(jnp.bfloat16)
    return big, (x - big.astype(jnp.float32)).astype(jnp.bfloat16)


def fine_dot(a, b, dims=NN):
    a_big, a_small = halves(a)
    b_big, b_small = halves(b)
    return dot(a_big, b_big, dims) + (dot(a_big, b_small, dims) + dot(a_small, b_big, dims))


def split_rows(picked, rows):
    total, members = rows.shape
    block = picked + EXTRA
    place = lax.broadcasted_iota(jnp.int32, (total, members), 0) % block
    observed = jnp.where(place < picked, rows.astype(jnp.float32), 0.0).astype(jnp.bfloat16)
    slot = lax.broadcasted_iota(jnp.int32, (16, total), 1) % block
    return observed, dot(jnp.where(slot >= picked, 1.0, 0.0).astype(jnp.bfloat16), rows)


def gram_kernel(picked, rows_ref, order_ref, gram_ref, pieces_ref, select_ref, select_t_ref):
    members = rows_ref.shape[1]
    bf16, f32 = jnp.bfloat16, jnp.float32
    row = lax.broadcasted_iota(jnp.int32, (members, members), 0)
    column = lax.broadcasted_iota(jnp.int32, (members, members), 1)
    order = order_ref[...]
    select_ref[...] = jnp.where(order == row, 1.0, 0.0).astype(bf16)
    select_t = jnp.where(upright(order.astype(f32)) == column.astype(f32), 1.0, 0.0).astype(bf16)
    select_t_ref[...] = select_t
    observed, pieces_ref[...] = split_rows(picked, rows_ref[...])
    ordered_t = dot(select_t, observed, NT).astype(bf16)
    gram_ref[...] = dot(ordered_t, ordered_t, NT) + jnp.where(row == column, members - 1.0, 0.0)


def gram_part(picked, rows, member_order):
    total, members = rows.shape
    vmem = pl.BlockSpec(memory_space=pltpu.VMEM)
    square = (members, members)
    return pl.pallas_call(
        functools.partial(gram_kernel, picked),
        in_specs=[vmem] * 2,
        out_specs=[vmem] * 4,
        out_shape=[
            jax.ShapeDtypeStruct(square, jnp.float32),
            jax.ShapeDtypeStruct((16, members), jnp.float32),
            jax.ShapeDtypeStruct(square, jnp.bfloat16),
            jax.ShapeDtypeStruct(square, jnp.bfloat16),
        ],
        compiler_params=params(LIMIT),
        cost_estimate=cost(1000 * members * 4, 4 * total * members),
    )(rows, member_order[None, :])


def update_kernel(picked, rows_ref, gram_ref, pieces_ref, select_ref, select_t_ref, *refs):
    part_refs = refs[:-6]
    out_ref, gram, factor, weights_t, results, out_sem = refs[-6:]
    members = rows_ref.shape[1]
    bf16, f32 = jnp.bfloat16, jnp.float32
    row = lax.broadcasted_iota(jnp.int32, (members, members), 0)
    column = lax.broadcasted_iota(jnp.int32, (members, members), 1)
    diagonal, lower = row == column, row > column
    identity = jnp.where(diagonal, 1.0, 0.0)
    select = select_ref[...]
    observed, pieces = split_rows(picked, rows_ref[...])
    ordered_t = dot(select_t_ref[...], observed, NT).astype(bf16)
    full = gram_ref[...] + dot(ordered_t, ordered_t, NT)
    gram[...] = full
    pieces = pieces_ref[...] + pieces
    piece_one = pieces.astype(bf16)
    piece_two, piece_three = halves(pieces - piece_one.astype(f32))
    projection = dot(piece_one, select) + (dot(piece_two, select) + dot(piece_three, select))
    on_diagonal = jnp.where(diagonal, full, 0.0)
    scale_row = lax.rsqrt(jnp.sum(on_diagonal, axis=0, keepdims=True))
    scale_column = lax.rsqrt(jnp.sum(on_diagonal, axis=1, keepdims=True))
    unit = full * scale_row * scale_column

    def lower_part(residual):
        return jnp.where(lower, residual, jnp.where(diagonal, 0.5 * residual, 0.0)).astype(bf16)

    def refine(inverse, unit):
        unit_big, unit_small = halves(unit)
        inverse = inverse.astype(bf16)
        half_way = dot(inverse, unit_big) + dot(inverse, unit_small)
        big, small = halves(half_way)
        residual = dot(big, inverse, NT) + dot(small, inverse, NT) - identity
        better = inverse.astype(f32) - dot(lower_part(residual), inverse)
        return better, jnp.sum(residual * residual)

    def finish(inverse):
        inverse_big, inverse_small = halves(inverse)
        turned = dot(inverse_big, select, NT) + dot(inverse_small, select, NT)
        coefficients = fine_dot(projection, inverse, NT)
        big, small = halves(turned)
        placed = dot(select, big) + dot(select, small)
        shift = fine_dot(coefficients, turned)[:1]
        weights_t[...] = ((members - 1.0) ** 0.5 * placed + shift).astype(bf16)

    inverse = identity - jnp.where(lower, unit, 0.0)
    unit_big = unit.astype(bf16)
    for _ in range(2):
        inverse_big = inverse.astype(bf16)
        half_way = dot(inverse_big, unit_big).astype(bf16)
        residual = dot(half_way, inverse_big, NT) - identity
        inverse = inverse - dot(lower_part(residual), inverse_big)
    inverse, error = refine(inverse, unit)
    factor[...] = inverse
    finish(inverse * scale_row)

    @pl.when(jnp.logical_not(error <= 0.04))
    def _():
        def again(carried):
            step, _ = carried
            better, error = refine(factor[...], gram[...] * scale_row * scale_column)
            factor[...] = better
            return step + 1, error

        def unfinished(carried):
            step, error = carried
            return (step < 8) & (error > 0.04) & (error < 64.0)

        _, last_error = lax.while_loop(unfinished, again, (0, error))
        factor[...] = factor[...] * scale_row

        @pl.when(jnp.logical_not(last_error <= 0.04))
        def _():
            factor[...] = identity

            def eliminate(k, carry):
                held = gram[...]
                pivot_row = gram[pl.ds(k, 1), :]
                pivot = jnp.sum(jnp.where(column[:1] == k, pivot_row, 0.0), axis=1, keepdims=True)
                pivot_column = jnp.sum(jnp.where(column == k, held, 0.0), axis=1, keepdims=True)
                share = jnp.where(row[:, :1] > k, pivot_column / pivot, 0.0)
                factor[...] = factor[...] - share * factor[pl.ds(k, 1), :]
                gram[...] = held - share * pivot_row
                return carry

            lax.fori_loop(0, members, eliminate, 0)
            pivots = jnp.sum(jnp.where(diagonal, gram[...], 0.0), axis=1, keepdims=True)
            factor[...] = factor[...] * lax.rsqrt(pivots)

        finish(factor[...])

    stores = []
    for ref, mean_ref in zip(part_refs[::2], part_refs[1::2]):
        for p in range(ref.shape[0]):
            at = len(stores)
            mean = jnp.concatenate([mean_ref[p]] * (members // mean_ref.shape[2]), axis=1)
            analysis = mean + dot(ref[p].reshape(-1, members), weights_t[...], NT)
            results[at] = analysis.astype(bf16).reshape(ref.shape[1:])
            store = pltpu.make_async_copy(results.at[at], out_ref.at[at], out_sem.at[at])
            store.start()
            stores.append(store)
    for store in stores:
        store.wait()


def updated(picked, rows, part, parts, shape):
    planes, span, height, members = shape
    size = planes * span * height * members
    vmem = pl.BlockSpec(memory_space=pltpu.VMEM)
    return pl.pallas_call(
        functools.partial(update_kernel, picked),
        in_specs=[vmem] * (1 + len(part) + len(parts)),
        out_specs=pl.BlockSpec(memory_space=pltpu.HBM),
        out_shape=jax.ShapeDtypeStruct(shape, jnp.bfloat16),
        scratch_shapes=[
            pltpu.VMEM((members, members), jnp.float32),
            pltpu.VMEM((members, members), jnp.float32),
            pltpu.VMEM((members, members), jnp.bfloat16),
            pltpu.VMEM(shape, jnp.bfloat16),
            pltpu.SemaphoreType.DMA((planes,)),
        ],
        compiler_params=params(LIMIT),
        cost_estimate=cost(4 * size, 5 * size),
    )(rows, *part, *parts)


def pairs(count, first):
    low = [(i, i + 1) for i in range(first, count - 1, 2)]
    return low + [(j, i) for i, j in low]


def downstream(value, rate):
    count = lax.axis_size("stream")
    steps = [(i, i + 1) for i in range(count - 1)]
    incoming = lax.ppermute(value, "stream", steps)
    for _ in range(count - 2):
        incoming = lax.ppermute(rate * incoming + value, "stream", steps)
    return incoming


def rounds():
    steps = []
    for axis in ("height", "span"):
        bits = (lax.axis_size(axis) - 1).bit_length()
        steps.append([(axis, (2 << bit) - 1 if axis == "height" else 1 << bit) for bit in reversed(range(bits))])
    mixed = []
    while steps[0] or steps[1]:
        pair = [axis.pop(0) for axis in steps if axis]
        mixed += [(pair[0], pair[-1]), (pair[-1], pair[0])][: len(pair)]
    return mixed


def exchanges():
    sizes = [lax.axis_size(axis) for axis in AXES]
    places = [
        {"stream": i // (sizes[1] * sizes[2]), "span": i // sizes[2] % sizes[1], "height": i % sizes[2]}
        for i in range(sizes[0] * sizes[1] * sizes[2])
    ]

    def flat(place):
        return (place["stream"] * sizes[1] + place["span"]) * sizes[2] + place["height"]

    steps = rounds()
    apart = sizes[0] // 2
    while apart:
        steps.append((("stream", apart), ("stream", apart)))
        apart //= 2
    moves = []
    for step in steps:
        taken = [(place, *step[place["stream"] % 2]) for place in places]
        moves.append([(flat(at), flat(at | {axis: at[axis] ^ bit})) for at, axis, bit in taken])
    return moves


def shards(source, inflow, recovery, obs_rows, obs, observation_weight, member_order):
    planes, span, height, members = source.shape
    levels = lax.axis_size("height")
    place = (lax.axis_index("height") % 2 + 2 * lax.axis_index("stream"))[None]
    together = lax.optimization_barrier

    first = border(pltpu.with_memory_space_constraint(source, pltpu.HBM), place, True)
    source = pltpu.with_memory_space_constraint(source, pltpu.VMEM)
    inflow, first = together((inflow, first))
    inflow = pltpu.with_memory_space_constraint(inflow, pltpu.VMEM)
    second = border(source, place, False)
    first = lax.ppermute(first, "height", pairs(levels, 0))
    second = lax.ppermute(second, "height", pairs(levels, 1))
    end, picks, share, rates, low_rate, high_rate = march(source, inflow, recovery, obs_rows)
    end, first, second = together((end, first, second))
    term, edge, leaving = edge_march(place, first, second, low_rate, high_rate, end)
    total = jnp.prod(recovery, axis=0)[..., None] if lax.axis_size("stream") > 2 else None
    incoming = downstream(leaving, total)
    picks, obs, weight, first = prepare(obs_rows, obs, observation_weight, picks, edge, height)
    rows = observe(place, obs_rows, obs, weight, picks, share, first, incoming)
    state = incoming.reshape(span * height, members)
    cuts = [planes * part // 16 for part in CUTS]
    parts = []
    *moves, last_moves = exchanges()
    for pairing in moves:
        other = lax.ppermute(rows, AXES, pairing)
        if len(cuts) > 1:
            state, rows = together((state, rows))
            anomaly, mean, state = anomalies(source, inflow, rates, state, term, cuts[0], cuts[1])
            other, state, anomaly, mean = together((other, state, anomaly, mean))
            parts += [anomaly, mean]
            cuts = cuts[1:]
        rows = jnp.concatenate([rows, other], axis=0)
    while len(cuts) > 1:
        anomaly, mean, state = anomalies(source, inflow, rates, state, term, cuts[0], cuts[1])
        parts += [anomaly, mean]
        cuts = cuts[1:]
    other = lax.ppermute(rows, AXES, last_moves)
    part = gram_part(obs_rows.shape[0], rows, member_order)
    return updated(obs_rows.shape[0], other, part, parts, source.shape)


def solution(mesh):
    placed = (
        P("stream", "span", "height", None),
        P("stream", "span", "height", None),
        P("stream", "span", "height"),
        P(("stream", "span", "height")),
        P(("stream", "span", "height")),
        P(("stream", "span", "height")),
        P(),
    )
    return jax.shard_map(
        shards,
        mesh=mesh,
        in_specs=placed,
        out_specs=P("stream", "span", "height", None),
        check_vma=False,
    )
```

```python
import functools

import jax
import jax.numpy as jnp
from jax import lax
from jax.experimental import pallas as pl
from jax.experimental.pallas import tpu as pltpu
from jax.sharding import PartitionSpec as P

vertical_mix = 0.25
MIB = 1024 * 1024
NT = (((1,), (1,)), ((), ()))
NN = (((1,), (0,)), ((), ()))
LIMIT = 24
CUTS = (0, 4, 8, 12, 16)
AXES = ("stream", "span", "height")
EXTRA = 8


def dot(a, b, dims=NN):
    return lax.dot_general(a, b, dims, preferred_element_type=jnp.float32)


def params(mib):
    return pltpu.CompilerParams(vmem_limit_bytes=mib * MIB)


def cost(elements, nbytes):
    return pl.CostEstimate(flops=1000 * elements, bytes_accessed=nbytes, transcendentals=0)


def take_border(out_ref, p, block, top):
    span = block.shape[0]
    block = block.astype(jnp.float32)
    low = jnp.concatenate([block[a, :1] for a in range(span)], axis=0)
    high = jnp.concatenate([block[a, 15:] for a in range(span)], axis=0)
    out_ref[p] = jnp.where(top, high, low).astype(jnp.bfloat16)


def first_border_kernel(place_ref, source_ref, out_ref, held, sems):
    planes, _, height, _ = source_ref.shape
    top = lax.bitwise_and(place_ref[0], 1) == 0
    start = pl.multiple_of(jnp.where(top, height - 16, 0), 16)
    step = planes // sems.shape[0]

    def fetch(c):
        part = pl.ds(c * step, step)
        return pltpu.make_async_copy(source_ref.at[part, :, pl.ds(start, 16), :], held.at[part], sems.at[c])

    for c in range(sems.shape[0]):
        fetch(c).start()
    for c in range(sems.shape[0]):
        fetch(c).wait()
        for p in range(c * step, (c + 1) * step):
            take_border(out_ref, p, held[p], top)


def second_border_kernel(place_ref, source_ref, out_ref):
    height = source_ref.shape[2]
    top = lax.bitwise_and(place_ref[0], 1) == 1
    start = pl.multiple_of(jnp.where(top, height - 16, 0), 16)
    for p in range(source_ref.shape[0]):
        take_border(out_ref, p, source_ref[p, :, pl.ds(start, 16), :], top)


def border(source, place, far):
    planes, span, _, members = source.shape
    count = 4 if planes % 4 == 0 else 1
    vmem, hbm = pl.BlockSpec(memory_space=pltpu.VMEM), pl.BlockSpec(memory_space=pltpu.HBM)
    scratch = [
        pltpu.VMEM((planes, span, 16, members), jnp.bfloat16),
        pltpu.SemaphoreType.DMA((count,)),
    ]
    return pl.pallas_call(
        first_border_kernel if far else second_border_kernel,
        in_specs=[pl.BlockSpec(memory_space=pltpu.SMEM), hbm if far else vmem],
        out_specs=vmem,
        out_shape=jax.ShapeDtypeStruct((planes, span, members), jnp.bfloat16),
        scratch_shapes=scratch if far else [],
        compiler_params=params(LIMIT),
        cost_estimate=cost(source.size // 2, source.size),
    )(place, source)


def parted(value, size):
    if size & (size - 1):
        return lax.div(value, size), lax.rem(value, size)
    return lax.shift_right_logical(value, size.bit_length() - 1), lax.bitwise_and(value, size - 1)


def place_of(r, shape):
    _, span, height = shape
    rest, b = parted(r, height)
    p, a = parted(rest, span)
    return p, a, b


def group_of(span, height):
    cells = max(1, min(span, 256 // height))
    while span % cells:
        cells -= 1
    return cells


def stencil(rows, height):
    row = lax.broadcasted_iota(jnp.int32, (rows, rows), 0)
    column = lax.broadcasted_iota(jnp.int32, (rows, rows), 1)
    apart = jnp.where(row // height == column // height, jnp.abs(row - column), 2)
    entry = jnp.where(apart == 0, 1.0 - 2.0 * vertical_mix, jnp.where(apart == 1, vertical_mix, 0.0))
    return entry.astype(jnp.bfloat16)


def upright(row):
    count = row.shape[1]
    place = lax.broadcasted_iota(jnp.int32, (count, count), 0)
    lane = lax.broadcasted_iota(jnp.int32, (count, count), 1)
    return jnp.sum(jnp.where(place == lane, row, jnp.zeros_like(row)), axis=1, keepdims=True)


def march_kernel(
    rows_ref, rows_row_ref, source_ref, recovery_ref, inflow_ref,
    end_ref, picks_ref, share_ref, rate_ref, low_rate_ref, high_rate_ref,
    deficits, tiles, through_rows, through,
):
    shape = source_ref.shape[:3]
    planes, span, height = shape
    count, members = picks_ref.shape
    cells = group_of(span, height)
    group = cells * height
    blocks = [jnp.transpose(recovery_ref[:, a, :]) for a in range(span)]
    for a in range(span):
        rate_ref[a * height : (a + 1) * height] = blocks[a]
    low_rate_ref[...] = jnp.concatenate([block[:1] for block in blocks], axis=0)
    high_rate_ref[...] = jnp.concatenate([block[height - 1 :] for block in blocks], axis=0)
    mix = stencil(group, height)
    product = None
    for p in range(planes):
        product = recovery_ref[p] if p == 0 else product * recovery_ref[p]
        through[p] = product
        for c in range(span // cells):
            part = slice(c * group, (c + 1) * group)
            term = dot(mix, source_ref[p, c * cells : (c + 1) * cells].reshape(group, members))
            if p > 0:
                term = rate_ref[part, p : p + 1] * deficits[p - 1, part] + term
            deficits[p, part] = term
    end_ref[...] = deficits[planes - 1]
    for k in range(count):
        p, a, b = place_of(rows_ref[k], shape)
        first = pl.multiple_of(b - lax.bitwise_and(b, 15), 16)
        tiles[k] = inflow_ref[p, a, pl.ds(first, 16), :].astype(jnp.float32)
        through_rows[pl.ds(k, 1), :] = through[p, pl.ds(a, 1), :]
    for k in range(count):
        p, a, b = place_of(rows_ref[k], shape)
        picks_ref[pl.ds(k, 1), :] = (
            tiles[k, pl.ds(lax.bitwise_and(b, 15), 1), :] - deficits[p, pl.ds(a * height + b, 1), :]
        )
    cell = upright(rows_row_ref[...].astype(jnp.float32)).astype(jnp.int32) % height
    lane = lax.broadcasted_iota(jnp.int32, (count, height), 1)
    share = jnp.sum(jnp.where(lane == cell, through_rows[...], 0.0), axis=1, keepdims=True)
    share_ref[...] = jnp.broadcast_to(share, share_ref.shape)


def march(source, inflow, recovery, obs_rows):
    planes, span, height, members = source.shape
    observed = obs_rows.shape[0]
    cells = span * height
    f32 = jnp.float32
    vmem = pl.BlockSpec(memory_space=pltpu.VMEM)
    return pl.pallas_call(
        march_kernel,
        in_specs=[pl.BlockSpec(memory_space=pltpu.SMEM)] + [vmem] * 4,
        out_specs=[vmem] * 6,
        out_shape=[
            jax.ShapeDtypeStruct((cells, members), f32),
            jax.ShapeDtypeStruct((observed, members), f32),
            jax.ShapeDtypeStruct((observed, members), f32),
            jax.ShapeDtypeStruct((cells, planes), f32),
            jax.ShapeDtypeStruct((span, planes), f32),
            jax.ShapeDtypeStruct((span, planes), f32),
        ],
        scratch_shapes=[
            pltpu.VMEM((planes, cells, members), f32),
            pltpu.VMEM((observed, 16, members), f32),
            pltpu.VMEM((observed, height), f32),
            pltpu.VMEM((planes, span, height), f32),
        ],
        compiler_params=params(LIMIT),
        cost_estimate=cost(3 * source.size, 4 * source.size),
    )(obs_rows, obs_rows[None, :], source, recovery, inflow)


def edge_kernel(
    place_ref, first_ref, second_ref, low_rate_ref, high_rate_ref, end_ref, term_ref, edge_ref, leaving_ref
):
    planes, span, members = first_ref.shape
    height = leaving_ref.shape[1]
    even = lax.bitwise_and(place_ref[0], 1) == 0
    low, high = None, None
    for p in range(planes):
        one = vertical_mix * first_ref[p].astype(jnp.float32)
        two = vertical_mix * second_ref[p].astype(jnp.float32)
        low_term = jnp.where(even, two, one)
        high_term = jnp.where(even, one, two)
        term_ref[0, p] = low_term
        term_ref[1, p] = high_term
        low = low_term if p == 0 else low_rate_ref[:, p : p + 1] * low + low_term
        high = high_term if p == 0 else high_rate_ref[:, p : p + 1] * high + high_term
        edge_ref[0, p] = low
        edge_ref[1, p] = high
    row = lax.broadcasted_iota(jnp.int32, (height, members), 0)
    for a in range(span):
        share = jnp.where(row == 0, low[a : a + 1], jnp.where(row == height - 1, high[a : a + 1], 0.0))
        leaving_ref[a] = end_ref[a * height : (a + 1) * height] + share


def edge_march(place, first, second, low_rate, high_rate, end):
    planes, span, members = first.shape
    vmem = pl.BlockSpec(memory_space=pltpu.VMEM)
    return pl.pallas_call(
        edge_kernel,
        in_specs=[pl.BlockSpec(memory_space=pltpu.SMEM)] + [vmem] * 5,
        out_specs=[vmem] * 3,
        out_shape=[
            jax.ShapeDtypeStruct((2, planes, span, members), jnp.float32),
            jax.ShapeDtypeStruct((2, planes, span, members), jnp.float32),
            jax.ShapeDtypeStruct((span, end.shape[0] // span, members), jnp.float32),
        ],
        compiler_params=params(LIMIT),
        cost_estimate=cost(first.size, 8 * first.size),
    )(place, first, second, low_rate, high_rate, end)


def payload(forecast, obs, weight):
    members = forecast.shape[1]
    mean = jnp.sum(forecast, axis=1, keepdims=True) * (1.0 / members)
    anomaly = (forecast - mean).astype(jnp.bfloat16).astype(jnp.float32)
    observed = weight * anomaly
    misfit = weight * (obs - mean)
    projection = jnp.sum(observed * misfit, axis=0, keepdims=True)
    one = projection.astype(jnp.bfloat16).astype(jnp.float32)
    two = (projection - one).astype(jnp.bfloat16).astype(jnp.float32)
    three = projection - one - two
    row = lax.broadcasted_iota(jnp.int32, (EXTRA, members), 0)
    pieces = jnp.where(row == 0, one, jnp.where(row == 1, two, jnp.where(row == 2, three, 0.0)))
    return jnp.concatenate([observed, pieces], axis=0).astype(jnp.bfloat16)


def prepare_kernel(
    height, rows_ref, edge_ref, picks_ref, obs_ref, weight_ref, out_ref, obs_out_ref, weight_out_ref, first_ref
):
    _, planes, span, _ = edge_ref.shape
    for k in range(picks_ref.shape[0]):
        p, a, b = place_of(rows_ref[k], (planes, span, height))
        side = jnp.where(b == height - 1, 1, 0)
        at_edge = jnp.where((b == 0) | (b == height - 1), 1.0, 0.0)
        out_ref[pl.ds(k, 1), :] = picks_ref[pl.ds(k, 1), :] - at_edge * edge_ref[side, p, pl.ds(a, 1), :]
    obs, weight = upright(obs_ref[...]), upright(weight_ref[...])
    obs_out_ref[...] = jnp.broadcast_to(obs, obs_out_ref.shape)
    weight_out_ref[...] = jnp.broadcast_to(weight, weight_out_ref.shape)
    first_ref[...] = payload(out_ref[...], obs, weight)


def prepare(obs_rows, obs, weight, picks, edge, height):
    count, members = picks.shape
    vmem = pl.BlockSpec(memory_space=pltpu.VMEM)
    out = jax.ShapeDtypeStruct(picks.shape, jnp.float32)
    return pl.pallas_call(
        functools.partial(prepare_kernel, height),
        in_specs=[pl.BlockSpec(memory_space=pltpu.SMEM)] + [vmem] * 4,
        out_specs=[vmem] * 4,
        out_shape=[out] * 3 + [jax.ShapeDtypeStruct((count + EXTRA, members), jnp.bfloat16)],
        compiler_params=params(LIMIT),
        cost_estimate=cost(100 * picks.size, 64 * picks.size),
    )(obs_rows, edge, picks, obs[None, :], weight[None, :])


def exact_pick(chosen, table):
    big = table.astype(jnp.bfloat16)
    middle, small = halves(table - big.astype(jnp.float32))
    return dot(chosen, big) + (dot(chosen, middle) + dot(chosen, small))


def observe_kernel(
    place_ref, rows_ref, obs_ref, weight_ref, picks_ref, share_ref, first_ref, incoming_ref, out_ref
):
    @pl.when(place_ref[0] < 2)
    def _():
        out_ref[...] = first_ref[...]

    @pl.when(place_ref[0] >= 2)
    def _():
        span, height, members = incoming_ref.shape
        cells = span * height
        row = upright(rows_ref[...].astype(jnp.float32)).astype(jnp.int32)
        _, cell = parted(row, cells)
        lane = lax.broadcasted_iota(jnp.int32, (row.shape[0], cells), 1)
        chosen = jnp.where(lane == cell, 1.0, 0.0).astype(jnp.bfloat16)
        arriving = exact_pick(chosen, incoming_ref[...].reshape(cells, members))
        forecast = picks_ref[...] - share_ref[...] * arriving
        out_ref[...] = payload(forecast, obs_ref[...], weight_ref[...])


def observe(place, obs_rows, obs, weight, picks, share, first, incoming):
    count, members = picks.shape
    vmem, smem = pl.BlockSpec(memory_space=pltpu.VMEM), pl.BlockSpec(memory_space=pltpu.SMEM)
    return pl.pallas_call(
        observe_kernel,
        in_specs=[smem] + [vmem] * 7,
        out_specs=vmem,
        out_shape=jax.ShapeDtypeStruct((count + EXTRA, members), jnp.bfloat16),
        compiler_params=params(LIMIT),
        cost_estimate=cost(40 * count * members, 64 * count * members),
    )(place, obs_rows[None, :], obs, weight, picks, share, first, incoming)


def anomaly_kernel(start, planes, source_ref, inflow_ref, rate_ref, state_ref, term_ref, *refs):
    out_ref, mean_ref, end_ref = refs
    _, span, height, members = source_ref.shape
    wide = mean_ref.shape[2]
    cells = group_of(span, height)
    group = cells * height
    mix = stencil(group, height)
    row = lax.broadcasted_iota(jnp.int32, (height, members), 0)
    for p in range(start, start + planes):
        before = state_ref if p == start else end_ref
        for c in range(span // cells):
            term = dot(mix, source_ref[p, c * cells : (c + 1) * cells].reshape(group, members))
            some = slice(c * cells, (c + 1) * cells)
            part = slice(c * group, (c + 1) * group)
            halo = []
            for a in range(c * cells, (c + 1) * cells):
                low, high = term_ref[0, p, a : a + 1, :], term_ref[1, p, a : a + 1, :]
                halo.append(jnp.where(row == 0, low, jnp.where(row == height - 1, high, 0.0)))
            deficit = rate_ref[part, p : p + 1] * before[part] + (term + jnp.concatenate(halo, axis=0))
            end_ref[part] = deficit
            forecast = inflow_ref[p, some].astype(jnp.float32).reshape(group, members) - deficit
            mean = jnp.sum(forecast, axis=1, keepdims=True) * (1.0 / members)
            anomaly = (forecast - mean).astype(jnp.bfloat16)
            out_ref[p - start, some] = anomaly.reshape(cells, height, members)
            mean_ref[p - start, part] = jnp.broadcast_to(mean, (group, wide))


def anomalies(source, inflow, rates, state, term, start, stop):
    planes = stop - start
    vmem = pl.BlockSpec(memory_space=pltpu.VMEM)
    size = state.size * planes
    return pl.pallas_call(
        functools.partial(anomaly_kernel, start, planes),
        in_specs=[vmem] * 5,
        out_specs=[vmem] * 3,
        out_shape=[
            pltpu.VMEM((planes,) + source.shape[1:], jnp.bfloat16),
            pltpu.VMEM((planes, state.shape[0], min(128, state.shape[1])), jnp.float32),
            pltpu.VMEM(state.shape, jnp.float32),
        ],
        compiler_params=params(LIMIT),
        cost_estimate=cost(4 * size, 6 * size),
    )(source, inflow, rates, state, term)


def halves(x):
    big = x.astype(jnp.bfloat16)
    return big, (x - big.astype(jnp.float32)).astype(jnp.bfloat16)


def fine_dot(a, b, dims=NN):
    a_big, a_small = halves(a)
    b_big, b_small = halves(b)
    return dot(a_big, b_big, dims) + (dot(a_big, b_small, dims) + dot(a_small, b_big, dims))


def split_rows(picked, rows):
    total, members = rows.shape
    block = picked + EXTRA
    place = lax.broadcasted_iota(jnp.int32, (total, members), 0) % block
    observed = jnp.where(place < picked, rows.astype(jnp.float32), 0.0).astype(jnp.bfloat16)
    slot = lax.broadcasted_iota(jnp.int32, (16, total), 1) % block
    return observed, dot(jnp.where(slot >= picked, 1.0, 0.0).astype(jnp.bfloat16), rows)


def gram_kernel(picked, rows_ref, order_ref, gram_ref, pieces_ref, select_ref, select_t_ref):
    members = rows_ref.shape[1]
    bf16, f32 = jnp.bfloat16, jnp.float32
    row = lax.broadcasted_iota(jnp.int32, (members, members), 0)
    column = lax.broadcasted_iota(jnp.int32, (members, members), 1)
    order = order_ref[...]
    select_ref[...] = jnp.where(order == row, 1.0, 0.0).astype(bf16)
    select_t = jnp.where(upright(order.astype(f32)) == column.astype(f32), 1.0, 0.0).astype(bf16)
    select_t_ref[...] = select_t
    observed, pieces_ref[...] = split_rows(picked, rows_ref[...])
    ordered_t = dot(select_t, observed, NT).astype(bf16)
    gram_ref[...] = dot(ordered_t, ordered_t, NT) + jnp.where(row == column, members - 1.0, 0.0)


def gram_part(picked, rows, member_order):
    total, members = rows.shape
    vmem = pl.BlockSpec(memory_space=pltpu.VMEM)
    square = (members, members)
    return pl.pallas_call(
        functools.partial(gram_kernel, picked),
        in_specs=[vmem] * 2,
        out_specs=[vmem] * 4,
        out_shape=[
            jax.ShapeDtypeStruct(square, jnp.float32),
            jax.ShapeDtypeStruct((16, members), jnp.float32),
            jax.ShapeDtypeStruct(square, jnp.bfloat16),
            jax.ShapeDtypeStruct(square, jnp.bfloat16),
        ],
        compiler_params=params(LIMIT),
        cost_estimate=cost(1000 * members * 4, 4 * total * members),
    )(rows, member_order[None, :])


def update_kernel(picked, rows_ref, gram_ref, pieces_ref, select_ref, select_t_ref, *refs):
    part_refs = refs[:-6]
    out_ref, gram, factor, weights_t, results, out_sem = refs[-6:]
    members = rows_ref.shape[1]
    bf16, f32 = jnp.bfloat16, jnp.float32
    row = lax.broadcasted_iota(jnp.int32, (members, members), 0)
    column = lax.broadcasted_iota(jnp.int32, (members, members), 1)
    diagonal, lower = row == column, row > column
    identity = jnp.where(diagonal, 1.0, 0.0)
    select = select_ref[...]
    observed, pieces = split_rows(picked, rows_ref[...])
    ordered_t = dot(select_t_ref[...], observed, NT).astype(bf16)
    full = gram_ref[...] + dot(ordered_t, ordered_t, NT)
    gram[...] = full
    pieces = pieces_ref[...] + pieces
    piece_one = pieces.astype(bf16)
    piece_two, piece_three = halves(pieces - piece_one.astype(f32))
    projection = dot(piece_one, select) + (dot(piece_two, select) + dot(piece_three, select))
    on_diagonal = jnp.where(diagonal, full, 0.0)
    scale_row = lax.rsqrt(jnp.sum(on_diagonal, axis=0, keepdims=True))
    scale_column = lax.rsqrt(jnp.sum(on_diagonal, axis=1, keepdims=True))
    unit = full * scale_row * scale_column

    def lower_part(residual):
        return jnp.where(lower, residual, jnp.where(diagonal, 0.5 * residual, 0.0)).astype(bf16)

    def refine(inverse, unit):
        unit_big, unit_small = halves(unit)
        inverse = inverse.astype(bf16)
        half_way = dot(inverse, unit_big) + dot(inverse, unit_small)
        big, small = halves(half_way)
        residual = dot(big, inverse, NT) + dot(small, inverse, NT) - identity
        better = inverse.astype(f32) - dot(lower_part(residual), inverse)
        return better, jnp.sum(residual * residual)

    def finish(inverse):
        inverse_big, inverse_small = halves(inverse)
        turned = dot(inverse_big, select, NT) + dot(inverse_small, select, NT)
        coefficients = fine_dot(projection, inverse, NT)
        big, small = halves(turned)
        placed = dot(select, big) + dot(select, small)
        shift = fine_dot(coefficients, turned)[:1]
        weights_t[...] = ((members - 1.0) ** 0.5 * placed + shift).astype(bf16)

    inverse = identity - jnp.where(lower, unit, 0.0)
    unit_big = unit.astype(bf16)
    for _ in range(2):
        inverse_big = inverse.astype(bf16)
        half_way = dot(inverse_big, unit_big).astype(bf16)
        residual = dot(half_way, inverse_big, NT) - identity
        inverse = inverse - dot(lower_part(residual), inverse_big)
    inverse, error = refine(inverse, unit)
    factor[...] = inverse
    finish(inverse * scale_row)

    @pl.when(jnp.logical_not(error <= 0.04))
    def _():
        def again(carried):
            step, _ = carried
            better, error = refine(factor[...], gram[...] * scale_row * scale_column)
            factor[...] = better
            return step + 1, error

        def unfinished(carried):
            step, error = carried
            return (step < 8) & (error > 0.04) & (error < 64.0)

        _, last_error = lax.while_loop(unfinished, again, (0, error))
        factor[...] = factor[...] * scale_row

        @pl.when(jnp.logical_not(last_error <= 0.04))
        def _():
            factor[...] = identity

            def eliminate(k, carry):
                held = gram[...]
                pivot_row = gram[pl.ds(k, 1), :]
                pivot = jnp.sum(jnp.where(column[:1] == k, pivot_row, 0.0), axis=1, keepdims=True)
                pivot_column = jnp.sum(jnp.where(column == k, held, 0.0), axis=1, keepdims=True)
                share = jnp.where(row[:, :1] > k, pivot_column / pivot, 0.0)
                factor[...] = factor[...] - share * factor[pl.ds(k, 1), :]
                gram[...] = held - share * pivot_row
                return carry

            lax.fori_loop(0, members, eliminate, 0)
            pivots = jnp.sum(jnp.where(diagonal, gram[...], 0.0), axis=1, keepdims=True)
            factor[...] = factor[...] * lax.rsqrt(pivots)

        finish(factor[...])

    stores = []
    for ref, mean_ref in zip(part_refs[::2], part_refs[1::2]):
        for p in range(ref.shape[0]):
            at = len(stores)
            mean = jnp.concatenate([mean_ref[p]] * (members // mean_ref.shape[2]), axis=1)
            analysis = mean + dot(ref[p].reshape(-1, members), weights_t[...], NT)
            results[at] = analysis.astype(bf16).reshape(ref.shape[1:])
            store = pltpu.make_async_copy(results.at[at], out_ref.at[at], out_sem.at[at])
            store.start()
            stores.append(store)
    for store in stores:
        store.wait()


def updated(picked, rows, part, parts, shape):
    planes, span, height, members = shape
    size = planes * span * height * members
    vmem = pl.BlockSpec(memory_space=pltpu.VMEM)
    return pl.pallas_call(
        functools.partial(update_kernel, picked),
        in_specs=[vmem] * (1 + len(part) + len(parts)),
        out_specs=pl.BlockSpec(memory_space=pltpu.HBM),
        out_shape=jax.ShapeDtypeStruct(shape, jnp.bfloat16),
        scratch_shapes=[
            pltpu.VMEM((members, members), jnp.float32),
            pltpu.VMEM((members, members), jnp.float32),
            pltpu.VMEM((members, members), jnp.bfloat16),
            pltpu.VMEM(shape, jnp.bfloat16),
            pltpu.SemaphoreType.DMA((planes,)),
        ],
        compiler_params=params(LIMIT),
        cost_estimate=cost(4 * size, 5 * size),
    )(rows, *part, *parts)


def pairs(count, first):
    low = [(i, i + 1) for i in range(first, count - 1, 2)]
    return low + [(j, i) for i, j in low]


def downstream(value, rate):
    count = lax.axis_size("stream")
    steps = [(i, i + 1) for i in range(count - 1)]
    incoming = lax.ppermute(value, "stream", steps)
    for _ in range(count - 2):
        incoming = lax.ppermute(rate * incoming + value, "stream", steps)
    return incoming


def rounds():
    steps = []
    for axis in ("height", "span"):
        bits = (lax.axis_size(axis) - 1).bit_length()
        steps.append([(axis, (2 << bit) - 1 if axis == "height" else 1 << bit) for bit in reversed(range(bits))])
    mixed = []
    while steps[0] or steps[1]:
        pair = [axis.pop(0) for axis in steps if axis]
        mixed += [(pair[0], pair[-1]), (pair[-1], pair[0])][: len(pair)]
    return mixed


def exchanges():
    sizes = [lax.axis_size(axis) for axis in AXES]
    places = [
        {"stream": i // (sizes[1] * sizes[2]), "span": i // sizes[2] % sizes[1], "height": i % sizes[2]}
        for i in range(sizes[0] * sizes[1] * sizes[2])
    ]

    def flat(place):
        return (place["stream"] * sizes[1] + place["span"]) * sizes[2] + place["height"]

    steps = rounds()
    apart = sizes[0] // 2
    while apart:
        steps.append((("stream", apart), ("stream", apart)))
        apart //= 2
    moves = []
    for step in steps:
        taken = [(place, *step[place["stream"] % 2]) for place in places]
        moves.append([(flat(at), flat(at | {axis: at[axis] ^ bit})) for at, axis, bit in taken])
    return moves


def shards(source, inflow, recovery, obs_rows, obs, observation_weight, member_order):
    planes, span, height, members = source.shape
    levels = lax.axis_size("height")
    place = (lax.axis_index("height") % 2 + 2 * lax.axis_index("stream"))[None]
    together = lax.optimization_barrier

    first = border(pltpu.with_memory_space_constraint(source, pltpu.HBM), place, True)
    source = pltpu.with_memory_space_constraint(source, pltpu.VMEM)
    inflow, first = together((inflow, first))
    inflow = pltpu.with_memory_space_constraint(inflow, pltpu.VMEM)
    second = border(source, place, False)
    first = lax.ppermute(first, "height", pairs(levels, 0))
    second = lax.ppermute(second, "height", pairs(levels, 1))
    end, picks, share, rates, low_rate, high_rate = march(source, inflow, recovery, obs_rows)
    end, first, second = together((end, first, second))
    term, edge, leaving = edge_march(place, first, second, low_rate, high_rate, end)
    total = jnp.prod(recovery, axis=0)[..., None] if lax.axis_size("stream") > 2 else None
    incoming = downstream(leaving, total)
    picks, obs, weight, first = prepare(obs_rows, obs, observation_weight, picks, edge, height)
    rows = observe(place, obs_rows, obs, weight, picks, share, first, incoming)
    state = incoming.reshape(span * height, members)
    cuts = [planes * part // 16 for part in CUTS]
    parts = []
    *moves, last_moves = exchanges()
    for pairing in moves:
        other = lax.ppermute(rows, AXES, pairing)
        if len(cuts) > 1:
            state, rows = together((state, rows))
            anomaly, mean, state = anomalies(source, inflow, rates, state, term, cuts[0], cuts[1])
            other, state, anomaly, mean = together((other, state, anomaly, mean))
            parts += [anomaly, mean]
            cuts = cuts[1:]
        rows = jnp.concatenate([rows, other], axis=0)
    while len(cuts) > 1:
        anomaly, mean, state = anomalies(source, inflow, rates, state, term, cuts[0], cuts[1])
        parts += [anomaly, mean]
        cuts = cuts[1:]
    other = lax.ppermute(rows, AXES, last_moves)
    part = gram_part(obs_rows.shape[0], rows, member_order)
    return updated(obs_rows.shape[0], other, part, parts, source.shape)


def solution(mesh):
    placed = (
        P("stream", "span", "height", None),
        P("stream", "span", "height", None),
        P("stream", "span", "height"),
        P(("stream", "span", "height")),
        P(("stream", "span", "height")),
        P(("stream", "span", "height")),
        P(),
    )
    return jax.shard_map(
        shards,
        mesh=mesh,
        in_specs=placed,
        out_specs=P("stream", "span", "height", None),
        check_vma=False,
    )
```
